256 devices in a mesh: gx: 64 (over z_lo, x, y, core), gy: 4 (over z_hi).
Axes of the slice: x: 4, y: 4, z: 8 (z_hi: 4, z_lo: 2; z = z_hi * 2 + z_lo), core: 2. Of those that a mesh axis runs over, the one named last changes fastest.
Arguments:
- flow_state: float32 [5, 512, 64, 128], P(None, 'gx', 'gy'), may hold values from -3 to 13, as said below
- cotangent: float32 [5, 512, 64, 128], P(None, 'gx', 'gy'), may hold values from -6 to 6
- clip_flags: int32 [64, 8, 16], P('gx', 'gy'), may hold values from 0 to 2
- successor_ids: int32 [16], replicated, may hold values from 0 to 15, as said below
Outputs:
- residual: float32 [5, 512, 64, 128], P(None, 'gx', 'gy')
- grad_state: float32 [5, 512, 64, 128], P(None, 'gx', 'gy')
The draws below stay inside these ranges and needn't reach their ends.
Inputs may be any that keep to these rules, and one draw needn't show every extreme that they name: `flow_state`: density and pressure, derived as in the reference program, are positive at every node, between 0.15 and 4.5; every velocity component has magnitude 0.05 or more at every node. Following successor_ids from any slot visits all 16 slots once before it returns.
All inputs are finite; a program needn't handle non-finite values.
Results may differ from the reference program's by a relative error of at most 0.0003.
Values sent between devices are 32-bit elements; how exact they have to be, the bound alone decides.
No kernel may reach another device: no remote copies, remote signals or barrier semaphores. Data moves between devices by JAX's collectives and lax.ppermute only.
A program may use at most 128 MiB of HBM per device.

```python
import math
import jax
import jax.numpy as jnp
import numpy as np
from jax import lax

NODES = 8
EZ = 16
NEX = 64
NEY = 8
NXN = 512
NYN = 64
NZN = 128


def draw_flow_state(key, part):
    key = jax.random.fold_in(key, 7)
    keys = jax.random.split(key, 7)
    elem_shape = (NEX, NEY, EZ)
    node_shape = (NXN, NYN, NZN)
    base_low, base_high, rough_low, rough_high, vel_range = (0.5, 2.0, 0.02, 0.5, 0.5)
    dens_base = jax.random.uniform(keys[0], elem_shape, jnp.float32, base_low, base_high)
    pres_base = jax.random.uniform(keys[1], elem_shape, jnp.float32, base_low, base_high)
    roughness = jnp.exp(jax.random.uniform(keys[2], elem_shape, jnp.float32, math.log(rough_low), math.log(rough_high)))

    def to_nodes(values):
        return jnp.repeat(jnp.repeat(jnp.repeat(values, NODES, axis=0), NODES, axis=1), NODES, axis=2)
    rough_nodes = to_nodes(roughness)
    density = to_nodes(dens_base) * (1.0 + rough_nodes * jax.random.uniform(keys[3], node_shape, jnp.float32, -1.0, 1.0))
    pressure = to_nodes(pres_base) * (1.0 + rough_nodes * jax.random.uniform(keys[4], node_shape, jnp.float32, -1.0, 1.0))
    magnitude = jax.random.uniform(keys[5], (3,) + node_shape, jnp.float32, 0.05, vel_range)
    sign_value = (2 * jax.random.randint(keys[6], (3,) + node_shape, 0, 2) - 1).astype(jnp.float32)
    velocity = magnitude * sign_value
    energy = pressure / 0.4 + 0.5 * density * jnp.sum(velocity * velocity, axis=0)
    return jnp.concatenate([density[None], density[None] * velocity, energy[None]], axis=0).astype(jnp.float32)


def draw_successor_ids(key, part):
    key = jax.random.fold_in(key, 13)
    visit_order = jax.random.permutation(key, EZ).astype(jnp.int32)
    return jnp.zeros((EZ,), jnp.int32).at[visit_order].set(jnp.roll(visit_order, -1)).astype(jnp.int32)


def place_ends(array, rng, low, top_value):
    shape = array.shape
    index_at = [jax.random.randint(jax.random.fold_in(rng, axis), (), 0, shape[axis]) for axis in range(len(shape))]
    array = array.at[tuple(index_at)].set(low)
    longest = shape.index(max(shape))
    index_at[longest] = (index_at[longest] + 1) % shape[longest]
    return array.at[tuple(index_at)].set(top_value)


def level_of(rng, shape, cuts, least, top_value):
    factor_of = 1.0
    for axis_at, shards_of in cuts:
        draws = jax.random.uniform(jax.random.fold_in(jax.random.fold_in(rng, 6), axis_at), (shards_of,), jnp.float32, least / len(cuts), top_value / len(cuts))
        factor_of = factor_of * jnp.repeat(jnp.exp(draws), shape[axis_at] // shards_of).reshape((-1,) + (1,) * (len(shape) - 1 - axis_at))
    return factor_of


def noise(key, shape, scale, limit, cuts=(), kind=jnp.bfloat16):
    entries = scale * jax.random.normal(key, shape, jnp.float32)
    if cuts:
        entries = entries * level_of(key, shape, cuts, -0.22, 0.18)
    return jnp.clip(entries, -limit, limit).astype(kind)


def setup_inputs(seed: int = 0) -> dict:
    seeds = jax.random.split(jax.random.key(seed), 5)
    return {
        "flow_state": draw_flow_state(jax.random.fold_in(seeds[4], 71), 0),
        "cotangent": noise(seeds[1], (5, NXN, NYN, NZN), 1.0, 6.0, ((1, 64), (2, 4)), jnp.float32),
        "clip_flags": place_ends(jax.random.randint(seeds[2], (NEX, NEY, EZ), 0, 3), jax.random.fold_in(seeds[2], 1), 0, 2).astype(jnp.int32),
        "successor_ids": draw_successor_ids(jax.random.fold_in(seeds[4], 71), 0),
    }


HEAT_RATIO = 1.4
SERIES_LIMIT = 0.01
ENERGY_EPS = 1e-05
LOG_THRESHOLD = math.log(0.01)
ALPHA_UPPER = 0.5
HIGHEST = lax.Precision.HIGHEST

def legendre_values(points, node_count):
    values_table = np.zeros((points.shape[0], node_count))
    values_table[:, 0] = 1.0
    values_table[:, 1] = points
    for degree_index in range(2, node_count):
        values_table[:, degree_index] = ((2 * degree_index - 1) * points * values_table[:, degree_index - 1] - (degree_index - 1) * values_table[:, degree_index - 2]) / degree_index
    return values_table

def node_tables():
    degree = 7
    node_count = degree + 1
    points = -np.cos(np.pi * np.arange(node_count) / degree)
    for newton_step in range(60):
        legend = legendre_values(points, node_count)
        points = points - (points * legend[:, degree] - legend[:, degree - 1]) / (node_count * legend[:, degree])
    legend = legendre_values(points, node_count)
    weights = 2.0 / (degree * node_count * legend[:, degree] * legend[:, degree])
    differ = np.zeros((node_count, node_count))
    for row_index in range(node_count):
        for col_index in range(node_count):
            if row_index != col_index:
                differ[row_index, col_index] = legend[row_index, degree] / (legend[col_index, degree] * (points[row_index] - points[col_index]))
    differ[0, 0] = -degree * node_count / 4.0
    differ[degree, degree] = degree * node_count / 4.0
    split_matrix = 2.0 * differ
    split_matrix[0, 0] += 1.0 / weights[0]
    split_matrix[degree, degree] -= 1.0 / weights[degree]
    norm_table = 2.0 / (2.0 * np.arange(node_count) + 1.0)
    norm_table[degree] = 2.0 / degree
    to_modal = legend.T * weights[None, :] / norm_table[:, None]
    return (weights, split_matrix, to_modal)

def primitive(conserved):
    density = conserved[0]
    velocity = conserved[1:4] / density
    pressure = (HEAT_RATIO - 1.0) * (conserved[4] - 0.5 * density * lax.optimization_barrier(jnp.sum(velocity * velocity, axis=0)))
    return (density, velocity, pressure)

def log_mean(left_value, right_value):
    quotient = left_value / right_value
    factor = (quotient - 1.0) / (quotient + 1.0)
    square = factor * factor
    series = 1.0 + square / 3.0 + square * square / 5.0 + square * square * square / 7.0
    is_close = square < SERIES_LIMIT
    safe_quotient = jnp.where(is_close, 2.0, quotient)
    safe_factor = (safe_quotient - 1.0) / (safe_quotient + 1.0)
    logarithm = jnp.log(safe_quotient) / (2.0 * safe_factor)
    return (left_value + right_value) / (2.0 * jnp.where(is_close, series, logarithm))

def entropy_flux(low_side, up_side, direction):
    dens_low, vel_low, pres_low = low_side
    dens_up, vel_up, pres_up = up_side
    dens_mean = log_mean(dens_low, dens_up)
    inv_mean = pres_low * pres_up / log_mean(dens_low * pres_up, dens_up * pres_low)
    vel_avg = 0.5 * (vel_low + vel_up)
    pres_avg = 0.5 * (pres_low + pres_up)
    vel_prod = 0.5 * lax.optimization_barrier(jnp.sum(vel_low * vel_up, axis=0))
    mass_flux = dens_mean * vel_avg[direction]
    pieces = [mass_flux]
    for component in range(3):
        moment = mass_flux * vel_avg[component]
        if component == direction:
            moment = moment + pres_avg
        pieces.append(moment)
    pieces.append(mass_flux * (vel_prod + inv_mean / (HEAT_RATIO - 1.0)) + 0.5 * (pres_low * vel_up[direction] + pres_up * vel_low[direction]))
    return jnp.stack(pieces)

def euler_flux(conserved, state_prim, direction):
    density, velocity, pressure = state_prim
    normal = velocity[direction]
    pieces = [conserved[0] * normal]
    for component in range(3):
        moment = conserved[component + 1] * normal
        if component == direction:
            moment = moment + pressure
        pieces.append(moment)
    pieces.append((conserved[4] + pressure) * normal)
    return jnp.stack(pieces)

def wave_speed(state_prim, direction):
    density, velocity, pressure = state_prim
    sound_speed = jnp.sqrt(HEAT_RATIO * pressure / density)
    return jnp.abs(velocity[direction]) + sound_speed

def dissipative(low_side, up_side, direction):
    prim_low = primitive(low_side)
    prim_up = primitive(up_side)
    mean_speed = 0.5 * (wave_speed(prim_low, direction) + wave_speed(prim_up, direction))
    return 0.5 * (euler_flux(low_side, prim_low, direction) + euler_flux(up_side, prim_up, direction)) - 0.5 * mean_speed * (up_side - low_side)

def line_terms(node_lines, flux_low, flux_up, direction):
    weights, split_matrix, to_modal = node_tables()
    inv_weight = jnp.asarray(1.0 / weights, jnp.float32)[:, None]
    split_table = jnp.asarray(split_matrix, jnp.float32)
    first_node = jnp.asarray(np.eye(8)[:, 0], jnp.float32)[:, None]
    last_node = jnp.asarray(np.eye(8)[:, 7], jnp.float32)[:, None]
    density, velocity, pressure = primitive(node_lines)
    low_side = (density[:, :, None], velocity[:, :, :, None], pressure[:, :, None])
    up_side = (density[:, None], velocity[:, :, None], pressure[:, None])
    paired = entropy_flux(low_side, up_side, direction)
    volume = jnp.einsum('kj,vakjb->vakb', split_table, paired, precision=HIGHEST)
    boundary = last_node * flux_up[:, :, None] - first_node * flux_low[:, :, None]
    galerkin = -(volume + inv_weight * boundary)
    inner_flux = dissipative(node_lines[:, :, :-1], node_lines[:, :, 1:], direction)
    interfaces = jnp.concatenate([flux_low[:, :, None], inner_flux, flux_up[:, :, None]], axis=2)
    subcell = -(interfaces[:, :, 1:] - interfaces[:, :, :-1]) * inv_weight
    return (galerkin, subcell)

def blend_factor(flow_field, clip_flags):
    node_x, node_y, node_z = flow_field.shape[1:]
    elem_x, elem_y, elem_z = (node_x // 8, node_y // 8, node_z // 8)
    weights, split_matrix, to_modal = node_tables()
    modal_table = jnp.asarray(to_modal, jnp.float32)
    density, velocity, pressure = primitive(flow_field)
    product = density * pressure
    coeffs = jnp.einsum('ka,eab->ekb', modal_table, product.reshape(elem_x, 8, node_y * node_z), precision=HIGHEST)
    coeffs = jnp.einsum('kb,xebz->xekz', modal_table, coeffs.reshape(node_x, elem_y, 8, node_z), precision=HIGHEST)
    block_size = 128 if node_z % 128 == 0 else node_z
    block_table = jnp.asarray(np.kron(np.eye(block_size // 8), to_modal.T), jnp.float32)
    coeffs = jnp.dot(coeffs.reshape(node_x * node_y * node_z // block_size, block_size), block_table, precision=HIGHEST)
    squares = (coeffs * coeffs).reshape(elem_x, 8, elem_y, 8, elem_z, 8)
    mode_index = np.arange(8)
    high_modes = np.maximum(np.maximum(mode_index[:, None, None], mode_index[None, :, None]), mode_index[None, None, :]) >= 6
    high_table = jnp.asarray(np.where(high_modes, 1.0, 0.0), jnp.float32).reshape(1, 8, 1, 8, 1, 8)
    top_energy = lax.optimization_barrier(jnp.sum(squares * high_table, axis=(1, 3, 5)))
    all_energy = lax.optimization_barrier(jnp.sum(squares, axis=(1, 3, 5)))
    raw_blend = ALPHA_UPPER * jax.nn.sigmoid(jnp.log(top_energy + ENERGY_EPS) - jnp.log(all_energy + ENERGY_EPS) - LOG_THRESHOLD)
    return jnp.where(clip_flags == 1, 0.0, jnp.where(clip_flags == 2, ALPHA_UPPER, raw_blend))

def face_and_blend(flow_field, clip_flags):
    node_x, node_y, node_z = flow_field.shape[1:]
    elem_x, elem_y = (node_x // 8, node_y // 8)
    along_x = flow_field.reshape(5, elem_x, 8, node_y * node_z)
    x_low = along_x[:, :, 0].reshape(5, elem_x, elem_y, 8, node_z)
    x_high = along_x[:, :, 7].reshape(5, elem_x, elem_y, 8, node_z)
    along_y = flow_field.reshape(5, node_x * elem_y, 8, node_z)
    y_low = along_y[:, :, 0].reshape(5, elem_x, 8, elem_y, node_z).swapaxes(2, 3)
    y_high = along_y[:, :, 7].reshape(5, elem_x, 8, elem_y, node_z).swapaxes(2, 3)
    traces = jnp.stack([x_low, x_high, y_low, y_high])
    return (traces, blend_factor(flow_field, clip_flags))

def element_terms(flow_field, neighbours, blend_ext, successor):
    x_left, x_right, y_left, y_right = neighbours
    node_x, node_y, node_z = flow_field.shape[1:]
    elem_x, elem_y, elem_z = (node_x // 8, node_y // 8, node_z // 8)
    line_fn = jax.checkpoint(line_terms, static_argnums=(3,))
    along_x = flow_field.reshape(5, elem_x, 8, node_y * node_z)
    face_low = jnp.concatenate([x_left.reshape(5, 1, node_y * node_z), along_x[:, :, 7]], axis=1)
    face_up = jnp.concatenate([along_x[:, :, 0], x_right.reshape(5, 1, node_y * node_z)], axis=1)
    face_x = dissipative(face_low, face_up, 0)
    gal_x, sub_x = line_fn(along_x, face_x[:, :-1], face_x[:, 1:], 0)
    along_y = flow_field.reshape(5, node_x * elem_y, 8, node_z)
    y_high = along_y[:, :, 7].reshape(5, node_x, elem_y, node_z)
    y_low = along_y[:, :, 0].reshape(5, node_x, elem_y, node_z)
    face_low = jnp.concatenate([y_left.reshape(5, node_x, 1, node_z), y_high], axis=2)
    face_up = jnp.concatenate([y_low, y_right.reshape(5, node_x, 1, node_z)], axis=2)
    face_y = dissipative(face_low, face_up, 1)
    gal_y, sub_y = line_fn(along_y, face_y[:, :, :-1].reshape(5, node_x * elem_y, node_z), face_y[:, :, 1:].reshape(5, node_x * elem_y, node_z), 1)
    column_count = node_x * node_y * elem_z
    along_z = flow_field.reshape(5, node_x, node_y, elem_z, 8).transpose(0, 4, 1, 2, 3).reshape(5, 1, 8, column_count)
    z_low = along_z[:, 0, 0].reshape(5, node_x * node_y, elem_z)
    z_high = along_z[:, 0, 7].reshape(5, node_x * node_y, elem_z)
    z_next = jnp.einsum('vqj,kj->vqk', z_low, successor, precision=HIGHEST)
    face_z = dissipative(z_high, z_next, 2)
    face_prev = jnp.einsum('vqk,km->vqm', face_z, successor, precision=HIGHEST)
    gal_z, sub_z = line_fn(along_z, face_prev.reshape(5, 1, column_count), face_z.reshape(5, 1, column_count), 2)

    def from_z(values):
        return values.reshape(5, 8, node_x, node_y, elem_z).transpose(0, 2, 3, 4, 1).reshape(5, node_x, node_y, node_z)
    galerkin = gal_x.reshape(flow_field.shape) + gal_y.reshape(flow_field.shape) + from_z(gal_z)
    subcell = sub_x.reshape(flow_field.shape) + sub_y.reshape(flow_field.shape) + from_z(sub_z)
    blend = blend_ext[1:-1, 1:-1]
    blend_above = jnp.einsum('xyj,kj->xyk', blend, successor, precision=HIGHEST)
    blend_below = jnp.einsum('xyk,km->xym', blend, successor, precision=HIGHEST)
    beside_all = blend_ext[:-2, 1:-1] + blend_ext[2:, 1:-1] + blend_ext[1:-1, :-2] + blend_ext[1:-1, 2:] + blend_above + blend_below
    smooth = blend + 0.5 * (1.0 - blend) * beside_all / 6.0
    node_blend = jnp.broadcast_to(smooth[:, None, :, None, :, None], (elem_x, 8, elem_y, 8, elem_z, 8)).reshape(node_x, node_y, node_z)
    return (1.0 - node_blend) * galerkin + node_blend * subcell

def reference(flow_state, cotangent, clip_flags, successor_ids):
    slot_count = successor_ids.shape[0]
    successor = (successor_ids[:, None] == jnp.arange(slot_count, dtype=jnp.int32)[None, :]).astype(jnp.float32)

    def whole_residual(flow_field):
        traces, blend = face_and_blend(flow_field, clip_flags)
        elem_x, elem_y = (traces.shape[2], traces.shape[3])
        node_y, node_z = (flow_field.shape[2], flow_field.shape[3])
        row_states = flow_field.reshape(5, elem_x, 8, node_y, node_z).transpose(1, 0, 2, 3, 4)
        x_left = jnp.roll(traces[1], 1, axis=1).transpose(1, 0, 2, 3, 4)
        x_right = jnp.roll(traces[0], -1, axis=1).transpose(1, 0, 2, 3, 4)
        y_left = traces[3][:, :, elem_y - 1].transpose(1, 0, 2, 3)[:, :, None]
        y_right = traces[2][:, :, 0].transpose(1, 0, 2, 3)[:, :, None]
        padded = jnp.pad(blend, ((1, 1), (1, 1), (0, 0)), mode='wrap')
        windows = jnp.stack([padded[0:elem_x], padded[1:elem_x + 1], padded[2:elem_x + 2]], axis=1)

        def one_row(row_items):
            row_state, left_x, right_x, left_y, right_y, window = row_items
            return element_terms(row_state, (left_x, right_x, left_y, right_y), window, successor)
        result = lax.map(jax.checkpoint(one_row), (row_states, x_left, x_right, y_left, y_right, windows))
        return result.transpose(1, 0, 2, 3, 4).reshape(flow_field.shape)
    residual, pullback = jax.vjp(whole_residual, flow_state)
    gradient, = pullback(cotangent)
    return (residual, gradient)
```

```python
import functools

import jax
import jax.numpy as jnp
import numpy as np
from jax import lax
from jax.experimental import pallas as pl
from jax.experimental.pallas import tpu as pltpu
from jax.sharding import PartitionSpec as P
from numpy.polynomial import chebyshev, polynomial

F32 = jnp.float32
HIGHEST = lax.Precision.HIGHEST
EPS = 1e-05
PERMS = ((0, 1, 2), (1, 0, 2), (2, 0, 1))
NQ = 13
ROWS = 128


def legendre_values(points, node_count):
    values_table = np.zeros((points.shape[0], node_count))
    values_table[:, 0] = 1.0
    values_table[:, 1] = points
    for degree_index in range(2, node_count):
        values_table[:, degree_index] = (
            (2 * degree_index - 1) * points * values_table[:, degree_index - 1]
            - (degree_index - 1) * values_table[:, degree_index - 2]
        ) / degree_index
    return values_table


def node_tables():
    degree = 7
    node_count = degree + 1
    points = -np.cos(np.pi * np.arange(node_count) / degree)
    for newton_step in range(60):
        legend = legendre_values(points, node_count)
        points = points - (points * legend[:, degree] - legend[:, degree - 1]) / (
            node_count * legend[:, degree]
        )
    legend = legendre_values(points, node_count)
    weights = 2.0 / (degree * node_count * legend[:, degree] * legend[:, degree])
    differ = np.zeros((node_count, node_count))
    for row_index in range(node_count):
        for col_index in range(node_count):
            if row_index != col_index:
                differ[row_index, col_index] = legend[row_index, degree] / (
                    legend[col_index, degree] * (points[row_index] - points[col_index])
                )
    norm_table = 2.0 / (2.0 * np.arange(node_count) + 1.0)
    norm_table[degree] = 2.0 / degree
    to_modal = legend.T * weights[None, :] / norm_table[:, None]
    return (weights, differ, to_modal)


WEIGHTS, DIFFER, TO_MODAL = node_tables()
INV_W = [float(1.0 / w) for w in WEIGHTS]
SKEW = 2.0 * DIFFER * WEIGHTS[:, None]


def fitted(function, top, degree):
    series = chebyshev.Chebyshev.interpolate(function, degree, domain=[0.0, top])
    return [float(np.float32(c)) for c in series.convert(kind=polynomial.Polynomial).coef]


def sinhc(square):
    root = np.sqrt(np.maximum(square, 1e-12))
    return np.sinh(root) / root


def sinhc_slope(square):
    root = np.sqrt(np.maximum(square, 1e-12))
    exact = (np.cosh(root) - np.sinh(root) / root) / (root * root)
    series = 1.0 / 3.0 + square / 30.0 + square**2 / 840.0 + square**3 / 45360.0
    return np.where(square < 1e-2, series, exact)


MEAN_R = fitted(sinhc, 3.0, 4)
SLOPE_R = fitted(sinhc_slope, 3.0, 3)
MEAN_B = fitted(sinhc, 12.0, 5)
SLOPE_B = fitted(sinhc_slope, 12.0, 5)


def horner(coeffs, value):
    total = coeffs[-1] * value + coeffs[-2]
    for c in coeffs[-3::-1]:
        total = total * value + c
    return total


def rcp(value):
    return 1.0 / value


def log_parts(density, pressure):
    inv = rcp(density)
    ratio = pressure * inv
    half_log = 0.5 * jnp.log(density)
    return (
        jnp.sqrt(density),
        half_log,
        jnp.sqrt(5.0 * ratio),
        half_log - 0.5 * jnp.log(pressure),
    )


class Node:
    def __init__(self, vel, pres, root, theta, cot):
        self.vel, self.pres, self.cot = vel, pres, cot
        density = root * root
        vn, v1, v2 = vel
        mom = [density * v for v in vel]
        self.square = vn * vn + v1 * v1 + v2 * v2
        energy = 2.5 * pres + (0.5 * density) * self.square
        self.state = [density] + mom + [energy]
        mn = mom[0]
        self.flux = [mn, mn * vn + pres, mn * v1, mn * v2, (energy + pres) * vn]
        self.sound = theta * float(np.sqrt(1.4 / 5.0))
        self.speed = jnp.abs(vn) + self.sound

    def pull(self, half, direct, speed_cot):
        density = self.state[0]
        vn, v1, v2 = self.vel
        grad = [direct[i] + half[i] * vn for i in range(5)]
        sign = jnp.where(vn >= 0.0, 1.0, -1.0)
        dvn = half[0] * self.state[0]
        for i in range(1, 5):
            dvn = dvn + half[i] * self.state[i]
        dvn = dvn + half[4] * self.pres + speed_cot * sign
        inv = rcp(density)
        part = (0.5 * speed_cot) * self.sound
        dpres = half[1] + half[4] * vn + part * rcp(self.pres)
        over = dvn * inv
        pull_e = 0.4 * dpres
        grad[0] = grad[0] - part * inv - over * vn + (0.5 * pull_e) * self.square
        grad[1] = grad[1] + over - pull_e * vn
        grad[2] = grad[2] - pull_e * v1
        grad[3] = grad[3] - pull_e * v2
        grad[4] = grad[4] + pull_e
        return grad


def face(low, up):
    jump = [b - a for a, b in zip(low.state, up.state)]
    weight = [b - a for a, b in zip(low.cot, up.cot)]
    half_speed = 0.25 * (low.speed + up.speed)
    flux = [0.5 * (a + b) - half_speed * j for a, b, j in zip(low.flux, up.flux, jump)]
    dot = weight[0] * jump[0]
    for i in range(1, 5):
        dot = dot + weight[i] * jump[i]
    direct = [half_speed * w for w in weight]
    return flux, weight, direct, -0.25 * dot


def kernel_volume(
    flow, cot, flags, kxy, kzt, group, spread, out, zends, modes, msg, nat, turned, lines, prod, gsum
):
    for x in range(8):
        for h in range(2):
            src = pl.ds(x * 16 + h * 8, 8)
            dst = pl.ds(h * 64 + x * 8, 8)
            density = flow[0, src, :]
            inv = rcp(density)
            mom = [flow[1 + i, src, :] for i in range(3)]
            vel = [m * inv for m in mom]
            kinetic = mom[0] * vel[0] + mom[1] * vel[1] + mom[2] * vel[2]
            pres = 0.4 * (flow[4, src, :] - 0.5 * kinetic)
            prod[dst, :] = density * pres
            parts = vel + [pres] + list(log_parts(density, pres))
            for q in range(8):
                nat[q, dst, :] = parts[q]
            for q in range(5):
                value = cot[q, src, :]
                nat[8 + q, dst, :] = 2.0 * value if q == 0 else value
    for q in range(NQ):
        turned[q] = jnp.transpose(nat[q])
    for d in range(3):
        perm = PERMS[d]
        order = [perm[0], perm[1], perm[2], 3, 4, 5, 6, 7, 8] + [9 + i for i in perm] + [12]
        source = nat if d < 2 else turned
        for q in range(NQ):
            for h in range(2):
                for k in range(8):
                    rows = pl.ds(h * 64 + 8 * k, 8) if d == 0 else pl.ds(h * 64 + k, 8, stride=8)
                    value = source[order[q], rows, :]
                    lines[d, q, pl.ds(h * 64 + 8 * k, 8), :] = value * INV_W[k] if q >= 8 else value
    for q in range(NQ):
        for end in range(2):
            for h in range(2):
                zends[q, pl.ds(end * 16 + h * 8, 8), :] = lines[2, q, pl.ds(h * 64 + 56 * end, 8), :]

    def one(step, carry):
        d = step // 2
        base = (step % 2) * 64

        def rows(k):
            return pl.ds(pl.multiple_of(base + 8 * k, 8), 8)

        for k in range(7):
            a = [lines[d, q, rows(k), :] for q in range(NQ)]
            acc = [None] * 11 if k == 0 else [out[d, q, rows(k), :] for q in range(11)]
            for j in range(k + 1, 8):
                skew = float(SKEW[k, j])
                b = [lines[d, q, rows(j), :] for q in range(NQ)]
                vn, v1, v2 = (a[i] + b[i] for i in range(3))
                delta = [a[8 + i] - b[8 + i] for i in range(5)]
                y = a[5] - b[5]
                square = y * y
                scale = (0.25 * skew) * (a[4] * b[4])
                mean = scale * horner(MEAN_R, square)
                slope = (scale * y) * horner(SLOPE_R, square)
                yb = a[7] - b[7]
                square_b = yb * yb
                quot = rcp(horner(MEAN_B, square_b))
                inv5 = (a[6] * b[6]) * quot
                tilt = yb * (horner(SLOPE_B, square_b) * quot)
                dot = a[0] * b[0] + a[1] * b[1] + a[2] * b[2] + inv5
                mass = mean * vn
                half = 0.5 * skew
                flux = [
                    mass,
                    mass * vn + half * (a[3] + b[3]),
                    mass * v1,
                    mass * v2,
                    mass * dot + half * (a[3] * b[0] + b[3] * a[0]),
                ]
                phi = delta[0] + delta[1] * vn + delta[2] * v1 + delta[3] * v2 + delta[4] * dot
                common = phi * mean + delta[1] * mass
                t = half * delta[4]
                u = half * delta[1]
                w = mass * delta[4]
                r1 = mass * delta[2]
                r2 = mass * delta[3]
                pp = phi * mass
                qq = (phi * vn) * slope
                xx = w * inv5
                zz = xx * tilt
                grad_a = [
                    pp + qq,
                    common + w * b[0] + t * b[3],
                    r1 + w * b[1],
                    r2 + w * b[2],
                    u + t * b[0],
                    xx + zz,
                ]
                grad_b = [
                    pp - qq,
                    common + w * a[0] + t * a[3],
                    r1 + w * a[1],
                    r2 + w * a[2],
                    u + t * a[0],
                    xx - zz,
                ]
                for q in range(5):
                    acc[q] = flux[q] if acc[q] is None else acc[q] + flux[q]
                    before = 0.0 if k == 0 else out[d, q, rows(j), :]
                    out[d, q, rows(j), :] = before - flux[q]
                for q in range(6):
                    acc[5 + q] = grad_a[q] if acc[5 + q] is None else acc[5 + q] + grad_a[q]
                    out[d, 5 + q, rows(j), :] = grad_b[q] if k == 0 else out[d, 5 + q, rows(j), :] + grad_b[q]
            for q in range(11):
                out[d, q, rows(k), :] = acc[q]

        low = None
        zero = jnp.zeros((8, 128), F32)
        low_flux, low_weight, low_direct, low_dot = [zero] * 5, [zero] * 5, [zero] * 5, zero
        gained = zero
        for k in range(9):
            if k < 8:
                a = [lines[d, q, rows(k), :] for q in range(NQ)]
                node = Node(a[0:3], a[3], a[4], a[6], [0.5 * a[8]] + a[9:13])
            if k == 0:
                low = node
                continue
            if k < 8:
                flux, weight, direct, dot = face(low, node)
            else:
                flux, weight, direct, dot = [zero] * 5, [zero] * 5, [zero] * 5, zero
            m = k - 1
            total = [out[d, q, rows(m), :] for q in range(11)]
            total[0] = 2.0 * total[0]
            for q in range(5):
                diff = total[q] - (flux[q] - low_flux[q])
                gained = gained + low.cot[q] * diff
                out[d, q, rows(m), :] = total[q] * (-INV_W[m])
                out[d, 5 + q, rows(m), :] = diff * INV_W[m]
            fv = low.pull(
                [0.5 * (x + z) for x, z in zip(low_weight, weight)],
                [x - z for x, z in zip(direct, low_direct)],
                low_dot + dot,
            )
            inv = rcp(low.state[0])
            beta = 0.5 * total[10]
            g_rho = (beta - 0.5 * total[5]) * inv
            g_e = -0.4 * (total[9] + beta * rcp(low.pres))
            g_m = [-(total[6 + i] * inv) - g_e * low.vel[i] for i in range(3)]
            inner = g_m[0] * low.vel[0] + g_m[1] * low.vel[1] + g_m[2] * low.vel[2]
            dg = [g_rho - inner - (0.5 * g_e) * low.square] + g_m + [g_e]
            for q in range(5):
                out[d, 10 + q, rows(m), :] = dg[q]
                out[d, 15 + q, rows(m), :] = fv[q] - dg[q]
            low, low_flux, low_weight, low_direct, low_dot = node, flux, weight, direct, dot
        gsum[step] = gained
        return carry

    lax.fori_loop(0, 6, one, 0)

    coeffs = jnp.dot(kxy[...], prod[...], precision=HIGHEST, preferred_element_type=F32)
    coeffs = jnp.dot(coeffs, kzt[...], precision=HIGHEST, preferred_element_type=F32)
    modes[...] = coeffs
    squares = coeffs * coeffs
    sub = lax.broadcasted_iota(jnp.int32, (8, 128), 0)
    lane = lax.broadcasted_iota(jnp.int32, (8, 128), 1)
    high = (sub >= 6) | ((lane & 7) >= 6)
    packed = jnp.zeros((8, 128), F32)
    tops, alls, gains = [], [], []
    for h in range(2):
        every = squares[h * 64 : h * 64 + 8]
        for x in range(1, 6):
            every = every + squares[h * 64 + 8 * x : h * 64 + 8 * x + 8]
        ends = squares[h * 64 + 48 : h * 64 + 56] + squares[h * 64 + 56 : h * 64 + 64]
        tops.append(jnp.sum(jnp.where(high, every, 0.0) + ends, axis=0, keepdims=True))
        alls.append(jnp.sum(every + ends, axis=0, keepdims=True))
        gains.append(jnp.sum(gsum[h] + gsum[2 + h], axis=0, keepdims=True))
    for i, row in enumerate(tops + alls + gains):
        packed = jnp.where(sub == i, row, packed)
    sums = jnp.dot(packed, group[...], precision=HIGHEST, preferred_element_type=F32)
    along = jnp.concatenate([gsum[4], gsum[5]], axis=0)
    left = jnp.where(((sub == 4) & (lane < 64)) | ((sub == 5) & (lane >= 64)), 1.0, 0.0)
    per_slot = lax.dot_general(
        left, along, (((1,), (1,)), ((), ())), precision=HIGHEST, preferred_element_type=F32
    )
    sums = sums + jnp.dot(per_slot, spread[...], precision=HIGHEST, preferred_element_type=F32)
    flag_rows = jnp.dot(
        flags[...].astype(F32), spread[...], precision=HIGHEST, preferred_element_type=F32
    )
    packed = jnp.zeros((16, 128), F32)
    sub16 = lax.broadcasted_iota(jnp.int32, (16, 128), 0)
    for h in range(2):
        top = sums[h : h + 1] + EPS
        every = 0.01 * (sums[2 + h : 3 + h] + EPS)
        gain = sums[4 + h : 5 + h]
        flag = flag_rows[h : h + 1]
        over = rcp(top + every)
        keep = flag < 0.5
        alpha = jnp.where(keep, 0.5 * top * over, jnp.where(flag > 1.5, 0.5, 0.0))
        d_top = jnp.where(keep, every * over * over, 0.0)
        d_all = jnp.where(keep, -0.01 * top * over * over, 0.0)
        for i, row in enumerate((alpha, gain * (1.0 - alpha), gain, d_top, d_all)):
            packed = jnp.where(sub16 == 2 * i + h, row, packed)
    msg[...] = packed


def conserved_node(state, cot, direction):
    perm = PERMS[direction]
    density = state[0]
    inv = rcp(density)
    vel = [state[1 + i] * inv for i in perm]
    square = vel[0] * vel[0] + vel[1] * vel[1] + vel[2] * vel[2]
    pres = 0.4 * (state[4] - 0.5 * density * square)
    scaled = [cot[0]] + [cot[1 + i] for i in perm] + [cot[4]]
    return Node(vel, pres, jnp.sqrt(density), jnp.sqrt(5.0 * pres * inv), [c * INV_W[0] for c in scaled])


def face_shares(low, up):
    flux, weight, direct, dot = face(low, up)
    half = [0.5 * w for w in weight]
    return (
        [-INV_W[7] * f for f in flux],
        low.pull(half, direct, dot),
        [INV_W[0] * f for f in flux],
        up.pull(half, [-x for x in direct], dot),
    )


def kernel_faces(
    ids, flow, cot, x_left, x_right, y_left, y_right, parts, zends, modes, msg, kxyt, kz, base, extra, slope, zacc, znext, zback
):
    for k in range(16):
        znext[:, pl.ds(k, 1), :] = zends[:, pl.ds(ids[k], 1), :]
    for h in range(2):
        def side(ref, start):
            v = [ref[q, pl.ds(start + h * 8, 8), :] for q in range(NQ)]
            return Node(v[0:3], v[3], v[4], v[6], [0.5 * v[8]] + v[9:13])

        low_r, low_g, up_r, up_g = face_shares(side(zends, 16), side(znext, 0))
        for q in range(5):
            zacc[q, pl.ds(h * 8, 8), :] = low_r[q]
            zacc[5 + q, pl.ds(h * 8, 8), :] = low_g[q]
            zback[q, pl.ds(h * 8, 8), :] = up_r[q]
            zback[5 + q, pl.ds(h * 8, 8), :] = up_g[q]
    for k in range(16):
        zacc[:, pl.ds(16 + ids[k], 1), :] = zback[:, pl.ds(k, 1), :]

    def place(d, q):
        return q if q in (0, 4) else 1 + PERMS[d][q - 1]

    back = [[place(d, q) for q in range(5)] for d in range(3)]
    for group_at, target, offset in ((0, base, 0), (1, extra, 0), (2, base, 5), (3, extra, 5)):
        for q in range(5):
            first = group_at * 5
            qx = first + back[0].index(q)
            qy = first + back[1].index(q)
            qz = back[2].index(q)
            pieces = []
            for slot in range(16):
                h, s = slot // 8, slot % 8
                pieces.append(parts[2, first + qz, pl.ds(h * 64 + s, 8, stride=8), :])
            if group_at in (0, 2):
                source = qz + (0 if group_at == 0 else 5)
                sub = lax.broadcasted_iota(jnp.int32, (8, 128), 0)
                for slot in range(16):
                    upper = zacc[source, pl.ds(slot, 1), :]
                    lower = zacc[source, pl.ds(16 + slot, 1), :]
                    add = jnp.where(sub == 7, upper, jnp.where(sub == 0, lower, 0.0))
                    pieces[slot] = pieces[slot] + add
            whole = jnp.transpose(jnp.concatenate(pieces, axis=0))
            for h in range(2):
                for x in range(8):
                    value = (
                        parts[0, qx, pl.ds(h * 64 + 8 * x, 8), :]
                        + parts[1, qy, pl.ds(h * 64 + x, 8, stride=8), :]
                        + whole[h * 64 + 8 * x : h * 64 + 8 * x + 8]
                    )
                    target[offset + q, pl.ds(x * 16 + h * 8, 8), :] = value

    def own(direction, rows):
        return conserved_node([flow[q, rows, :] for q in range(5)], [cot[q, rows, :] for q in range(5)], direction)

    def add(direction, rows, res, grad):
        for q in range(5):
            p = place(direction, q)
            base[p, rows, :] += res[q]
            base[5 + p, rows, :] += grad[q]

    def near(ref, rows, direction):
        return conserved_node([ref[q, rows, :] for q in range(5)], [ref[5 + q, rows, :] for q in range(5)], direction)

    for h in range(2):
        here = pl.ds(h * 8, 8)
        top = pl.ds(112 + h * 8, 8)
        low_r, low_g, up_r, up_g = face_shares(near(x_left, here, 0), own(0, here))
        add(0, here, up_r, up_g)
        low_r, low_g, up_r, up_g = face_shares(own(0, top), near(x_right, here, 0))
        add(0, top, low_r, low_g)
    whole = pl.ds(0, 8)
    rows = [pl.ds(k, 8, stride=16) for k in (0, 7, 8, 15)]
    low_r, low_g, up_r, up_g = face_shares(near(y_left, whole, 1), own(1, rows[0]))
    add(1, rows[0], up_r, up_g)
    low_r, low_g, up_r, up_g = face_shares(own(1, rows[1]), own(1, rows[2]))
    add(1, rows[1], low_r, low_g)
    add(1, rows[2], up_r, up_g)
    low_r, low_g, up_r, up_g = face_shares(own(1, rows[3]), near(y_right, whole, 1))
    add(1, rows[3], low_r, low_g)

    sub = lax.broadcasted_iota(jnp.int32, (8, 128), 0)
    lane = lax.broadcasted_iota(jnp.int32, (8, 128), 1)
    high = (sub >= 6) | ((lane & 7) >= 6)
    tiles = []
    for h in range(2):
        d_top = msg[pl.ds(6 + h, 1), :]
        d_all = msg[pl.ds(8 + h, 1), :]
        both = d_top + d_all
        mixed = jnp.where(high, both, d_all)
        for x in range(8):
            tiles.append(modes[pl.ds(h * 64 + 8 * x, 8), :] * (both if x >= 6 else mixed))
    weighed = jnp.concatenate(tiles, axis=0)
    weighed = jnp.dot(kxyt[...], weighed, precision=HIGHEST, preferred_element_type=F32)
    weighed = jnp.dot(weighed, kz[...], precision=HIGHEST, preferred_element_type=F32)
    for h in range(2):
        for x in range(8):
            rows = pl.ds(x * 16 + h * 8, 8)
            density = flow[0, rows, :]
            inv = rcp(density)
            vel = [flow[1 + i, rows, :] * inv for i in range(3)]
            square = vel[0] * vel[0] + vel[1] * vel[1] + vel[2] * vel[2]
            pres = 0.4 * (flow[4, rows, :] - 0.5 * density * square)
            value = weighed[h * 64 + 8 * x : h * 64 + 8 * x + 8]
            pull_e = 0.4 * (value * density)
            slope[0, rows, :] = value * pres + (0.5 * pull_e) * square
            for i in range(3):
                slope[1 + i, rows, :] = -(pull_e * vel[i])
            slope[4, rows, :] = pull_e


def kernel_blend(ids, msg, from_left, from_right, from_low, from_up, base, extra, slope, residual, grad):
    row = lax.broadcasted_iota(jnp.int32, (128, 128), 0)
    lane = lax.broadcasted_iota(jnp.int32, (128, 128), 1)
    slot = lane >> 3
    above = jnp.zeros((128, 128), jnp.int32)
    for k in range(16):
        above = jnp.where(slot == k, ids[k], above)
    up = jnp.where((above * 8 + (lane & 7)) == row, 1.0, 0.0)
    own = msg[0:8, :]
    beside = jnp.dot(own, up, precision=HIGHEST, preferred_element_type=F32) + lax.dot_general(
        own, up, (((1,), (1,)), ((), ())), precision=HIGHEST, preferred_element_type=F32
    )
    beside = beside + from_left[0:8, :] + from_right[0:8, :]
    for h in range(2):
        def beside_of(i):
            low = from_low[2 * i + 1 : 2 * i + 2, :] if h == 0 else msg[2 * i : 2 * i + 1, :]
            high = msg[2 * i + 1 : 2 * i + 2, :] if h == 0 else from_up[2 * i : 2 * i + 1, :]
            return beside[2 * i + h : 2 * i + h + 1, :] + low + high

        alpha = msg[h : h + 1, :]
        gain = msg[4 + h : 5 + h, :]
        around = beside_of(0)
        smooth = alpha + (1.0 - alpha) * around * (0.5 / 6.0)
        pull = gain * (1.0 - around * (0.5 / 6.0)) + beside_of(1) * (0.5 / 6.0)
        smooth = jnp.broadcast_to(smooth, (8, 128))
        pull = jnp.broadcast_to(pull, (8, 128))
        for x in range(8):
            rows = pl.ds(x * 16 + h * 8, 8)
            for q in range(5):
                residual[q, rows, :] = base[q, rows, :] + smooth * extra[q, rows, :]
                grad[q, rows, :] = (
                    base[5 + q, rows, :] + smooth * extra[5 + q, rows, :] + pull * slope[q, rows, :]
                )


def shifted(value, axis, steps):
    count = lax.axis_size(axis)
    return lax.ppermute(value, axis, [(i, (i + steps) % count) for i in range(count)])


def shape(*dims):
    return jax.ShapeDtypeStruct(dims, F32)


def shards(flow_state, cotangent, clip_flags, successor_ids):
    flow = flow_state.reshape(5, ROWS, 128)
    cot = cotangent.reshape(5, ROWS, 128)
    vmem = pl.BlockSpec(memory_space=pltpu.VMEM)
    smem = pl.BlockSpec(memory_space=pltpu.SMEM)
    params = pltpu.CompilerParams(vmem_limit_bytes=48 * 1024 * 1024)

    both = jnp.concatenate([flow_state, cotangent], axis=0)
    x_left = shifted(both[:, 7], "gx", 1)
    x_right = shifted(both[:, 0], "gx", -1)
    y_left = shifted(both[:, :, 15], "gy", 1)
    y_right = shifted(both[:, :, 0], "gy", -1)

    modal = np.asarray(TO_MODAL, np.float32)
    kxy = np.kron(np.eye(2), np.kron(modal, modal)).astype(np.float32)
    kz = np.kron(np.eye(16), modal).astype(np.float32)
    group = np.kron(np.eye(16), np.ones((8, 8))).astype(np.float32)
    spread = np.kron(np.eye(16), np.ones((1, 8))).astype(np.float32)

    parts, zends, modes, msg = pl.pallas_call(
        kernel_volume,
        out_shape=(shape(3, 20, ROWS, 128), shape(NQ, 32, 128), shape(ROWS, 128), shape(16, 128)),
        in_specs=[vmem] * 7,
        out_specs=[vmem] * 4,
        scratch_shapes=[
            pltpu.VMEM((NQ, ROWS, 128), F32),
            pltpu.VMEM((NQ, ROWS, 128), F32),
            pltpu.VMEM((3, NQ, ROWS, 128), F32),
            pltpu.VMEM((ROWS, 128), F32),
            pltpu.VMEM((6, 8, 128), F32),
        ],
        compiler_params=params,
        name="volume",
    )(flow, cot, clip_flags.reshape(2, 16), kxy, np.ascontiguousarray(kz.T), group, spread)

    sent = msg[0:8]
    from_left = shifted(sent, "gx", 1)
    from_right = shifted(sent, "gx", -1)
    from_low = shifted(sent, "gy", 1)
    from_up = shifted(sent, "gy", -1)

    base, extra, slope = pl.pallas_call(
        kernel_faces,
        out_shape=(shape(10, ROWS, 128), shape(10, ROWS, 128), shape(5, ROWS, 128)),
        in_specs=[smem] + [vmem] * 12,
        out_specs=[vmem] * 3,
        scratch_shapes=[
            pltpu.VMEM((10, 32, 128), F32),
            pltpu.VMEM((NQ, 16, 128), F32),
            pltpu.VMEM((10, 16, 128), F32),
        ],
        compiler_params=params,
        name="faces",
    )(
        successor_ids, flow, cot, x_left, x_right, y_left, y_right, parts, zends, modes, msg,
        np.ascontiguousarray(kxy.T), kz,
    )

    residual, grad = pl.pallas_call(
        kernel_blend,
        out_shape=(shape(5, ROWS, 128), shape(5, ROWS, 128)),
        in_specs=[smem] + [vmem] * 8,
        out_specs=[vmem] * 2,
        compiler_params=params,
        name="blend",
    )(successor_ids, msg, from_left, from_right, from_low, from_up, base, extra, slope)
    return residual.reshape(flow_state.shape), grad.reshape(flow_state.shape)


def solution(mesh):
    placed = P(None, "gx", "gy", None)
    return jax.shard_map(
        shards,
        mesh=mesh,
        in_specs=(placed, placed, P("gx", "gy", None), P()),
        out_specs=(placed, placed),
        check_vma=False,
    )
```

```python
import jax
import jax.numpy as jnp
import numpy as np
from jax import lax
from jax.experimental import pallas as pl
from jax.experimental.pallas import tpu as pltpu
from jax.sharding import PartitionSpec as P
from numpy.polynomial import chebyshev, polynomial

F32 = jnp.float32
HIGHEST = lax.Precision.HIGHEST
EPS = 1e-05
PERMS = ((0, 1, 2), (1, 0, 2), (2, 0, 1))
NQ = 13
ROWS = 128


def legendre_values(points, node_count):
    values_table = np.zeros((points.shape[0], node_count))
    values_table[:, 0] = 1.0
    values_table[:, 1] = points
    for degree_index in range(2, node_count):
        values_table[:, degree_index] = (
            (2 * degree_index - 1) * points * values_table[:, degree_index - 1]
            - (degree_index - 1) * values_table[:, degree_index - 2]
        ) / degree_index
    return values_table


def node_tables():
    degree = 7
    node_count = degree + 1
    points = -np.cos(np.pi * np.arange(node_count) / degree)
    for newton_step in range(60):
        legend = legendre_values(points, node_count)
        points = points - (points * legend[:, degree] - legend[:, degree - 1]) / (
            node_count * legend[:, degree]
        )
    legend = legendre_values(points, node_count)
    weights = 2.0 / (degree * node_count * legend[:, degree] * legend[:, degree])
    differ = np.zeros((node_count, node_count))
    for row_index in range(node_count):
        for col_index in range(node_count):
            if row_index != col_index:
                differ[row_index, col_index] = legend[row_index, degree] / (
                    legend[col_index, degree] * (points[row_index] - points[col_index])
                )
    norm_table = 2.0 / (2.0 * np.arange(node_count) + 1.0)
    norm_table[degree] = 2.0 / degree
    to_modal = legend.T * weights[None, :] / norm_table[:, None]
    return (weights, differ, to_modal)


WEIGHTS, DIFFER, TO_MODAL = node_tables()
INV_W = [float(1.0 / w) for w in WEIGHTS]
SKEW = 2.0 * DIFFER * WEIGHTS[:, None]


def fitted(function, top, degree):
    series = chebyshev.Chebyshev.interpolate(function, degree, domain=[0.0, top])
    return [float(np.float32(c)) for c in series.convert(kind=polynomial.Polynomial).coef]


def sinhc(square):
    root = np.sqrt(np.maximum(square, 1e-12))
    return np.sinh(root) / root


def sinhc_slope(square):
    root = np.sqrt(np.maximum(square, 1e-12))
    exact = (np.cosh(root) - np.sinh(root) / root) / (root * root)
    series = 1.0 / 3.0 + square / 30.0 + square**2 / 840.0 + square**3 / 45360.0
    return np.where(square < 1e-2, series, exact)


MEAN_R = fitted(sinhc, 3.0, 4)
SLOPE_R = fitted(sinhc_slope, 3.0, 3)
MEAN_B = fitted(sinhc, 12.0, 5)
SLOPE_B = fitted(sinhc_slope, 12.0, 5)


def horner(coeffs, value):
    total = coeffs[-1] * value + coeffs[-2]
    for c in coeffs[-3::-1]:
        total = total * value + c
    return total


def rcp(value):
    return 1.0 / value


def log_parts(density, pressure):
    inv = rcp(density)
    ratio = pressure * inv
    half_log = 0.5 * jnp.log(density)
    return (
        jnp.sqrt(density),
        half_log,
        jnp.sqrt(5.0 * ratio),
        half_log - 0.5 * jnp.log(pressure),
    )


class Node:
    def __init__(self, vel, pres, root, theta, cot):
        self.vel, self.pres, self.cot = vel, pres, cot
        density = root * root
        vn, v1, v2 = vel
        mom = [density * v for v in vel]
        self.square = vn * vn + v1 * v1 + v2 * v2
        energy = 2.5 * pres + (0.5 * density) * self.square
        self.state = [density] + mom + [energy]
        mn = mom[0]
        self.flux = [mn, mn * vn + pres, mn * v1, mn * v2, (energy + pres) * vn]
        self.sound = theta * float(np.sqrt(1.4 / 5.0))
        self.speed = jnp.abs(vn) + self.sound

    def pull(self, half, direct, speed_cot):
        density = self.state[0]
        vn, v1, v2 = self.vel
        grad = [direct[i] + half[i] * vn for i in range(5)]
        sign = jnp.where(vn >= 0.0, 1.0, -1.0)
        dvn = half[0] * self.state[0]
        for i in range(1, 5):
            dvn = dvn + half[i] * self.state[i]
        dvn = dvn + half[4] * self.pres + speed_cot * sign
        inv = rcp(density)
        part = (0.5 * speed_cot) * self.sound
        dpres = half[1] + half[4] * vn + part * rcp(self.pres)
        over = dvn * inv
        pull_e = 0.4 * dpres
        grad[0] = grad[0] - part * inv - over * vn + (0.5 * pull_e) * self.square
        grad[1] = grad[1] + over - pull_e * vn
        grad[2] = grad[2] - pull_e * v1
        grad[3] = grad[3] - pull_e * v2
        grad[4] = grad[4] + pull_e
        return grad


def face(low, up):
    jump = [b - a for a, b in zip(low.state, up.state)]
    weight = [b - a for a, b in zip(low.cot, up.cot)]
    half_speed = 0.25 * (low.speed + up.speed)
    flux = [0.5 * (a + b) - half_speed * j for a, b, j in zip(low.flux, up.flux, jump)]
    dot = weight[0] * jump[0]
    for i in range(1, 5):
        dot = dot + weight[i] * jump[i]
    direct = [half_speed * w for w in weight]
    return flux, weight, direct, -0.25 * dot


def kernel_volume(
    flow_hbm,
    cot_hbm,
    flags_hbm,
    tables_hbm,
    out,
    zends,
    modes,
    msg,
    to_right,
    to_left,
    to_up,
    to_low,
    flow,
    cot,
    tables,
    nat,
    turned,
    lines,
    prod,
    gsum,
    flags,
    sems,
):
    copies = [
        pltpu.make_async_copy(source, target, sems.at[i])
        for i, (source, target) in enumerate(
            ((flow_hbm, flow), (cot_hbm, cot), (tables_hbm, tables), (flags_hbm, flags))
        )
    ]
    for copy in copies:
        copy.start()
    copies[0].wait()
    copies[1].wait()
    for c in range(10):
        source, q = (flow, c) if c < 5 else (cot, c - 5)
        to_right[pl.ds(16 * c, 16), :] = source[q, pl.ds(112, 16), :]
        to_left[pl.ds(16 * c, 16), :] = source[q, pl.ds(0, 16), :]
        to_up[pl.ds(8 * c, 8), :] = source[q, pl.ds(15, 8, stride=16), :]
        to_low[pl.ds(8 * c, 8), :] = source[q, pl.ds(0, 8, stride=16), :]

    for x in range(8):
        for h in range(2):
            src = pl.ds(x * 16 + h * 8, 8)
            dst = pl.ds(h * 64 + x * 8, 8)
            density = flow[0, src, :]
            inv = rcp(density)
            mom = [flow[1 + i, src, :] for i in range(3)]
            vel = [m * inv for m in mom]
            kinetic = mom[0] * vel[0] + mom[1] * vel[1] + mom[2] * vel[2]
            pres = 0.4 * (flow[4, src, :] - 0.5 * kinetic)
            prod[dst, :] = density * pres
            parts = vel + [pres] + list(log_parts(density, pres))
            for q in range(8):
                nat[q, dst, :] = parts[q]
            for q in range(5):
                value = cot[q, src, :]
                nat[8 + q, dst, :] = 2.0 * value if q == 0 else value
    for q in range(NQ):
        turned[q] = jnp.transpose(nat[q])
    for d in range(3):
        perm = PERMS[d]
        order = [perm[0], perm[1], perm[2], 3, 4, 5, 6, 7, 8] + [9 + i for i in perm] + [12]
        source = nat if d < 2 else turned
        for q in range(NQ):
            for h in range(2):
                for k in range(8):
                    rows = pl.ds(h * 64 + 8 * k, 8) if d == 0 else pl.ds(h * 64 + k, 8, stride=8)
                    value = source[order[q], rows, :]
                    lines[d, q, pl.ds(h * 64 + 8 * k, 8), :] = value * INV_W[k] if q >= 8 else value
    for q in range(NQ):
        for end in range(2):
            for h in range(2):
                zends[q, pl.ds(end * 16 + h * 8, 8), :] = lines[2, q, pl.ds(h * 64 + 56 * end, 8), :]

    def one(step, carry):
        d = step // 2
        base = (step % 2) * 64

        def rows(k):
            return pl.ds(pl.multiple_of(base + 8 * k, 8), 8)

        for k in range(7):
            a = [lines[d, q, rows(k), :] for q in range(NQ)]
            acc = [None] * 11 if k == 0 else [out[d, q, rows(k), :] for q in range(11)]
            for j in range(k + 1, 8):
                skew = float(SKEW[k, j])
                b = [lines[d, q, rows(j), :] for q in range(NQ)]
                vn, v1, v2 = (a[i] + b[i] for i in range(3))
                delta = [a[8 + i] - b[8 + i] for i in range(5)]
                y = a[5] - b[5]
                square = y * y
                scale = (0.25 * skew) * (a[4] * b[4])
                mean = scale * horner(MEAN_R, square)
                slope = (scale * y) * horner(SLOPE_R, square)
                yb = a[7] - b[7]
                square_b = yb * yb
                quot = rcp(horner(MEAN_B, square_b))
                inv5 = (a[6] * b[6]) * quot
                tilt = yb * (horner(SLOPE_B, square_b) * quot)
                dot = a[0] * b[0] + a[1] * b[1] + a[2] * b[2] + inv5
                mass = mean * vn
                half = 0.5 * skew
                flux = [
                    mass,
                    mass * vn + half * (a[3] + b[3]),
                    mass * v1,
                    mass * v2,
                    mass * dot + half * (a[3] * b[0] + b[3] * a[0]),
                ]
                phi = delta[0] + delta[1] * vn + delta[2] * v1 + delta[3] * v2 + delta[4] * dot
                common = phi * mean + delta[1] * mass
                t = half * delta[4]
                u = half * delta[1]
                w = mass * delta[4]
                r1 = mass * delta[2]
                r2 = mass * delta[3]
                pp = phi * mass
                qq = (phi * vn) * slope
                xx = w * inv5
                zz = xx * tilt
                grad_a = [
                    pp + qq,
                    common + w * b[0] + t * b[3],
                    r1 + w * b[1],
                    r2 + w * b[2],
                    u + t * b[0],
                    xx + zz,
                ]
                grad_b = [
                    pp - qq,
                    common + w * a[0] + t * a[3],
                    r1 + w * a[1],
                    r2 + w * a[2],
                    u + t * a[0],
                    xx - zz,
                ]
                for q in range(5):
                    acc[q] = flux[q] if acc[q] is None else acc[q] + flux[q]
                    before = 0.0 if k == 0 else out[d, q, rows(j), :]
                    out[d, q, rows(j), :] = before - flux[q]
                for q in range(6):
                    acc[5 + q] = grad_a[q] if acc[5 + q] is None else acc[5 + q] + grad_a[q]
                    out[d, 5 + q, rows(j), :] = grad_b[q] if k == 0 else out[d, 5 + q, rows(j), :] + grad_b[q]
            for q in range(11):
                out[d, q, rows(k), :] = acc[q]

        low = None
        zero = jnp.zeros((8, 128), F32)
        low_flux, low_weight, low_direct, low_dot = [zero] * 5, [zero] * 5, [zero] * 5, zero
        gained = zero
        for k in range(9):
            if k < 8:
                a = [lines[d, q, rows(k), :] for q in range(NQ)]
                node = Node(a[0:3], a[3], a[4], a[6], [0.5 * a[8]] + a[9:13])
            if k == 0:
                low = node
                continue
            if k < 8:
                flux, weight, direct, dot = face(low, node)
            else:
                flux, weight, direct, dot = [zero] * 5, [zero] * 5, [zero] * 5, zero
            m = k - 1
            total = [out[d, q, rows(m), :] for q in range(11)]
            total[0] = 2.0 * total[0]
            for q in range(5):
                diff = total[q] - (flux[q] - low_flux[q])
                gained = gained + low.cot[q] * diff
                out[d, q, rows(m), :] = total[q] * (-INV_W[m])
                out[d, 5 + q, rows(m), :] = diff * INV_W[m]
            fv = low.pull(
                [0.5 * (x + z) for x, z in zip(low_weight, weight)],
                [x - z for x, z in zip(direct, low_direct)],
                low_dot + dot,
            )
            inv = rcp(low.state[0])
            beta = 0.5 * total[10]
            g_rho = (beta - 0.5 * total[5]) * inv
            g_e = -0.4 * (total[9] + beta * rcp(low.pres))
            g_m = [-(total[6 + i] * inv) - g_e * low.vel[i] for i in range(3)]
            inner = g_m[0] * low.vel[0] + g_m[1] * low.vel[1] + g_m[2] * low.vel[2]
            dg = [g_rho - inner - (0.5 * g_e) * low.square] + g_m + [g_e]
            for q in range(5):
                out[d, 10 + q, rows(m), :] = dg[q]
                out[d, 15 + q, rows(m), :] = fv[q] - dg[q]
            low, low_flux, low_weight, low_direct, low_dot = node, flux, weight, direct, dot
        gsum[step] = gained
        return carry

    lax.fori_loop(0, 6, one, 0)

    copies[2].wait()
    copies[3].wait()
    coeffs = jnp.dot(tables[0], prod[...], precision=HIGHEST, preferred_element_type=F32)
    coeffs = jnp.dot(coeffs, tables[1], precision=HIGHEST, preferred_element_type=F32)
    modes[...] = coeffs
    squares = coeffs * coeffs
    sub = lax.broadcasted_iota(jnp.int32, (8, 128), 0)
    lane = lax.broadcasted_iota(jnp.int32, (8, 128), 1)
    high = (sub >= 6) | ((lane & 7) >= 6)
    packed = jnp.zeros((8, 128), F32)
    tops, alls, gains = [], [], []
    for h in range(2):
        every = squares[h * 64 : h * 64 + 8]
        for x in range(1, 6):
            every = every + squares[h * 64 + 8 * x : h * 64 + 8 * x + 8]
        ends = squares[h * 64 + 48 : h * 64 + 56] + squares[h * 64 + 56 : h * 64 + 64]
        tops.append(jnp.sum(jnp.where(high, every, 0.0) + ends, axis=0, keepdims=True))
        alls.append(jnp.sum(every + ends, axis=0, keepdims=True))
        gains.append(jnp.sum(gsum[h] + gsum[2 + h], axis=0, keepdims=True))
    for i, row in enumerate(tops + alls + gains):
        packed = jnp.where(sub == i, row, packed)
    group = jnp.where(
        lax.broadcasted_iota(jnp.int32, (128, 128), 0) >> 3
        == lax.broadcasted_iota(jnp.int32, (128, 128), 1) >> 3,
        1.0,
        0.0,
    )
    spread = jnp.where(
        lax.broadcasted_iota(jnp.int32, (16, 128), 0)
        == lax.broadcasted_iota(jnp.int32, (16, 128), 1) >> 3,
        1.0,
        0.0,
    )
    sums = jnp.dot(packed, group, precision=HIGHEST, preferred_element_type=F32)
    along = jnp.concatenate([gsum[4], gsum[5]], axis=0)
    left = jnp.where(((sub == 4) & (lane < 64)) | ((sub == 5) & (lane >= 64)), 1.0, 0.0)
    per_slot = lax.dot_general(
        left, along, (((1,), (1,)), ((), ())), precision=HIGHEST, preferred_element_type=F32
    )
    sums = sums + jnp.dot(per_slot, spread, precision=HIGHEST, preferred_element_type=F32)
    flag_rows = jnp.dot(
        flags[...].astype(F32), spread, precision=HIGHEST, preferred_element_type=F32
    )
    packed = jnp.zeros((16, 128), F32)
    sub16 = lax.broadcasted_iota(jnp.int32, (16, 128), 0)
    for h in range(2):
        top = sums[h : h + 1] + EPS
        every = 0.01 * (sums[2 + h : 3 + h] + EPS)
        gain = sums[4 + h : 5 + h]
        flag = flag_rows[h : h + 1]
        over = rcp(top + every)
        keep = flag < 0.5
        alpha = jnp.where(keep, 0.5 * top * over, jnp.where(flag > 1.5, 0.5, 0.0))
        d_top = jnp.where(keep, every * over * over, 0.0)
        d_all = jnp.where(keep, -0.01 * top * over * over, 0.0)
        for i, row in enumerate((alpha, gain * (1.0 - alpha), gain, d_top, d_all)):
            packed = jnp.where(sub16 == 2 * i + h, row, packed)
    msg[...] = packed
    for target, row in ((to_right, 160), (to_left, 160), (to_up, 80), (to_low, 80)):
        target[pl.ds(row, 8), :] = packed[0:8]


def conserved_node(state, cot, direction):
    perm = PERMS[direction]
    density = state[0]
    inv = rcp(density)
    vel = [state[1 + i] * inv for i in perm]
    square = vel[0] * vel[0] + vel[1] * vel[1] + vel[2] * vel[2]
    pres = 0.4 * (state[4] - 0.5 * density * square)
    scaled = [cot[0]] + [cot[1 + i] for i in perm] + [cot[4]]
    return Node(vel, pres, jnp.sqrt(density), jnp.sqrt(5.0 * pres * inv), [c * INV_W[0] for c in scaled])


def face_shares(low, up):
    flux, weight, direct, dot = face(low, up)
    half = [0.5 * w for w in weight]
    return (
        [-INV_W[7] * f for f in flux],
        low.pull(half, direct, dot),
        [INV_W[0] * f for f in flux],
        up.pull(half, [-x for x in direct], dot),
    )


def place(d, q):
    return q if q in (0, 4) else 1 + PERMS[d][q - 1]


def own_node(flow, cot, direction, rows):
    return conserved_node(
        [flow[q, rows, :] for q in range(5)], [cot[q, rows, :] for q in range(5)], direction
    )


def near_node(ref, count, start, direction):
    return conserved_node(
        [ref[pl.ds(q * count + start, 8), :] for q in range(5)],
        [ref[pl.ds((5 + q) * count + start, 8), :] for q in range(5)],
        direction,
    )


def kernel_local(
    ids_hbm,
    flow,
    cot,
    parts,
    zends,
    modes,
    msg,
    tables,
    base,
    extra,
    slope,
    zsum,
    zacc,
    znext,
    zback,
    ids,
    sem,
):
    copy = pltpu.make_async_copy(ids_hbm, ids, sem)
    copy.start()

    sub = lax.broadcasted_iota(jnp.int32, (8, 128), 0)
    lane = lax.broadcasted_iota(jnp.int32, (8, 128), 1)
    high = (sub >= 6) | ((lane & 7) >= 6)
    tiles = []
    for h in range(2):
        d_top = msg[pl.ds(6 + h, 1), :]
        d_all = msg[pl.ds(8 + h, 1), :]
        both = d_top + d_all
        mixed = jnp.where(high, both, d_all)
        for x in range(8):
            tiles.append(modes[pl.ds(h * 64 + 8 * x, 8), :] * (both if x >= 6 else mixed))
    weighed = jnp.concatenate(tiles, axis=0)
    weighed = jnp.dot(tables[2], weighed, precision=HIGHEST, preferred_element_type=F32)
    weighed = jnp.dot(weighed, tables[3], precision=HIGHEST, preferred_element_type=F32)
    for h in range(2):
        for x in range(8):
            rows = pl.ds(x * 16 + h * 8, 8)
            density = flow[0, rows, :]
            inv = rcp(density)
            vel = [flow[1 + i, rows, :] * inv for i in range(3)]
            square = vel[0] * vel[0] + vel[1] * vel[1] + vel[2] * vel[2]
            pres = 0.4 * (flow[4, rows, :] - 0.5 * density * square)
            value = weighed[h * 64 + 8 * x : h * 64 + 8 * x + 8]
            pull_e = 0.4 * (value * density)
            slope[0, rows, :] = value * pres + (0.5 * pull_e) * square
            for i in range(3):
                slope[1 + i, rows, :] = -(pull_e * vel[i])
            slope[4, rows, :] = pull_e

    copy.wait()
    row = lax.broadcasted_iota(jnp.int32, (128, 128), 0)
    lanes = lax.broadcasted_iota(jnp.int32, (8, 128), 1)
    above = jnp.zeros((8, 128), jnp.int32)
    for k in range(16):
        above = jnp.where((lanes >> 3) == k, ids[k], above)
    above = above * 8 + (lanes & 7)
    above = jnp.concatenate([above] * 16, axis=0)
    up = jnp.where(above == row, 1.0, 0.0)
    own = msg[0:8, :]
    zsum[...] = jnp.dot(own, up, precision=HIGHEST, preferred_element_type=F32) + lax.dot_general(
        own, up, (((1,), (1,)), ((), ())), precision=HIGHEST, preferred_element_type=F32
    )

    for k in range(16):
        znext[:, pl.ds(k, 1), :] = zends[:, pl.ds(ids[k], 1), :]
    for h in range(2):
        def side(ref, start):
            v = [ref[q, pl.ds(start + h * 8, 8), :] for q in range(NQ)]
            return Node(v[0:3], v[3], v[4], v[6], [0.5 * v[8]] + v[9:13])

        low_r, low_g, up_r, up_g = face_shares(side(zends, 16), side(znext, 0))
        for q in range(5):
            zacc[q, pl.ds(h * 8, 8), :] = low_r[q]
            zacc[5 + q, pl.ds(h * 8, 8), :] = low_g[q]
            zback[q, pl.ds(h * 8, 8), :] = up_r[q]
            zback[5 + q, pl.ds(h * 8, 8), :] = up_g[q]
    for k in range(16):
        zacc[:, pl.ds(16 + ids[k], 1), :] = zback[:, pl.ds(k, 1), :]

    back = [[place(d, q) for q in range(5)] for d in range(3)]
    for group_at, target, offset in ((0, base, 0), (1, extra, 0), (2, base, 5), (3, extra, 5)):
        for q in range(5):
            first = group_at * 5
            qx = first + back[0].index(q)
            qy = first + back[1].index(q)
            qz = back[2].index(q)
            pieces = []
            for slot in range(16):
                h, s = slot // 8, slot % 8
                pieces.append(parts[2, first + qz, pl.ds(h * 64 + s, 8, stride=8), :])
            if group_at in (0, 2):
                source = qz + (0 if group_at == 0 else 5)
                sub = lax.broadcasted_iota(jnp.int32, (8, 128), 0)
                for slot in range(16):
                    upper = zacc[source, pl.ds(slot, 1), :]
                    lower = zacc[source, pl.ds(16 + slot, 1), :]
                    add = jnp.where(sub == 7, upper, jnp.where(sub == 0, lower, 0.0))
                    pieces[slot] = pieces[slot] + add
            whole = jnp.transpose(jnp.concatenate(pieces, axis=0))
            for h in range(2):
                for x in range(8):
                    value = (
                        parts[0, qx, pl.ds(h * 64 + 8 * x, 8), :]
                        + parts[1, qy, pl.ds(h * 64 + x, 8, stride=8), :]
                        + whole[h * 64 + 8 * x : h * 64 + 8 * x + 8]
                    )
                    target[offset + q, pl.ds(x * 16 + h * 8, 8), :] = value

    rows = [pl.ds(7, 8, stride=16), pl.ds(8, 8, stride=16)]
    shares = face_shares(own_node(flow, cot, 1, rows[0]), own_node(flow, cot, 1, rows[1]))
    for side in range(2):
        for q in range(5):
            p = place(1, q)
            base[p, rows[side], :] += shares[2 * side][q]
            base[5 + p, rows[side], :] += shares[2 * side + 1][q]


def kernel_blend(
    msg,
    zsum,
    from_left,
    from_right,
    from_low,
    from_up,
    flow,
    cot,
    base,
    extra,
    slope,
    residual_hbm,
    grad_hbm,
    total,
    sems,
):
    for h in range(2):

        def beside_of(i):
            r = 2 * i + h
            low = from_low[81 + 2 * i : 82 + 2 * i, :] if h == 0 else msg[2 * i : 2 * i + 1, :]
            high = msg[2 * i + 1 : 2 * i + 2, :] if h == 0 else from_up[80 + 2 * i : 81 + 2 * i, :]
            return (
                zsum[r : r + 1, :]
                + from_left[160 + r : 161 + r, :]
                + from_right[160 + r : 161 + r, :]
                + low
                + high
            )

        alpha = msg[h : h + 1, :]
        gain = msg[4 + h : 5 + h, :]
        around = beside_of(0)
        smooth = alpha + (1.0 - alpha) * around * (0.5 / 6.0)
        pull = gain * (1.0 - around * (0.5 / 6.0)) + beside_of(1) * (0.5 / 6.0)
        smooth = jnp.broadcast_to(smooth, (8, 128))
        pull = jnp.broadcast_to(pull, (8, 128))
        for x in range(8):
            rows = pl.ds(x * 16 + h * 8, 8)
            for q in range(5):
                total[q, rows, :] = base[q, rows, :] + smooth * extra[q, rows, :]
                total[5 + q, rows, :] = (
                    base[5 + q, rows, :] + smooth * extra[5 + q, rows, :] + pull * slope[q, rows, :]
                )

    def add(direction, rows, res, grad):
        for q in range(5):
            p = place(direction, q)
            total[p, rows, :] += res[q]
            total[5 + p, rows, :] += grad[q]

    for h in range(2):
        here, top = pl.ds(h * 8, 8), pl.ds(112 + h * 8, 8)
        shares = face_shares(near_node(from_left, 16, h * 8, 0), own_node(flow, cot, 0, here))
        add(0, here, shares[2], shares[3])
        shares = face_shares(own_node(flow, cot, 0, top), near_node(from_right, 16, h * 8, 0))
        add(0, top, shares[0], shares[1])
    here, top = pl.ds(0, 8, stride=16), pl.ds(15, 8, stride=16)
    shares = face_shares(near_node(from_low, 8, 0, 1), own_node(flow, cot, 1, here))
    add(1, here, shares[2], shares[3])
    shares = face_shares(own_node(flow, cot, 1, top), near_node(from_up, 8, 0, 1))
    add(1, top, shares[0], shares[1])
    copies = [
        pltpu.make_async_copy(total.at[pl.ds(0, 5)], residual_hbm, sems.at[0]),
        pltpu.make_async_copy(total.at[pl.ds(5, 5)], grad_hbm, sems.at[1]),
    ]
    for copy in copies:
        copy.start()
    for copy in copies:
        copy.wait()


def shifted(value, axis, steps):
    count = lax.axis_size(axis)
    return lax.ppermute(value, axis, [(i, (i + steps) % count) for i in range(count)])


def shape(*dims):
    return jax.ShapeDtypeStruct(dims, F32)


def in_hbm(value):
    return pltpu.with_memory_space_constraint(value, pltpu.HBM)


def shards(flow_state, cotangent, clip_flags, successor_ids):
    flow = flow_state.reshape(5, ROWS, 128)
    cot = cotangent.reshape(5, ROWS, 128)
    vmem = pl.BlockSpec(memory_space=pltpu.VMEM)
    hbm = pl.BlockSpec(memory_space=pltpu.HBM)
    modal = np.asarray(TO_MODAL, np.float32)
    kxy = np.kron(np.eye(2), np.kron(modal, modal)).astype(np.float32)
    kz = np.kron(np.eye(16), modal).astype(np.float32)
    constants = np.stack([kxy, kz.T, kxy.T, kz])

    parts, zends, modes, msg, to_right, to_left, to_up, to_low, flow_v, cot_v, tables = pl.pallas_call(
        kernel_volume,
        out_shape=(
            shape(3, 20, ROWS, 128),
            shape(NQ, 32, 128),
            shape(ROWS, 128),
            shape(16, 128),
            shape(168, 128),
            shape(168, 128),
            shape(88, 128),
            shape(88, 128),
            shape(5, ROWS, 128),
            shape(5, ROWS, 128),
            shape(4, 128, 128),
        ),
        in_specs=[hbm] * 4,
        out_specs=[vmem] * 11,
        scratch_shapes=[
            pltpu.VMEM((NQ, ROWS, 128), F32),
            pltpu.VMEM((NQ, ROWS, 128), F32),
            pltpu.VMEM((3, NQ, ROWS, 128), F32),
            pltpu.VMEM((ROWS, 128), F32),
            pltpu.VMEM((6, 8, 128), F32),
            pltpu.VMEM((2, 16), jnp.int32),
            pltpu.SemaphoreType.DMA((4,)),
        ],
        compiler_params=pltpu.CompilerParams(vmem_limit_bytes=20 * 1024 * 1024),
        name="volume",
    )(in_hbm(flow), in_hbm(cot), in_hbm(clip_flags.reshape(2, 16)), in_hbm(jnp.asarray(constants)))

    from_low = shifted(to_up, "gy", 1)
    from_up = shifted(to_low, "gy", -1)
    from_left = shifted(to_right, "gx", 1)
    from_right = shifted(to_left, "gx", -1)

    base, extra, slope, zsum = pl.pallas_call(
        kernel_local,
        out_shape=(shape(10, ROWS, 128), shape(10, ROWS, 128), shape(5, ROWS, 128), shape(8, 128)),
        in_specs=[hbm] + [vmem] * 7,
        out_specs=[vmem] * 4,
        scratch_shapes=[
            pltpu.VMEM((10, 32, 128), F32),
            pltpu.VMEM((NQ, 16, 128), F32),
            pltpu.VMEM((10, 16, 128), F32),
            pltpu.SMEM((16,), jnp.int32),
            pltpu.SemaphoreType.DMA(()),
        ],
        compiler_params=pltpu.CompilerParams(vmem_limit_bytes=16 * 1024 * 1024),
        name="local",
    )(in_hbm(successor_ids), flow_v, cot_v, parts, zends, modes, msg, tables)

    residual, grad = pl.pallas_call(
        kernel_blend,
        out_shape=(shape(5, ROWS, 128), shape(5, ROWS, 128)),
        in_specs=[vmem] * 11,
        out_specs=[hbm] * 2,
        scratch_shapes=[pltpu.VMEM((10, ROWS, 128), F32), pltpu.SemaphoreType.DMA((2,))],
        compiler_params=pltpu.CompilerParams(vmem_limit_bytes=16 * 1024 * 1024),
        name="blend",
    )(msg, zsum, from_left, from_right, from_low, from_up, flow_v, cot_v, base, extra, slope)
    return residual.reshape(flow_state.shape), grad.reshape(flow_state.shape)


def solution(mesh):
    placed = P(None, "gx", "gy", None)
    return jax.shard_map(
        shards,
        mesh=mesh,
        in_specs=(placed, placed, P("gx", "gy", None), P()),
        out_specs=(placed, placed),
        check_vma=False,
    )
```

```python
import jax
import jax.numpy as jnp
import numpy as np
from jax import lax
from jax.experimental import pallas as pl
from jax.experimental.pallas import tpu as pltpu
from jax.sharding import PartitionSpec as P
from numpy.polynomial import chebyshev, polynomial

F32 = jnp.float32
HIGHEST = lax.Precision.HIGHEST
EPS = 1e-05
PERMS = ((0, 1, 2), (1, 0, 2), (2, 0, 1))
NQ = 13
ROWS = 128


def legendre_values(points, node_count):
    values_table = np.zeros((points.shape[0], node_count))
    values_table[:, 0] = 1.0
    values_table[:, 1] = points
    for degree_index in range(2, node_count):
        values_table[:, degree_index] = (
            (2 * degree_index - 1) * points * values_table[:, degree_index - 1]
            - (degree_index - 1) * values_table[:, degree_index - 2]
        ) / degree_index
    return values_table


def node_tables():
    degree = 7
    node_count = degree + 1
    points = -np.cos(np.pi * np.arange(node_count) / degree)
    for newton_step in range(60):
        legend = legendre_values(points, node_count)
        points = points - (points * legend[:, degree] - legend[:, degree - 1]) / (
            node_count * legend[:, degree]
        )
    legend = legendre_values(points, node_count)
    weights = 2.0 / (degree * node_count * legend[:, degree] * legend[:, degree])
    differ = np.zeros((node_count, node_count))
    for row_index in range(node_count):
        for col_index in range(node_count):
            if row_index != col_index:
                differ[row_index, col_index] = legend[row_index, degree] / (
                    legend[col_index, degree] * (points[row_index] - points[col_index])
                )
    norm_table = 2.0 / (2.0 * np.arange(node_count) + 1.0)
    norm_table[degree] = 2.0 / degree
    to_modal = legend.T * weights[None, :] / norm_table[:, None]
    return (weights, differ, to_modal)


WEIGHTS, DIFFER, TO_MODAL = node_tables()
INV_W = [float(1.0 / w) for w in WEIGHTS]
SKEW = 2.0 * DIFFER * WEIGHTS[:, None]


def fitted(function, top, degree):
    series = chebyshev.Chebyshev.interpolate(function, degree, domain=[0.0, top])
    return [float(np.float32(c)) for c in series.convert(kind=polynomial.Polynomial).coef]


def sinhc(square):
    root = np.sqrt(np.maximum(square, 1e-12))
    return np.sinh(root) / root


def sinhc_slope(square):
    root = np.sqrt(np.maximum(square, 1e-12))
    exact = (np.cosh(root) - np.sinh(root) / root) / (root * root)
    series = 1.0 / 3.0 + square / 30.0 + square**2 / 840.0 + square**3 / 45360.0
    return np.where(square < 1e-2, series, exact)


PAIR = {pair: i for i, pair in enumerate((k, j) for k in range(7) for j in range(k + 1, 8))}

MEAN_R = fitted(sinhc, 3.0, 4)
SLOPE_R = fitted(sinhc_slope, 3.0, 3)
MEAN_B = fitted(sinhc, 12.0, 5)
SLOPE_B = fitted(sinhc_slope, 12.0, 5)


def horner(coeffs, value):
    total = coeffs[-1] * value + coeffs[-2]
    for c in coeffs[-3::-1]:
        total = total * value + c
    return total


def rcp(value):
    return 1.0 / value


def log_parts(density, pressure):
    inv = rcp(density)
    ratio = pressure * inv
    half_log = 0.5 * jnp.log(density)
    return (
        jnp.sqrt(density),
        half_log,
        jnp.sqrt(5.0 * ratio),
        half_log - 0.5 * jnp.log(pressure),
    )


class Node:
    def __init__(self, vel, pres, root, theta, cot):
        self.vel, self.pres, self.cot = vel, pres, cot
        density = root * root
        vn, v1, v2 = vel
        mom = [density * v for v in vel]
        self.square = vn * vn + v1 * v1 + v2 * v2
        energy = 2.5 * pres + (0.5 * density) * self.square
        self.state = [density] + mom + [energy]
        mn = mom[0]
        self.flux = [mn, mn * vn + pres, mn * v1, mn * v2, (energy + pres) * vn]
        self.sound = theta * float(np.sqrt(1.4 / 5.0))
        self.speed = jnp.abs(vn) + self.sound

    def pull(self, half, direct, speed_cot):
        density = self.state[0]
        vn, v1, v2 = self.vel
        grad = [direct[i] + half[i] * vn for i in range(5)]
        sign = jnp.where(vn >= 0.0, 1.0, -1.0)
        dvn = half[0] * self.state[0]
        for i in range(1, 5):
            dvn = dvn + half[i] * self.state[i]
        dvn = dvn + half[4] * self.pres + speed_cot * sign
        inv = rcp(density)
        part = (0.5 * speed_cot) * self.sound
        dpres = half[1] + half[4] * vn + part * rcp(self.pres)
        over = dvn * inv
        pull_e = 0.4 * dpres
        grad[0] = grad[0] - part * inv - over * vn + (0.5 * pull_e) * self.square
        grad[1] = grad[1] + over - pull_e * vn
        grad[2] = grad[2] - pull_e * v1
        grad[3] = grad[3] - pull_e * v2
        grad[4] = grad[4] + pull_e
        return grad


def face(low, up):
    jump = [b - a for a, b in zip(low.state, up.state)]
    weight = [b - a for a, b in zip(low.cot, up.cot)]
    half_speed = 0.25 * (low.speed + up.speed)
    flux = [0.5 * (a + b) - half_speed * j for a, b, j in zip(low.flux, up.flux, jump)]
    dot = weight[0] * jump[0]
    for i in range(1, 5):
        dot = dot + weight[i] * jump[i]
    direct = [half_speed * w for w in weight]
    return flux, weight, direct, -0.25 * dot


def lane_tables():
    sub = lax.broadcasted_iota(jnp.int32, (8, 128), 0)
    lane = lax.broadcasted_iota(jnp.int32, (8, 128), 1)
    return sub, lane, (sub >= 6) | ((lane & 7) >= 6)


def kernel_first(
    flow_hbm,
    cot_hbm,
    flags_hbm,
    tables_hbm,
    lines,
    mid,
    modes,
    msg,
    to_partner,
    to_other,
    to_ahead,
    to_behind,
    flow,
    cot,
    tables,
    nat,
    turned,
    prod,
    gsum,
    flags,
    sems,
):
    copies = [
        pltpu.make_async_copy(source, target, sems.at[i])
        for i, (source, target) in enumerate(
            ((flow_hbm, flow), (cot_hbm, cot), (tables_hbm, tables), (flags_hbm, flags))
        )
    ]
    for copy in copies:
        copy.start()
    even_x = lax.axis_index("gx") % 2 == 0
    even_y = lax.axis_index("gy") % 2 == 0
    copies[0].wait()
    copies[1].wait()
    for c in range(10):
        source, q = (flow, c) if c < 5 else (cot, c - 5)
        top, low = source[q, pl.ds(112, 16), :], source[q, pl.ds(0, 16), :]
        to_partner[pl.ds(16 * c, 16), :] = jnp.where(even_x, top, low)
        to_other[pl.ds(16 * c, 16), :] = jnp.where(even_x, low, top)
        top, low = source[q, pl.ds(15, 8, stride=16), :], source[q, pl.ds(0, 8, stride=16), :]
        to_ahead[pl.ds(8 * c, 8), :] = jnp.where(even_y, top, low)
        to_behind[pl.ds(8 * c, 8), :] = jnp.where(even_y, low, top)

    for x in range(8):
        for h in range(2):
            src = pl.ds(x * 16 + h * 8, 8)
            dst = pl.ds(h * 64 + x * 8, 8)
            density = flow[0, src, :]
            inv = rcp(density)
            mom = [flow[1 + i, src, :] for i in range(3)]
            vel = [m * inv for m in mom]
            kinetic = mom[0] * vel[0] + mom[1] * vel[1] + mom[2] * vel[2]
            pres = 0.4 * (flow[4, src, :] - 0.5 * kinetic)
            prod[dst, :] = density * pres
            parts = vel + [pres] + list(log_parts(density, pres))
            for q in range(8):
                nat[q, dst, :] = parts[q]
            for q in range(5):
                value = cot[q, src, :]
                nat[8 + q, dst, :] = 2.0 * value if q == 0 else value
    for q in range(NQ):
        turned[q] = jnp.transpose(nat[q])
    for d in range(3):
        perm = PERMS[d]
        order = [perm[0], perm[1], perm[2], 3, 4, 5, 6, 7, 8] + [9 + i for i in perm] + [12]
        source = nat if d < 2 else turned
        for q in range(NQ):
            for h in range(2):
                for k in range(8):
                    rows = pl.ds(h * 64 + 8 * k, 8) if d == 0 else pl.ds(h * 64 + k, 8, stride=8)
                    value = source[order[q], rows, :]
                    lines[d, q, pl.ds(h * 64 + 8 * k, 8), :] = value * INV_W[k] if q >= 8 else value

    copies[2].wait()
    copies[3].wait()
    sub, lane, high = lane_tables()
    coeffs = jnp.dot(tables[0], prod[...], precision=HIGHEST, preferred_element_type=F32)
    coeffs = jnp.dot(coeffs, tables[1], precision=HIGHEST, preferred_element_type=F32)
    modes[...] = coeffs
    squares = coeffs * coeffs
    group = jnp.where(
        lax.broadcasted_iota(jnp.int32, (128, 128), 0) >> 3
        == lax.broadcasted_iota(jnp.int32, (128, 128), 1) >> 3,
        1.0,
        0.0,
    )
    spread = (
        lax.broadcasted_iota(jnp.int32, (16, 128), 0)
        == lax.broadcasted_iota(jnp.int32, (16, 128), 1) >> 3
    )
    packed = jnp.zeros((8, 128), F32)
    for h in range(2):
        every = squares[h * 64 : h * 64 + 8]
        for x in range(1, 6):
            every = every + squares[h * 64 + 8 * x : h * 64 + 8 * x + 8]
        ends = squares[h * 64 + 48 : h * 64 + 56] + squares[h * 64 + 56 : h * 64 + 64]
        top = jnp.sum(jnp.where(high, every, 0.0) + ends, axis=0, keepdims=True)
        packed = jnp.where(sub == h, top, packed)
        packed = jnp.where(sub == 2 + h, jnp.sum(every + ends, axis=0, keepdims=True), packed)
    sums = jnp.dot(packed, group, precision=HIGHEST, preferred_element_type=F32)
    flag_rows = jnp.dot(
        flags[...].astype(F32),
        jnp.where(spread, 1.0, 0.0),
        precision=HIGHEST,
        preferred_element_type=F32,
    )
    sub16 = lax.broadcasted_iota(jnp.int32, (16, 128), 0)
    factors = jnp.zeros((16, 128), F32)
    for h in range(2):
        top = sums[h : h + 1] + EPS
        every = 0.01 * (sums[2 + h : 3 + h] + EPS)
        flag = flag_rows[h : h + 1]
        over = rcp(top + every)
        keep = flag < 0.5
        alpha = jnp.where(keep, 0.5 * top * over, jnp.where(flag > 1.5, 0.5, 0.0))
        d_top = jnp.where(keep, every * over * over, 0.0)
        d_all = jnp.where(keep, -0.01 * top * over * over, 0.0)
        for i, row in ((0, alpha), (6, d_top), (8, d_all)):
            factors = jnp.where(sub16 == i + h, row, factors)
    msg[...] = factors

    def one(step, carry):
        d = step // 2
        base = (step % 2) * 64

        def load(k):
            rows = pl.ds(pl.multiple_of(base + 8 * k, 8), 8)
            return [lines[d, q, rows, :] for q in range(NQ)]

        gained = jnp.zeros((8, 128), F32)
        for k in range(7):
            a = load(k)
            for j in range(k + 1, 8):
                skew = float(SKEW[k, j])
                b = load(j)
                vn, v1, v2 = (a[i] + b[i] for i in range(3))
                delta = [a[8 + i] - b[8 + i] for i in range(5)]
                y = a[5] - b[5]
                mean = ((0.25 * skew) * (a[4] * b[4])) * horner(MEAN_R, y * y)
                yb = a[7] - b[7]
                quot = rcp(horner(MEAN_B, yb * yb))
                inv5 = (a[6] * b[6]) * quot
                dot = a[0] * b[0] + a[1] * b[1] + a[2] * b[2] + inv5
                phi = delta[0] + delta[1] * vn + delta[2] * v1 + delta[3] * v2 + delta[4] * dot
                for q, value in enumerate((mean, quot, inv5, dot, phi)):
                    mid[step, 5 * PAIR[k, j] + q] = value
                work = delta[1] * (a[3] + b[3]) + delta[4] * (a[3] * b[0] + b[3] * a[0])
                gained = gained + (mean * vn) * phi + (0.5 * skew) * work
        low = None
        for k in range(8):
            a = load(k)
            node = Node(a[0:3], a[3], a[4], a[6], [0.5 * a[8]] + a[9:13])
            if k:
                half_speed = 0.5 * (low.speed + node.speed)
                for q in range(5):
                    rate = low.flux[q] + node.flux[q] - half_speed * (node.state[q] - low.state[q])
                    gained = gained + (0.5 * rate) * (node.cot[q] - low.cot[q])
            low = node
        gsum[step] = gained
        return carry

    lax.fori_loop(0, 6, one, 0)

    half_lane = lax.broadcasted_iota(jnp.int32, (16, 128), 1) >> 6
    along = jnp.concatenate([gsum[4], gsum[5]], axis=0)
    factors = msg[...]
    for h in range(2):
        row = jnp.sum(gsum[h] + gsum[2 + h], axis=0, keepdims=True)
        both = jnp.where(half_lane == h, along, 0.0) + jnp.where(spread, row, 0.0)
        column = jnp.sum(both, axis=1, keepdims=True)
        gain = jnp.sum(jnp.where(spread, column, 0.0), axis=0, keepdims=True)
        factors = jnp.where(sub16 == 4 + h, gain, factors)
        factors = jnp.where(sub16 == 2 + h, gain * (1.0 - factors[h : h + 1]), factors)
    msg[...] = factors
    for target, row in ((to_partner, 160), (to_other, 160), (to_ahead, 80), (to_behind, 80)):
        target[pl.ds(row, 8), :] = factors[0:8]


def conserved_node(state, cot, direction):
    perm = PERMS[direction]
    density = state[0]
    inv = rcp(density)
    vel = [state[1 + i] * inv for i in perm]
    square = vel[0] * vel[0] + vel[1] * vel[1] + vel[2] * vel[2]
    pres = 0.4 * (state[4] - 0.5 * density * square)
    scaled = [cot[0]] + [cot[1 + i] for i in perm] + [cot[4]]
    return Node(vel, pres, jnp.sqrt(density), jnp.sqrt(5.0 * pres * inv), [c * INV_W[0] for c in scaled])


def face_shares(low, up):
    flux, weight, direct, dot = face(low, up)
    half = [0.5 * w for w in weight]
    return (
        [-INV_W[7] * f for f in flux],
        low.pull(half, direct, dot),
        [INV_W[0] * f for f in flux],
        up.pull(half, [-x for x in direct], dot),
    )


def place(d, q):
    return q if q in (0, 4) else 1 + PERMS[d][q - 1]


def own_node(flow, cot, direction, rows):
    return conserved_node(
        [flow[q, rows, :] for q in range(5)], [cot[q, rows, :] for q in range(5)], direction
    )


def near_node(first, other, choose, count, start, direction):
    def value(c):
        rows = pl.ds(c * count + start, 8)
        return jnp.where(choose, first[rows, :], other[rows, :])

    return conserved_node([value(q) for q in range(5)], [value(5 + q) for q in range(5)], direction)


def kernel_second(
    ids_hbm,
    flow,
    cot,
    lines,
    mid,
    modes,
    msg,
    tables,
    base,
    extra,
    slope,
    zsum,
    out,
    zacc,
    zends,
    znext,
    zback,
    ids,
    sem,
):
    copy = pltpu.make_async_copy(ids_hbm, ids, sem)
    copy.start()

    sub, lane, high = lane_tables()
    tiles = []
    for h in range(2):
        d_top = msg[pl.ds(6 + h, 1), :]
        d_all = msg[pl.ds(8 + h, 1), :]
        both = d_top + d_all
        mixed = jnp.where(high, both, d_all)
        for x in range(8):
            tiles.append(modes[pl.ds(h * 64 + 8 * x, 8), :] * (both if x >= 6 else mixed))
    weighed = jnp.concatenate(tiles, axis=0)
    weighed = jnp.dot(tables[2], weighed, precision=HIGHEST, preferred_element_type=F32)
    weighed = jnp.dot(weighed, tables[3], precision=HIGHEST, preferred_element_type=F32)
    for h in range(2):
        for x in range(8):
            rows = pl.ds(x * 16 + h * 8, 8)
            density = flow[0, rows, :]
            inv = rcp(density)
            vel = [flow[1 + i, rows, :] * inv for i in range(3)]
            square = vel[0] * vel[0] + vel[1] * vel[1] + vel[2] * vel[2]
            pres = 0.4 * (flow[4, rows, :] - 0.5 * density * square)
            value = weighed[h * 64 + 8 * x : h * 64 + 8 * x + 8]
            pull_e = 0.4 * (value * density)
            slope[0, rows, :] = value * pres + (0.5 * pull_e) * square
            for i in range(3):
                slope[1 + i, rows, :] = -(pull_e * vel[i])
            slope[4, rows, :] = pull_e

    def one(step, carry):
        d = step // 2
        base = (step % 2) * 64

        def rows(k):
            return pl.ds(pl.multiple_of(base + 8 * k, 8), 8)

        for k in range(7):
            a = [lines[d, q, rows(k), :] for q in range(NQ)]
            acc = [None] * 13 if k == 0 else [out[d, q, rows(k), :] for q in range(13)]
            for j in range(k + 1, 8):
                skew = float(SKEW[k, j])
                half = 0.5 * skew
                b = [lines[d, q, rows(j), :] for q in range(NQ)]
                mean, quot, inv5, dot, phi = (mid[step, 5 * PAIR[k, j] + q] for q in range(5))
                vn, v1, v2, pres = (a[i] + b[i] for i in range(4))
                delta = [None] + [a[8 + i] - b[8 + i] for i in range(1, 5)]
                y = a[5] - b[5]
                slope = (((0.25 * skew) * (a[4] * b[4])) * y) * horner(SLOPE_R, y * y)
                yb = a[7] - b[7]
                tilt = yb * (horner(SLOPE_B, yb * yb) * quot)
                mass = mean * vn
                flux = [
                    mass,
                    mass * vn + half * pres,
                    mass * v1,
                    mass * v2,
                    mass * dot + half * (a[3] * b[0] + b[3] * a[0]),
                ]
                t = half * delta[4]
                w = mass * delta[4]
                pp = phi * mass
                qq = (phi * vn) * slope
                xx = w * inv5
                zz = xx * tilt
                shared = [
                    phi * mean + mass * (delta[1] + delta[4] * vn) + t * pres,
                    mass * (delta[2] + delta[4] * v1),
                    mass * (delta[3] + delta[4] * v2),
                    half * (delta[1] + delta[4] * vn),
                ]
                ups = flux + [pp + qq] + shared + [xx + zz, w, t]
                downs = [None] * 5 + [pp - qq] + shared + [xx - zz, w, t]
                for q in range(13):
                    acc[q] = ups[q] if acc[q] is None else acc[q] + ups[q]
                    if q < 5:
                        value = -flux[q] if k == 0 else out[d, q, rows(j), :] - flux[q]
                    else:
                        value = downs[q] if k == 0 else out[d, q, rows(j), :] + downs[q]
                    out[d, q, rows(j), :] = value
            for q in range(13):
                out[d, q, rows(k), :] = acc[q]

        low = None
        zero = jnp.zeros((8, 128), F32)
        low_flux, low_weight, low_direct, low_dot = [zero] * 5, [zero] * 5, [zero] * 5, zero
        for k in range(9):
            if k < 8:
                a = [lines[d, q, rows(k), :] for q in range(NQ)]
                node = Node(a[0:3], a[3], a[4], a[6], [0.5 * a[8]] + a[9:13])
            if k == 0:
                low = node
                continue
            if k < 8:
                flux, weight, direct, dot = face(low, node)
            else:
                flux, weight, direct, dot = [zero] * 5, [zero] * 5, [zero] * 5, zero
            m = k - 1
            total = [out[d, q, rows(m), :] for q in range(13)]
            for i in range(3):
                total[6 + i] = total[6 + i] - total[11] * low.vel[i]
            total[6] = total[6] - total[12] * low.pres
            total[9] = total[9] - total[12] * low.vel[0]
            total[0] = 2.0 * total[0]
            for q in range(5):
                diff = total[q] - (flux[q] - low_flux[q])
                out[d, q, rows(m), :] = total[q] * (-INV_W[m])
                out[d, 5 + q, rows(m), :] = diff * INV_W[m]
            fv = low.pull(
                [0.5 * (x + z) for x, z in zip(low_weight, weight)],
                [x - z for x, z in zip(direct, low_direct)],
                low_dot + dot,
            )
            inv = rcp(low.state[0])
            beta = 0.5 * total[10]
            g_rho = (beta - 0.5 * total[5]) * inv
            g_e = -0.4 * (total[9] + beta * rcp(low.pres))
            g_m = [-(total[6 + i] * inv) - g_e * low.vel[i] for i in range(3)]
            inner = g_m[0] * low.vel[0] + g_m[1] * low.vel[1] + g_m[2] * low.vel[2]
            dg = [g_rho - inner - (0.5 * g_e) * low.square] + g_m + [g_e]
            for q in range(5):
                out[d, 10 + q, rows(m), :] = dg[q]
                out[d, 15 + q, rows(m), :] = fv[q] - dg[q]
            low, low_flux, low_weight, low_direct, low_dot = node, flux, weight, direct, dot
        return carry

    lax.fori_loop(0, 6, one, 0)

    copy.wait()
    row = lax.broadcasted_iota(jnp.int32, (128, 128), 0)
    lanes = lax.broadcasted_iota(jnp.int32, (8, 128), 1)
    above = jnp.zeros((8, 128), jnp.int32)
    for k in range(16):
        above = jnp.where((lanes >> 3) == k, ids[k], above)
    above = above * 8 + (lanes & 7)
    above = jnp.concatenate([above] * 16, axis=0)
    up = jnp.where(above == row, 1.0, 0.0)
    own = msg[0:8, :]
    zsum[...] = jnp.dot(own, up, precision=HIGHEST, preferred_element_type=F32) + lax.dot_general(
        own, up, (((1,), (1,)), ((), ())), precision=HIGHEST, preferred_element_type=F32
    )

    for q in range(NQ):
        for end in range(2):
            for h in range(2):
                zends[q, pl.ds(end * 16 + h * 8, 8), :] = lines[2, q, pl.ds(h * 64 + 56 * end, 8), :]
    for k in range(16):
        znext[:, pl.ds(k, 1), :] = zends[:, pl.ds(ids[k], 1), :]
    for h in range(2):
        def side(ref, start):
            v = [ref[q, pl.ds(start + h * 8, 8), :] for q in range(NQ)]
            return Node(v[0:3], v[3], v[4], v[6], [0.5 * v[8]] + v[9:13])

        low_r, low_g, up_r, up_g = face_shares(side(zends, 16), side(znext, 0))
        for q in range(5):
            zacc[q, pl.ds(h * 8, 8), :] = low_r[q]
            zacc[5 + q, pl.ds(h * 8, 8), :] = low_g[q]
            zback[q, pl.ds(h * 8, 8), :] = up_r[q]
            zback[5 + q, pl.ds(h * 8, 8), :] = up_g[q]
    for k in range(16):
        zacc[:, pl.ds(16 + ids[k], 1), :] = zback[:, pl.ds(k, 1), :]

    back = [[place(d, q) for q in range(5)] for d in range(3)]
    for group_at, target, offset in ((0, base, 0), (1, extra, 0), (2, base, 5), (3, extra, 5)):
        for q in range(5):
            first = group_at * 5
            qx = first + back[0].index(q)
            qy = first + back[1].index(q)
            qz = back[2].index(q)
            pieces = []
            for slot in range(16):
                h, s = slot // 8, slot % 8
                pieces.append(out[2, first + qz, pl.ds(h * 64 + s, 8, stride=8), :])
            if group_at in (0, 2):
                source = qz + (0 if group_at == 0 else 5)
                for slot in range(16):
                    upper = zacc[source, pl.ds(slot, 1), :]
                    lower = zacc[source, pl.ds(16 + slot, 1), :]
                    add = jnp.where(sub == 7, upper, jnp.where(sub == 0, lower, 0.0))
                    pieces[slot] = pieces[slot] + add
            whole = jnp.transpose(jnp.concatenate(pieces, axis=0))
            for h in range(2):
                for x in range(8):
                    value = (
                        out[0, qx, pl.ds(h * 64 + 8 * x, 8), :]
                        + out[1, qy, pl.ds(h * 64 + x, 8, stride=8), :]
                        + whole[h * 64 + 8 * x : h * 64 + 8 * x + 8]
                    )
                    target[offset + q, pl.ds(x * 16 + h * 8, 8), :] = value

    rows = [pl.ds(7, 8, stride=16), pl.ds(8, 8, stride=16)]
    shares = face_shares(own_node(flow, cot, 1, rows[0]), own_node(flow, cot, 1, rows[1]))
    for side in range(2):
        for q in range(5):
            p = place(1, q)
            base[p, rows[side], :] += shares[2 * side][q]
            base[5 + p, rows[side], :] += shares[2 * side + 1][q]


def kernel_blend(
    msg,
    zsum,
    partner,
    other,
    ahead,
    behind,
    flow,
    cot,
    base,
    extra,
    slope,
    residual_hbm,
    grad_hbm,
    total,
    sems,
):
    even_x = lax.axis_index("gx") % 2 == 0
    even_y = lax.axis_index("gy") % 2 == 0
    sides = partner[160:168, :] + other[160:168, :]
    met, left = ahead[80:88, :], behind[80:88, :]
    above, below = jnp.where(even_y, met, left), jnp.where(even_y, left, met)
    for h in range(2):

        def beside_of(i):
            r = 2 * i + h
            low = below[2 * i + 1 : 2 * i + 2] if h == 0 else msg[2 * i : 2 * i + 1, :]
            high = msg[2 * i + 1 : 2 * i + 2, :] if h == 0 else above[2 * i : 2 * i + 1]
            return zsum[r : r + 1, :] + sides[r : r + 1] + low + high

        alpha = msg[h : h + 1, :]
        gain = msg[4 + h : 5 + h, :]
        around = beside_of(0)
        smooth = alpha + (1.0 - alpha) * around * (0.5 / 6.0)
        pull = gain * (1.0 - around * (0.5 / 6.0)) + beside_of(1) * (0.5 / 6.0)
        smooth = jnp.broadcast_to(smooth, (8, 128))
        pull = jnp.broadcast_to(pull, (8, 128))
        for x in range(8):
            rows = pl.ds(x * 16 + h * 8, 8)
            for q in range(5):
                total[q, rows, :] = base[q, rows, :] + smooth * extra[q, rows, :]
                total[5 + q, rows, :] = (
                    base[5 + q, rows, :] + smooth * extra[5 + q, rows, :] + pull * slope[q, rows, :]
                )

    def add(direction, rows, res, grad):
        for q in range(5):
            p = place(direction, q)
            total[p, rows, :] += res[q]
            total[5 + p, rows, :] += grad[q]

    here, top = pl.ds(0, 8, stride=16), pl.ds(15, 8, stride=16)
    shares = face_shares(near_node(behind, ahead, even_y, 8, 0, 1), own_node(flow, cot, 1, here))
    add(1, here, shares[2], shares[3])
    shares = face_shares(own_node(flow, cot, 1, top), near_node(ahead, behind, even_y, 8, 0, 1))
    add(1, top, shares[0], shares[1])

    def send(i, start, count):
        rows = pl.ds(start, count)
        return [
            pltpu.make_async_copy(
                total.at[pl.ds(0, 5), rows], residual_hbm.at[pl.ds(0, 5), rows], sems.at[2 * i]
            ),
            pltpu.make_async_copy(
                total.at[pl.ds(5, 5), rows], grad_hbm.at[pl.ds(0, 5), rows], sems.at[2 * i + 1]
            ),
        ]

    copies = send(0, 16, 96)
    for copy in copies:
        copy.start()
    for h in range(2):
        here, top = pl.ds(h * 8, 8), pl.ds(112 + h * 8, 8)
        shares = face_shares(
            near_node(other, partner, even_x, 16, h * 8, 0), own_node(flow, cot, 0, here)
        )
        add(0, here, shares[2], shares[3])
        shares = face_shares(
            own_node(flow, cot, 0, top), near_node(partner, other, even_x, 16, h * 8, 0)
        )
        add(0, top, shares[0], shares[1])
    last = send(1, 0, 16) + send(2, 112, 16)
    for copy in last:
        copy.start()
    for copy in copies + last:
        copy.wait()


def swapped(value, axis, first):
    count = lax.axis_size(axis)
    pairs = []
    for i in range(first, count + first, 2):
        a, b = i % count, (i + 1) % count
        pairs += [(a, b), (b, a)]
    return lax.ppermute(value, axis, pairs)


def shape(*dims):
    return jax.ShapeDtypeStruct(dims, F32)


def in_hbm(value):
    return pltpu.with_memory_space_constraint(value, pltpu.HBM)


def shards(flow_state, cotangent, clip_flags, successor_ids):
    flow = flow_state.reshape(5, ROWS, 128)
    cot = cotangent.reshape(5, ROWS, 128)
    vmem = pl.BlockSpec(memory_space=pltpu.VMEM)
    hbm = pl.BlockSpec(memory_space=pltpu.HBM)
    modal = np.asarray(TO_MODAL, np.float32)
    kxy = np.kron(np.eye(2), np.kron(modal, modal)).astype(np.float32)
    kz = np.kron(np.eye(16), modal).astype(np.float32)
    constants = np.stack([kxy, kz.T, kxy.T, kz])

    lines, mid, modes, msg, to_partner, to_other, to_ahead, to_behind, flow_v, cot_v, tables = pl.pallas_call(
        kernel_first,
        out_shape=(
            shape(3, NQ, ROWS, 128),
            shape(6, 5 * 28, 8, 128),
            shape(ROWS, 128),
            shape(16, 128),
            shape(168, 128),
            shape(168, 128),
            shape(88, 128),
            shape(88, 128),
            shape(5, ROWS, 128),
            shape(5, ROWS, 128),
            shape(4, 128, 128),
        ),
        in_specs=[hbm] * 4,
        out_specs=[vmem] * 11,
        scratch_shapes=[
            pltpu.VMEM((NQ, ROWS, 128), F32),
            pltpu.VMEM((NQ, ROWS, 128), F32),
            pltpu.VMEM((ROWS, 128), F32),
            pltpu.VMEM((6, 8, 128), F32),
            pltpu.VMEM((2, 16), jnp.int32),
            pltpu.SemaphoreType.DMA((4,)),
        ],
        compiler_params=pltpu.CompilerParams(vmem_limit_bytes=16 * 1024 * 1024),
        name="first",
    )(in_hbm(flow), in_hbm(cot), in_hbm(clip_flags.reshape(2, 16)), in_hbm(jnp.asarray(constants)))

    ahead = swapped(to_ahead, "gy", 0)
    behind = swapped(to_behind, "gy", 1)
    other = swapped(to_other, "gx", 1)
    partner = swapped(to_partner, "gx", 0)

    base, extra, slope, zsum = pl.pallas_call(
        kernel_second,
        out_shape=(shape(10, ROWS, 128), shape(10, ROWS, 128), shape(5, ROWS, 128), shape(8, 128)),
        in_specs=[hbm] + [vmem] * 7,
        out_specs=[vmem] * 4,
        scratch_shapes=[
            pltpu.VMEM((3, 20, ROWS, 128), F32),
            pltpu.VMEM((10, 32, 128), F32),
            pltpu.VMEM((NQ, 32, 128), F32),
            pltpu.VMEM((NQ, 16, 128), F32),
            pltpu.VMEM((10, 16, 128), F32),
            pltpu.SMEM((16,), jnp.int32),
            pltpu.SemaphoreType.DMA(()),
        ],
        compiler_params=pltpu.CompilerParams(vmem_limit_bytes=16 * 1024 * 1024),
        name="second",
    )(in_hbm(successor_ids), flow_v, cot_v, lines, mid, modes, msg, tables)

    residual, grad = pl.pallas_call(
        kernel_blend,
        out_shape=(shape(5, ROWS, 128), shape(5, ROWS, 128)),
        in_specs=[vmem] * 11,
        out_specs=[hbm] * 2,
        scratch_shapes=[pltpu.VMEM((10, ROWS, 128), F32), pltpu.SemaphoreType.DMA((6,))],
        compiler_params=pltpu.CompilerParams(vmem_limit_bytes=16 * 1024 * 1024),
        name="blend",
    )(msg, zsum, partner, other, ahead, behind, flow_v, cot_v, base, extra, slope)
    return residual.reshape(flow_state.shape), grad.reshape(flow_state.shape)


def solution(mesh):
    placed = P(None, "gx", "gy", None)
    return jax.shard_map(
        shards,
        mesh=mesh,
        in_specs=(placed, placed, P("gx", "gy", None), P()),
        out_specs=(placed, placed),
        check_vma=False,
    )
```

```python
import jax
import jax.numpy as jnp
import numpy as np
from jax import lax
from jax.experimental import pallas as pl
from jax.experimental.pallas import tpu as pltpu
from jax.sharding import PartitionSpec as P
from numpy.polynomial import chebyshev, polynomial

F32 = jnp.float32
HIGHEST = lax.Precision.HIGHEST
EPS = 1e-05
PERMS = ((0, 1, 2), (1, 0, 2), (2, 0, 1))
NQ = 13
ROWS = 128


def legendre_values(points, node_count):
    values_table = np.zeros((points.shape[0], node_count))
    values_table[:, 0] = 1.0
    values_table[:, 1] = points
    for degree_index in range(2, node_count):
        values_table[:, degree_index] = (
            (2 * degree_index - 1) * points * values_table[:, degree_index - 1]
            - (degree_index - 1) * values_table[:, degree_index - 2]
        ) / degree_index
    return values_table


def node_tables():
    degree = 7
    node_count = degree + 1
    points = -np.cos(np.pi * np.arange(node_count) / degree)
    for newton_step in range(60):
        legend = legendre_values(points, node_count)
        points = points - (points * legend[:, degree] - legend[:, degree - 1]) / (
            node_count * legend[:, degree]
        )
    legend = legendre_values(points, node_count)
    weights = 2.0 / (degree * node_count * legend[:, degree] * legend[:, degree])
    differ = np.zeros((node_count, node_count))
    for row_index in range(node_count):
        for col_index in range(node_count):
            if row_index != col_index:
                differ[row_index, col_index] = legend[row_index, degree] / (
                    legend[col_index, degree] * (points[row_index] - points[col_index])
                )
    norm_table = 2.0 / (2.0 * np.arange(node_count) + 1.0)
    norm_table[degree] = 2.0 / degree
    to_modal = legend.T * weights[None, :] / norm_table[:, None]
    return (weights, differ, to_modal)


WEIGHTS, DIFFER, TO_MODAL = node_tables()
INV_W = [float(1.0 / w) for w in WEIGHTS]
SKEW = 2.0 * DIFFER * WEIGHTS[:, None]


def fitted(function, top, degree):
    series = chebyshev.Chebyshev.interpolate(function, degree, domain=[0.0, top])
    return [float(np.float32(c)) for c in series.convert(kind=polynomial.Polynomial).coef]


def sinhc(square):
    root = np.sqrt(np.maximum(square, 1e-12))
    return np.sinh(root) / root


def sinhc_slope(square):
    root = np.sqrt(np.maximum(square, 1e-12))
    exact = (np.cosh(root) - np.sinh(root) / root) / (root * root)
    series = 1.0 / 3.0 + square / 30.0 + square**2 / 840.0 + square**3 / 45360.0
    return np.where(square < 1e-2, series, exact)


RATES = 5 * 28
PAIR = {pair: i for i, pair in enumerate((k, j) for k in range(7) for j in range(k + 1, 8))}

MEAN_R = fitted(sinhc, 3.0, 4)
SLOPE_R = fitted(sinhc_slope, 3.0, 3)
MEAN_B = fitted(sinhc, 12.0, 5)
SLOPE_B = fitted(sinhc_slope, 12.0, 5)


def horner(coeffs, value):
    total = coeffs[-1] * value + coeffs[-2]
    for c in coeffs[-3::-1]:
        total = total * value + c
    return total


def rcp(value):
    return 1.0 / value


def log_parts(density, pressure):
    inv = rcp(density)
    ratio = pressure * inv
    half_log = 0.5 * jnp.log(density)
    return (
        jnp.sqrt(density),
        half_log,
        jnp.sqrt(5.0 * ratio),
        half_log - 0.5 * jnp.log(pressure),
    )


class Node:
    def __init__(self, vel, pres, root, theta, cot):
        self.vel, self.pres, self.cot = vel, pres, cot
        density = root * root
        vn, v1, v2 = vel
        mom = [density * v for v in vel]
        self.square = vn * vn + v1 * v1 + v2 * v2
        energy = 2.5 * pres + (0.5 * density) * self.square
        self.state = [density] + mom + [energy]
        mn = mom[0]
        self.flux = [mn, mn * vn + pres, mn * v1, mn * v2, (energy + pres) * vn]
        self.sound = theta * float(np.sqrt(1.4 / 5.0))
        self.speed = jnp.abs(vn) + self.sound

    def pull(self, half, direct, speed_cot):
        density = self.state[0]
        vn, v1, v2 = self.vel
        grad = [direct[i] + half[i] * vn for i in range(5)]
        sign = jnp.where(vn >= 0.0, 1.0, -1.0)
        dvn = half[0] * self.state[0]
        for i in range(1, 5):
            dvn = dvn + half[i] * self.state[i]
        dvn = dvn + half[4] * self.pres + speed_cot * sign
        inv = rcp(density)
        part = (0.5 * speed_cot) * self.sound
        dpres = half[1] + half[4] * vn + part * rcp(self.pres)
        over = dvn * inv
        pull_e = 0.4 * dpres
        grad[0] = grad[0] - part * inv - over * vn + (0.5 * pull_e) * self.square
        grad[1] = grad[1] + over - pull_e * vn
        grad[2] = grad[2] - pull_e * v1
        grad[3] = grad[3] - pull_e * v2
        grad[4] = grad[4] + pull_e
        return grad


def face_adjoint(low, up):
    jump = [b - a for a, b in zip(low.state, up.state)]
    weight = [b - a for a, b in zip(low.cot, up.cot)]
    speed = 0.5 * (low.speed + up.speed)
    dot = weight[0] * jump[0]
    for i in range(1, 5):
        dot = dot + weight[i] * jump[i]
    return weight, [speed * w for w in weight], -0.5 * dot


def face_rate(low, up):
    speed = 0.5 * (low.speed + up.speed)
    return [
        a + b - speed * (y - x) for a, b, x, y in zip(low.flux, up.flux, low.state, up.state)
    ]


def lane_tables():
    sub = lax.broadcasted_iota(jnp.int32, (8, 128), 0)
    lane = lax.broadcasted_iota(jnp.int32, (8, 128), 1)
    return sub, lane, (sub >= 6) | ((lane & 7) >= 6)


def kernel_first(
    flow_hbm,
    cot_hbm,
    flags_hbm,
    tables_hbm,
    lines,
    mid,
    modes,
    msg,
    to_partner,
    to_other,
    to_ahead,
    to_behind,
    flow,
    cot,
    tables,
    out,
    nat,
    turned,
    prod,
    gsum,
    flags,
    sems,
):
    copies = [
        pltpu.make_async_copy(source, target, sems.at[i])
        for i, (source, target) in enumerate(
            ((flow_hbm, flow), (cot_hbm, cot), (tables_hbm, tables), (flags_hbm, flags))
        )
    ]
    for copy in copies:
        copy.start()
    even_x = lax.axis_index("gx") % 2 == 0
    even_y = lax.axis_index("gy") % 2 == 0
    for copy in copies:
        copy.wait()
    for c in range(10):
        source, q = (flow, c) if c < 5 else (cot, c - 5)
        top, low = source[q, pl.ds(112, 16), :], source[q, pl.ds(0, 16), :]
        to_partner[pl.ds(16 * c, 16), :] = jnp.where(even_x, top, low)
        to_other[pl.ds(16 * c, 16), :] = jnp.where(even_x, low, top)
        top, low = source[q, pl.ds(15, 8, stride=16), :], source[q, pl.ds(0, 8, stride=16), :]
        to_ahead[pl.ds(8 * c, 8), :] = jnp.where(even_y, top, low)
        to_behind[pl.ds(8 * c, 8), :] = jnp.where(even_y, low, top)

    for x in range(8):
        for h in range(2):
            src = pl.ds(x * 16 + h * 8, 8)
            dst = pl.ds(h * 64 + x * 8, 8)
            density = flow[0, src, :]
            inv = rcp(density)
            mom = [flow[1 + i, src, :] for i in range(3)]
            vel = [m * inv for m in mom]
            kinetic = mom[0] * vel[0] + mom[1] * vel[1] + mom[2] * vel[2]
            pres = 0.4 * (flow[4, src, :] - 0.5 * kinetic)
            prod[dst, :] = density * pres
            parts = vel + [pres] + list(log_parts(density, pres))
            for q in range(8):
                nat[q, dst, :] = parts[q]
            for q in range(5):
                value = cot[q, src, :]
                nat[8 + q, dst, :] = 2.0 * value if q == 0 else value
    for q in range(NQ):
        turned[q] = jnp.transpose(nat[q])
    for d in range(3):
        perm = PERMS[d]
        order = [perm[0], perm[1], perm[2], 3, 4, 5, 6, 7, 8] + [9 + i for i in perm] + [12]
        source = nat if d < 2 else turned
        for q in range(NQ):
            for h in range(2):
                for k in range(8):
                    rows = pl.ds(h * 64 + 8 * k, 8) if d == 0 else pl.ds(h * 64 + k, 8, stride=8)
                    value = source[order[q], rows, :]
                    lines[d, q, pl.ds(h * 64 + 8 * k, 8), :] = value * (0.5 * INV_W[k]) if q >= 8 else value

    sub, lane, high = lane_tables()
    coeffs = jnp.dot(tables[0], prod[...], precision=HIGHEST, preferred_element_type=F32)
    coeffs = jnp.dot(coeffs, tables[1], precision=HIGHEST, preferred_element_type=F32)
    modes[...] = coeffs
    squares = coeffs * coeffs
    group = jnp.where(
        lax.broadcasted_iota(jnp.int32, (128, 128), 0) >> 3
        == lax.broadcasted_iota(jnp.int32, (128, 128), 1) >> 3,
        1.0,
        0.0,
    )
    spread = (
        lax.broadcasted_iota(jnp.int32, (16, 128), 0)
        == lax.broadcasted_iota(jnp.int32, (16, 128), 1) >> 3
    )
    packed = jnp.zeros((8, 128), F32)
    for h in range(2):
        every = squares[h * 64 : h * 64 + 8]
        for x in range(1, 6):
            every = every + squares[h * 64 + 8 * x : h * 64 + 8 * x + 8]
        ends = squares[h * 64 + 48 : h * 64 + 56] + squares[h * 64 + 56 : h * 64 + 64]
        top = jnp.sum(jnp.where(high, every, 0.0) + ends, axis=0, keepdims=True)
        packed = jnp.where(sub == h, top, packed)
        packed = jnp.where(sub == 2 + h, jnp.sum(every + ends, axis=0, keepdims=True), packed)
    sums = jnp.dot(packed, group, precision=HIGHEST, preferred_element_type=F32)
    flag_rows = jnp.dot(
        flags[...].astype(F32),
        jnp.where(spread, 1.0, 0.0),
        precision=HIGHEST,
        preferred_element_type=F32,
    )
    sub16 = lax.broadcasted_iota(jnp.int32, (16, 128), 0)
    factors = jnp.zeros((16, 128), F32)
    for h in range(2):
        top = sums[h : h + 1] + EPS
        every = 0.01 * (sums[2 + h : 3 + h] + EPS)
        flag = flag_rows[h : h + 1]
        over = rcp(top + every)
        keep = flag < 0.5
        alpha = jnp.where(keep, 0.5 * top * over, jnp.where(flag > 1.5, 0.5, 0.0))
        d_top = jnp.where(keep, every * over * over, 0.0)
        d_all = jnp.where(keep, -0.01 * top * over * over, 0.0)
        for i, row in ((0, alpha), (6, d_top), (8, d_all)):
            factors = jnp.where(sub16 == i + h, row, factors)
    msg[...] = factors

    def one(step, carry):
        d = step // 2
        base = (step % 2) * 64

        def load(k):
            rows = pl.ds(pl.multiple_of(base + 8 * k, 8), 8)
            return [lines[d, q, rows, :] for q in range(NQ)]

        gained = jnp.zeros((8, 128), F32)
        for k in range(7):
            a = load(k)
            for j in range(k + 1, 8):
                skew = float(SKEW[k, j])
                b = load(j)
                vn, v1, v2 = (a[i] + b[i] for i in range(3))
                delta = [a[8 + i] - b[8 + i] for i in range(5)]
                y = a[5] - b[5]
                mean = ((0.5 * skew) * (a[4] * b[4])) * horner(MEAN_R, y * y)
                yb = a[7] - b[7]
                quot = rcp(horner(MEAN_B, yb * yb))
                inv5 = (a[6] * b[6]) * quot
                dot = a[0] * b[0] + a[1] * b[1] + a[2] * b[2] + inv5
                phi = delta[0] + delta[1] * vn + delta[2] * v1 + delta[3] * v2 + delta[4] * dot
                for q, value in enumerate((mean, quot, inv5, dot, phi)):
                    mid[step, 5 * PAIR[k, j] + q] = value
                work = delta[1] * (a[3] + b[3]) + delta[4] * (a[3] * b[0] + b[3] * a[0])
                gained = gained + (mean * vn) * phi + skew * work
        low = None
        for k in range(8):
            a = load(k)
            node = Node(a[0:3], a[3], a[4], a[6], [0.5 * a[8]] + a[9:13])
            if k:
                for q, rate in enumerate(face_rate(low, node)):
                    mid[step, RATES + 5 * (k - 1) + q] = rate
                    gained = gained + rate * (node.cot[q] - low.cot[q])
            low = node
        gsum[step] = gained
        return carry

    lax.fori_loop(0, 6, one, 0)

    half_lane = lax.broadcasted_iota(jnp.int32, (16, 128), 1) >> 6
    along = jnp.concatenate([gsum[4], gsum[5]], axis=0)
    factors = msg[...]
    for h in range(2):
        row = jnp.sum(gsum[h] + gsum[2 + h], axis=0, keepdims=True)
        both = jnp.where(half_lane == h, along, 0.0) + jnp.where(spread, row, 0.0)
        column = jnp.sum(both, axis=1, keepdims=True)
        gain = jnp.sum(jnp.where(spread, column, 0.0), axis=0, keepdims=True)
        factors = jnp.where(sub16 == 4 + h, gain, factors)
        factors = jnp.where(sub16 == 2 + h, gain * (1.0 - factors[h : h + 1]), factors)
    msg[...] = factors
    for target, row in ((to_partner, 160), (to_other, 160), (to_ahead, 80), (to_behind, 80)):
        target[pl.ds(row, 8), :] = factors[0:8]

    def two(step, carry):
        adjoint_step(lines, mid, out, step)
        return carry

    lax.fori_loop(0, steps_ahead(), two, 0)


def conserved_node(state, cot, direction):
    perm = PERMS[direction]
    density = state[0]
    inv = rcp(density)
    vel = [state[1 + i] * inv for i in perm]
    square = vel[0] * vel[0] + vel[1] * vel[1] + vel[2] * vel[2]
    pres = 0.4 * (state[4] - 0.5 * density * square)
    scaled = [cot[0]] + [cot[1 + i] for i in perm] + [cot[4]]
    return Node(vel, pres, jnp.sqrt(density), jnp.sqrt(5.0 * pres * inv), [c * (0.5 * INV_W[0]) for c in scaled])


def face_shares(low, up):
    rate = face_rate(low, up)
    weight, direct, dot = face_adjoint(low, up)
    return (
        [(-0.5 * INV_W[7]) * f for f in rate],
        low.pull(weight, direct, dot),
        [(0.5 * INV_W[0]) * f for f in rate],
        up.pull(weight, [-x for x in direct], dot),
    )


def steps_ahead():
    gx = lax.axis_index("gx")
    plane = 2 * lax.axis_index("gy") + gx // 32
    corner = jnp.where(plane < 4, jnp.minimum(6 - plane, 5), 0)
    return jnp.where(gx % 32 == 0, corner, jnp.where(plane < 2, 5 - plane, 0))


def adjoint_step(lines, mid, out, step):
    d = step // 2
    base = (step % 2) * 64

    def rows(k):
        return pl.ds(pl.multiple_of(base + 8 * k, 8), 8)

    for k in range(7):
        a = [lines[d, q, rows(k), :] for q in range(NQ)]
        acc = [None] * 13 if k == 0 else [out[d, q, rows(k), :] for q in range(13)]
        for j in range(k + 1, 8):
            skew = float(SKEW[k, j])
            b = [lines[d, q, rows(j), :] for q in range(NQ)]
            mean, quot, inv5, dot, phi = (mid[step, 5 * PAIR[k, j] + q] for q in range(5))
            vn, v1, v2, pres = (a[i] + b[i] for i in range(4))
            delta = [None] + [a[8 + i] - b[8 + i] for i in range(1, 5)]
            y = a[5] - b[5]
            slope = (((0.5 * skew) * (a[4] * b[4])) * y) * horner(SLOPE_R, y * y)
            yb = a[7] - b[7]
            tilt = yb * (horner(SLOPE_B, yb * yb) * quot)
            mass = mean * vn
            flux = [
                mass,
                mass * vn + skew * pres,
                mass * v1,
                mass * v2,
                mass * dot + skew * (a[3] * b[0] + b[3] * a[0]),
            ]
            t = skew * delta[4]
            w = mass * delta[4]
            pp = phi * mass
            qq = (phi * vn) * slope
            xx = w * inv5
            zz = xx * tilt
            shared = [
                phi * mean + mass * (delta[1] + delta[4] * vn) + t * pres,
                mass * (delta[2] + delta[4] * v1),
                mass * (delta[3] + delta[4] * v2),
                skew * (delta[1] + delta[4] * vn),
            ]
            ups = flux + [pp + qq] + shared + [xx + zz, w, t]
            downs = [None] * 5 + [pp - qq] + shared + [xx - zz, w, t]
            for q in range(13):
                acc[q] = ups[q] if acc[q] is None else acc[q] + ups[q]
                if q < 5:
                    value = -flux[q] if k == 0 else out[d, q, rows(j), :] - flux[q]
                else:
                    value = downs[q] if k == 0 else out[d, q, rows(j), :] + downs[q]
                out[d, q, rows(j), :] = value
        for q in range(13):
            out[d, q, rows(k), :] = acc[q]

    low = None
    zero = jnp.zeros((8, 128), F32)
    low_flux, low_weight, low_direct, low_dot = [zero] * 5, [zero] * 5, [zero] * 5, zero
    for k in range(9):
        if k < 8:
            a = [lines[d, q, rows(k), :] for q in range(NQ)]
            node = Node(a[0:3], a[3], a[4], a[6], [0.5 * a[8]] + a[9:13])
        if k == 0:
            low = node
            continue
        if k < 8:
            weight, direct, dot = face_adjoint(low, node)
            flux = [mid[step, RATES + 5 * (k - 1) + q] for q in range(5)]
        else:
            flux, weight, direct, dot = [zero] * 5, [zero] * 5, [zero] * 5, zero
        m = k - 1
        total = [out[d, q, rows(m), :] for q in range(13)]
        for i in range(3):
            total[6 + i] = total[6 + i] - total[11] * low.vel[i]
        total[6] = total[6] - total[12] * low.pres
        total[9] = total[9] - total[12] * low.vel[0]
        total[0] = 2.0 * total[0]
        for q in range(5):
            diff = total[q] - (flux[q] - low_flux[q])
            out[d, q, rows(m), :] = total[q] * (-0.5 * INV_W[m])
            out[d, 5 + q, rows(m), :] = diff * (0.5 * INV_W[m])
        fv = low.pull(
            [x + z for x, z in zip(low_weight, weight)],
            [x - z for x, z in zip(direct, low_direct)],
            low_dot + dot,
        )
        inv = rcp(low.state[0])
        beta = 0.5 * total[10]
        g_rho = (beta - 0.5 * total[5]) * inv
        g_e = -0.4 * (total[9] + beta * rcp(low.pres))
        g_m = [-(total[6 + i] * inv) - g_e * low.vel[i] for i in range(3)]
        inner = g_m[0] * low.vel[0] + g_m[1] * low.vel[1] + g_m[2] * low.vel[2]
        dg = [g_rho - inner - (0.5 * g_e) * low.square] + g_m + [g_e]
        for q in range(5):
            out[d, 10 + q, rows(m), :] = dg[q]
            out[d, 15 + q, rows(m), :] = fv[q] - dg[q]
        low, low_flux, low_weight, low_direct, low_dot = node, flux, weight, direct, dot


def place(d, q):
    return q if q in (0, 4) else 1 + PERMS[d][q - 1]


def own_node(flow, cot, direction, rows):
    return conserved_node(
        [flow[q, rows, :] for q in range(5)], [cot[q, rows, :] for q in range(5)], direction
    )


def near_node(first, other, choose, count, start, direction):
    def value(c):
        rows = pl.ds(c * count + start, 8)
        return jnp.where(choose, first[rows, :], other[rows, :])

    return conserved_node([value(q) for q in range(5)], [value(5 + q) for q in range(5)], direction)


def kernel_second(
    ids_hbm,
    flow,
    cot,
    lines,
    mid,
    modes,
    msg,
    tables,
    ahead_sums,
    base,
    extra,
    slope,
    zsum,
    out,
    zacc,
    zends,
    znext,
    zback,
    ids,
    sem,
):
    copy = pltpu.make_async_copy(ids_hbm, ids, sem)
    copy.start()

    def one(step, carry):
        adjoint_step(lines, mid, out, step)
        return carry

    lax.fori_loop(steps_ahead(), 6, one, 0)
    sub, lane, high = lane_tables()
    tiles = []
    for h in range(2):
        d_top = msg[pl.ds(6 + h, 1), :]
        d_all = msg[pl.ds(8 + h, 1), :]
        both = d_top + d_all
        mixed = jnp.where(high, both, d_all)
        for x in range(8):
            tiles.append(modes[pl.ds(h * 64 + 8 * x, 8), :] * (both if x >= 6 else mixed))
    weighed = jnp.concatenate(tiles, axis=0)
    weighed = jnp.dot(tables[2], weighed, precision=HIGHEST, preferred_element_type=F32)
    weighed = jnp.dot(weighed, tables[3], precision=HIGHEST, preferred_element_type=F32)
    for h in range(2):
        for x in range(8):
            rows = pl.ds(x * 16 + h * 8, 8)
            density = flow[0, rows, :]
            inv = rcp(density)
            vel = [flow[1 + i, rows, :] * inv for i in range(3)]
            square = vel[0] * vel[0] + vel[1] * vel[1] + vel[2] * vel[2]
            pres = 0.4 * (flow[4, rows, :] - 0.5 * density * square)
            value = weighed[h * 64 + 8 * x : h * 64 + 8 * x + 8]
            pull_e = 0.4 * (value * density)
            slope[0, rows, :] = value * pres + (0.5 * pull_e) * square
            for i in range(3):
                slope[1 + i, rows, :] = -(pull_e * vel[i])
            slope[4, rows, :] = pull_e

    back = [[place(d, q) for q in range(5)] for d in range(3)]
    def combine(group_at, target, offset):
        for q in range(5):
            first = group_at * 5
            qx = first + back[0].index(q)
            qy = first + back[1].index(q)
            qz = back[2].index(q)
            pieces = []
            for slot in range(16):
                h, s = slot // 8, slot % 8
                pieces.append(out[2, first + qz, pl.ds(h * 64 + s, 8, stride=8), :])
            if group_at in (0, 2):
                source = qz + (0 if group_at == 0 else 5)
                for slot in range(16):
                    upper = zacc[source, pl.ds(slot, 1), :]
                    lower = zacc[source, pl.ds(16 + slot, 1), :]
                    add = jnp.where(sub == 7, upper, jnp.where(sub == 0, lower, 0.0))
                    pieces[slot] = pieces[slot] + add
            whole = jnp.transpose(jnp.concatenate(pieces, axis=0))
            for h in range(2):
                for x in range(8):
                    value = (
                        out[0, qx, pl.ds(h * 64 + 8 * x, 8), :]
                        + out[1, qy, pl.ds(h * 64 + x, 8, stride=8), :]
                        + whole[h * 64 + 8 * x : h * 64 + 8 * x + 8]
                    )
                    target[offset + q, pl.ds(x * 16 + h * 8, 8), :] = value

    combine(1, extra, 0)
    combine(3, extra, 5)

    copy.wait()
    row = lax.broadcasted_iota(jnp.int32, (128, 128), 0)
    lanes = lax.broadcasted_iota(jnp.int32, (8, 128), 1)
    above = jnp.zeros((8, 128), jnp.int32)
    for k in range(16):
        above = jnp.where((lanes >> 3) == k, ids[k], above)
    above = above * 8 + (lanes & 7)
    above = jnp.concatenate([above] * 16, axis=0)
    up = jnp.where(above == row, 1.0, 0.0)
    own = msg[0:8, :]
    zsum[...] = jnp.dot(own, up, precision=HIGHEST, preferred_element_type=F32) + lax.dot_general(
        own, up, (((1,), (1,)), ((), ())), precision=HIGHEST, preferred_element_type=F32
    )

    for q in range(NQ):
        for end in range(2):
            for h in range(2):
                zends[q, pl.ds(end * 16 + h * 8, 8), :] = lines[2, q, pl.ds(h * 64 + 56 * end, 8), :]
    for k in range(16):
        znext[:, pl.ds(k, 1), :] = zends[:, pl.ds(ids[k], 1), :]
    for h in range(2):
        def side(ref, start):
            v = [ref[q, pl.ds(start + h * 8, 8), :] for q in range(NQ)]
            return Node(v[0:3], v[3], v[4], v[6], [0.5 * v[8]] + v[9:13])

        low_r, low_g, up_r, up_g = face_shares(side(zends, 16), side(znext, 0))
        for q in range(5):
            zacc[q, pl.ds(h * 8, 8), :] = low_r[q]
            zacc[5 + q, pl.ds(h * 8, 8), :] = low_g[q]
            zback[q, pl.ds(h * 8, 8), :] = up_r[q]
            zback[5 + q, pl.ds(h * 8, 8), :] = up_g[q]
    for k in range(16):
        zacc[:, pl.ds(16 + ids[k], 1), :] = zback[:, pl.ds(k, 1), :]

    combine(0, base, 0)
    combine(2, base, 5)

    rows = [pl.ds(7, 8, stride=16), pl.ds(8, 8, stride=16)]
    shares = face_shares(own_node(flow, cot, 1, rows[0]), own_node(flow, cot, 1, rows[1]))
    for side in range(2):
        for q in range(5):
            p = place(1, q)
            base[p, rows[side], :] += shares[2 * side][q]
            base[5 + p, rows[side], :] += shares[2 * side + 1][q]


def kernel_blend(
    msg,
    zsum,
    partner,
    other,
    ahead,
    behind,
    flow,
    cot,
    base,
    extra,
    slope,
    residual_hbm,
    grad_hbm,
    total,
    sems,
):
    even_x = lax.axis_index("gx") % 2 == 0
    even_y = lax.axis_index("gy") % 2 == 0
    sides = partner[160:168, :] + other[160:168, :]
    met, left = ahead[80:88, :], behind[80:88, :]
    above, below = jnp.where(even_y, met, left), jnp.where(even_y, left, met)
    for h in range(2):

        def beside_of(i):
            r = 2 * i + h
            low = below[2 * i + 1 : 2 * i + 2] if h == 0 else msg[2 * i : 2 * i + 1, :]
            high = msg[2 * i + 1 : 2 * i + 2, :] if h == 0 else above[2 * i : 2 * i + 1]
            return zsum[r : r + 1, :] + sides[r : r + 1] + low + high

        alpha = msg[h : h + 1, :]
        gain = msg[4 + h : 5 + h, :]
        around = beside_of(0)
        smooth = alpha + (1.0 - alpha) * around * (0.5 / 6.0)
        pull = gain * (1.0 - around * (0.5 / 6.0)) + beside_of(1) * (0.5 / 6.0)
        smooth = jnp.broadcast_to(smooth, (8, 128))
        pull = jnp.broadcast_to(pull, (8, 128))
        for x in range(8):
            rows = pl.ds(x * 16 + h * 8, 8)
            for q in range(5):
                total[q, rows, :] = base[q, rows, :] + smooth * extra[q, rows, :]
                total[5 + q, rows, :] = (
                    base[5 + q, rows, :] + smooth * extra[5 + q, rows, :] + pull * slope[q, rows, :]
                )

    def add(direction, rows, res, grad):
        for q in range(5):
            p = place(direction, q)
            total[p, rows, :] += res[q]
            total[5 + p, rows, :] += grad[q]

    here, top = pl.ds(0, 8, stride=16), pl.ds(15, 8, stride=16)
    shares = face_shares(near_node(behind, ahead, even_y, 8, 0, 1), own_node(flow, cot, 1, here))
    add(1, here, shares[2], shares[3])
    shares = face_shares(own_node(flow, cot, 1, top), near_node(ahead, behind, even_y, 8, 0, 1))
    add(1, top, shares[0], shares[1])

    def send(i, start, count):
        rows = pl.ds(start, count)
        return [
            pltpu.make_async_copy(
                total.at[pl.ds(0, 5), rows], residual_hbm.at[pl.ds(0, 5), rows], sems.at[2 * i]
            ),
            pltpu.make_async_copy(
                total.at[pl.ds(5, 5), rows], grad_hbm.at[pl.ds(0, 5), rows], sems.at[2 * i + 1]
            ),
        ]

    copies = send(0, 16, 96)
    for copy in copies:
        copy.start()
    for h in range(2):
        here, top = pl.ds(h * 8, 8), pl.ds(112 + h * 8, 8)
        shares = face_shares(
            near_node(other, partner, even_x, 16, h * 8, 0), own_node(flow, cot, 0, here)
        )
        add(0, here, shares[2], shares[3])
        shares = face_shares(
            own_node(flow, cot, 0, top), near_node(partner, other, even_x, 16, h * 8, 0)
        )
        add(0, top, shares[0], shares[1])
    last = send(1, 0, 16) + send(2, 112, 16)
    for copy in last:
        copy.start()
    for copy in copies + last:
        copy.wait()


def swapped(value, axis, first):
    count = lax.axis_size(axis)
    pairs = []
    for i in range(first, count + first, 2):
        a, b = i % count, (i + 1) % count
        pairs += [(a, b), (b, a)]
    return lax.ppermute(value, axis, pairs)


def shape(*dims):
    return jax.ShapeDtypeStruct(dims, F32)


def in_hbm(value):
    return pltpu.with_memory_space_constraint(value, pltpu.HBM)


def shards(flow_state, cotangent, clip_flags, successor_ids):
    flow = flow_state.reshape(5, ROWS, 128)
    cot = cotangent.reshape(5, ROWS, 128)
    vmem = pl.BlockSpec(memory_space=pltpu.VMEM)
    hbm = pl.BlockSpec(memory_space=pltpu.HBM)
    modal = np.asarray(TO_MODAL, np.float32)
    kxy = np.kron(np.eye(2), np.kron(modal, modal)).astype(np.float32)
    kz = np.kron(np.eye(16), modal).astype(np.float32)
    constants = np.stack([kxy, kz.T, kxy.T, kz])

    lines, mid, modes, msg, to_partner, to_other, to_ahead, to_behind, flow_v, cot_v, tables, sums = pl.pallas_call(
        kernel_first,
        out_shape=(
            shape(3, NQ, ROWS, 128),
            shape(6, RATES + 35, 8, 128),
            shape(ROWS, 128),
            shape(16, 128),
            shape(168, 128),
            shape(168, 128),
            shape(88, 128),
            shape(88, 128),
            shape(5, ROWS, 128),
            shape(5, ROWS, 128),
            shape(4, 128, 128),
            shape(3, 20, ROWS, 128),
        ),
        in_specs=[hbm] * 4,
        out_specs=[vmem] * 12,
        scratch_shapes=[
            pltpu.VMEM((NQ, ROWS, 128), F32),
            pltpu.VMEM((NQ, ROWS, 128), F32),
            pltpu.VMEM((ROWS, 128), F32),
            pltpu.VMEM((6, 8, 128), F32),
            pltpu.VMEM((2, 16), jnp.int32),
            pltpu.SemaphoreType.DMA((4,)),
        ],
        compiler_params=pltpu.CompilerParams(vmem_limit_bytes=16 * 1024 * 1024),
        name="first",
    )(in_hbm(flow), in_hbm(cot), in_hbm(clip_flags.reshape(2, 16)), in_hbm(jnp.asarray(constants)))

    ahead = swapped(to_ahead, "gy", 0)
    behind = swapped(to_behind, "gy", 1)
    other = swapped(to_other, "gx", 1)
    partner = swapped(to_partner, "gx", 0)

    base, extra, slope, zsum, _ = pl.pallas_call(
        kernel_second,
        out_shape=(shape(10, ROWS, 128), shape(10, ROWS, 128), shape(5, ROWS, 128), shape(8, 128), shape(3, 20, ROWS, 128)),
        in_specs=[hbm] + [vmem] * 8,
        out_specs=[vmem] * 5,
        input_output_aliases={8: 4},
        scratch_shapes=[
            pltpu.VMEM((10, 32, 128), F32),
            pltpu.VMEM((NQ, 32, 128), F32),
            pltpu.VMEM((NQ, 16, 128), F32),
            pltpu.VMEM((10, 16, 128), F32),
            pltpu.SMEM((16,), jnp.int32),
            pltpu.SemaphoreType.DMA(()),
        ],
        compiler_params=pltpu.CompilerParams(vmem_limit_bytes=16 * 1024 * 1024),
        name="second",
    )(in_hbm(successor_ids), flow_v, cot_v, lines, mid, modes, msg, tables, sums)

    residual, grad = pl.pallas_call(
        kernel_blend,
        out_shape=(shape(5, ROWS, 128), shape(5, ROWS, 128)),
        in_specs=[vmem] * 11,
        out_specs=[hbm] * 2,
        scratch_shapes=[pltpu.VMEM((10, ROWS, 128), F32), pltpu.SemaphoreType.DMA((6,))],
        compiler_params=pltpu.CompilerParams(vmem_limit_bytes=16 * 1024 * 1024),
        name="blend",
    )(msg, zsum, partner, other, ahead, behind, flow_v, cot_v, base, extra, slope)
    return residual.reshape(flow_state.shape), grad.reshape(flow_state.shape)


def solution(mesh):
    placed = P(None, "gx", "gy", None)
    return jax.shard_map(
        shards,
        mesh=mesh,
        in_specs=(placed, placed, P("gx", "gy", None), P()),
        out_specs=(placed, placed),
        check_vma=False,
    )
```

```python
import jax
import jax.numpy as jnp
import numpy as np
from jax import lax
from jax.experimental import pallas as pl
from jax.experimental.pallas import tpu as pltpu
from jax.sharding import PartitionSpec as P
from numpy.polynomial import chebyshev, polynomial

F32 = jnp.float32
HIGHEST = lax.Precision.HIGHEST
EPS = 1e-05
PERMS = ((0, 1, 2), (1, 0, 2), (2, 0, 1))
NQ = 13
ROWS = 128


def legendre_values(points, node_count):
    values_table = np.zeros((points.shape[0], node_count))
    values_table[:, 0] = 1.0
    values_table[:, 1] = points
    for degree_index in range(2, node_count):
        values_table[:, degree_index] = (
            (2 * degree_index - 1) * points * values_table[:, degree_index - 1]
            - (degree_index - 1) * values_table[:, degree_index - 2]
        ) / degree_index
    return values_table


def node_tables():
    degree = 7
    node_count = degree + 1
    points = -np.cos(np.pi * np.arange(node_count) / degree)
    for newton_step in range(60):
        legend = legendre_values(points, node_count)
        points = points - (points * legend[:, degree] - legend[:, degree - 1]) / (
            node_count * legend[:, degree]
        )
    legend = legendre_values(points, node_count)
    weights = 2.0 / (degree * node_count * legend[:, degree] * legend[:, degree])
    differ = np.zeros((node_count, node_count))
    for row_index in range(node_count):
        for col_index in range(node_count):
            if row_index != col_index:
                differ[row_index, col_index] = legend[row_index, degree] / (
                    legend[col_index, degree] * (points[row_index] - points[col_index])
                )
    norm_table = 2.0 / (2.0 * np.arange(node_count) + 1.0)
    norm_table[degree] = 2.0 / degree
    to_modal = legend.T * weights[None, :] / norm_table[:, None]
    return (weights, differ, to_modal)


WEIGHTS, DIFFER, TO_MODAL = node_tables()
INV_W = [float(1.0 / w) for w in WEIGHTS]
SKEW = 2.0 * DIFFER * WEIGHTS[:, None]


def fitted(function, top, degree):
    series = chebyshev.Chebyshev.interpolate(function, degree, domain=[0.0, top])
    return [float(np.float32(c)) for c in series.convert(kind=polynomial.Polynomial).coef]


def sinhc(square):
    root = np.sqrt(np.maximum(square, 1e-12))
    return np.sinh(root) / root


def sinhc_slope(square):
    root = np.sqrt(np.maximum(square, 1e-12))
    exact = (np.cosh(root) - np.sinh(root) / root) / (root * root)
    series = 1.0 / 3.0 + square / 30.0 + square**2 / 840.0 + square**3 / 45360.0
    return np.where(square < 1e-2, series, exact)


RATES = 5 * 28
PAIR = {pair: i for i, pair in enumerate((k, j) for k in range(7) for j in range(k + 1, 8))}

MEAN_R = fitted(sinhc, 3.0, 4)
SLOPE_R = fitted(sinhc_slope, 3.0, 3)
MEAN_B = fitted(sinhc, 12.0, 5)
SLOPE_B = fitted(sinhc_slope, 12.0, 5)


def horner(coeffs, value):
    total = coeffs[-1] * value + coeffs[-2]
    for c in coeffs[-3::-1]:
        total = total * value + c
    return total


def rcp(value):
    return 1.0 / value


def log_parts(density, pressure):
    inv = rcp(density)
    ratio = pressure * inv
    half_log = 0.5 * jnp.log(density)
    return (
        jnp.sqrt(density),
        half_log,
        jnp.sqrt(5.0 * ratio),
        half_log - 0.5 * jnp.log(pressure),
    )


class Node:
    def __init__(self, vel, pres, root, theta, cot):
        self.vel, self.pres, self.cot = vel, pres, cot
        density = root * root
        vn, v1, v2 = vel
        mom = [density * v for v in vel]
        self.square = vn * vn + v1 * v1 + v2 * v2
        energy = 2.5 * pres + (0.5 * density) * self.square
        self.state = [density] + mom + [energy]
        mn = mom[0]
        self.flux = [mn, mn * vn + pres, mn * v1, mn * v2, (energy + pres) * vn]
        self.sound = theta * float(np.sqrt(1.4 / 5.0))
        self.speed = jnp.abs(vn) + self.sound

    def pull(self, half, direct, speed_cot):
        density = self.state[0]
        vn, v1, v2 = self.vel
        grad = [direct[i] + half[i] * vn for i in range(5)]
        sign = jnp.where(vn >= 0.0, 1.0, -1.0)
        dvn = half[0] * self.state[0]
        for i in range(1, 5):
            dvn = dvn + half[i] * self.state[i]
        dvn = dvn + half[4] * self.pres + speed_cot * sign
        inv = rcp(density)
        part = (0.5 * speed_cot) * self.sound
        dpres = half[1] + half[4] * vn + part * rcp(self.pres)
        over = dvn * inv
        pull_e = 0.4 * dpres
        grad[0] = grad[0] - part * inv - over * vn + (0.5 * pull_e) * self.square
        grad[1] = grad[1] + over - pull_e * vn
        grad[2] = grad[2] - pull_e * v1
        grad[3] = grad[3] - pull_e * v2
        grad[4] = grad[4] + pull_e
        return grad


def face_adjoint(low, up):
    jump = [b - a for a, b in zip(low.state, up.state)]
    weight = [b - a for a, b in zip(low.cot, up.cot)]
    speed = 0.5 * (low.speed + up.speed)
    dot = weight[0] * jump[0]
    for i in range(1, 5):
        dot = dot + weight[i] * jump[i]
    return weight, [speed * w for w in weight], -0.5 * dot


def face_rate(low, up):
    speed = 0.5 * (low.speed + up.speed)
    return [
        a + b - speed * (y - x) for a, b, x, y in zip(low.flux, up.flux, low.state, up.state)
    ]


def lane_tables():
    sub = lax.broadcasted_iota(jnp.int32, (8, 128), 0)
    lane = lax.broadcasted_iota(jnp.int32, (8, 128), 1)
    return sub, lane, (sub >= 6) | ((lane & 7) >= 6)


def kernel_first(
    flow_hbm,
    cot_hbm,
    flags_hbm,
    tables_hbm,
    lines,
    mid,
    modes,
    msg,
    to_partner,
    to_other,
    to_ahead,
    to_behind,
    flow,
    cot,
    tables,
    out,
    nat,
    turned,
    prod,
    gsum,
    flags,
    sems,
):
    copies = [
        pltpu.make_async_copy(source, target, sems.at[i])
        for i, (source, target) in enumerate(
            ((flow_hbm, flow), (cot_hbm, cot), (tables_hbm, tables), (flags_hbm, flags))
        )
    ]
    for copy in copies:
        copy.start()
    even_x = lax.axis_index("gx") % 2 == 0
    even_y = lax.axis_index("gy") % 2 == 0
    for copy in copies:
        copy.wait()
    for c in range(10):
        source, q = (flow, c) if c < 5 else (cot, c - 5)
        top, low = source[q, pl.ds(112, 16), :], source[q, pl.ds(0, 16), :]
        to_partner[pl.ds(16 * c, 16), :] = jnp.where(even_x, top, low)
        to_other[pl.ds(16 * c, 16), :] = jnp.where(even_x, low, top)
        top, low = source[q, pl.ds(15, 8, stride=16), :], source[q, pl.ds(0, 8, stride=16), :]
        to_ahead[pl.ds(8 * c, 8), :] = jnp.where(even_y, top, low)
        to_behind[pl.ds(8 * c, 8), :] = jnp.where(even_y, low, top)

    for x in range(8):
        for h in range(2):
            src = pl.ds(x * 16 + h * 8, 8)
            dst = pl.ds(h * 64 + x * 8, 8)
            density = flow[0, src, :]
            inv = rcp(density)
            mom = [flow[1 + i, src, :] for i in range(3)]
            vel = [m * inv for m in mom]
            kinetic = mom[0] * vel[0] + mom[1] * vel[1] + mom[2] * vel[2]
            pres = 0.4 * (flow[4, src, :] - 0.5 * kinetic)
            prod[dst, :] = density * pres
            parts = vel + [pres] + list(log_parts(density, pres))
            for q in range(8):
                nat[q, dst, :] = parts[q]
            for q in range(5):
                value = cot[q, src, :]
                nat[8 + q, dst, :] = 2.0 * value if q == 0 else value
    for q in range(NQ):
        turned[q] = jnp.transpose(nat[q])
    for d in range(3):
        perm = PERMS[d]
        order = [perm[0], perm[1], perm[2], 3, 4, 5, 6, 7, 8] + [9 + i for i in perm] + [12]
        source = nat if d < 2 else turned
        for q in range(NQ):
            for h in range(2):
                for k in range(8):
                    rows = pl.ds(h * 64 + 8 * k, 8) if d == 0 else pl.ds(h * 64 + k, 8, stride=8)
                    value = source[order[q], rows, :]
                    lines[d, q, pl.ds(h * 64 + 8 * k, 8), :] = value * (0.5 * INV_W[k]) if q >= 8 else value

    sub, lane, high = lane_tables()
    coeffs = jnp.dot(tables[0], prod[...], precision=HIGHEST, preferred_element_type=F32)
    coeffs = jnp.dot(coeffs, tables[1], precision=HIGHEST, preferred_element_type=F32)
    modes[...] = coeffs
    squares = coeffs * coeffs
    group = jnp.where(
        lax.broadcasted_iota(jnp.int32, (128, 128), 0) >> 3
        == lax.broadcasted_iota(jnp.int32, (128, 128), 1) >> 3,
        1.0,
        0.0,
    )
    spread = (
        lax.broadcasted_iota(jnp.int32, (16, 128), 0)
        == lax.broadcasted_iota(jnp.int32, (16, 128), 1) >> 3
    )
    packed = jnp.zeros((8, 128), F32)
    for h in range(2):
        every = squares[h * 64 : h * 64 + 8]
        for x in range(1, 6):
            every = every + squares[h * 64 + 8 * x : h * 64 + 8 * x + 8]
        ends = squares[h * 64 + 48 : h * 64 + 56] + squares[h * 64 + 56 : h * 64 + 64]
        top = jnp.sum(jnp.where(high, every, 0.0) + ends, axis=0, keepdims=True)
        packed = jnp.where(sub == h, top, packed)
        packed = jnp.where(sub == 2 + h, jnp.sum(every + ends, axis=0, keepdims=True), packed)
    sums = jnp.dot(packed, group, precision=HIGHEST, preferred_element_type=F32)
    flag_rows = jnp.dot(
        flags[...].astype(F32),
        jnp.where(spread, 1.0, 0.0),
        precision=HIGHEST,
        preferred_element_type=F32,
    )
    sub16 = lax.broadcasted_iota(jnp.int32, (16, 128), 0)
    factors = jnp.zeros((16, 128), F32)
    for h in range(2):
        top = sums[h : h + 1] + EPS
        every = 0.01 * (sums[2 + h : 3 + h] + EPS)
        flag = flag_rows[h : h + 1]
        over = rcp(top + every)
        keep = flag < 0.5
        alpha = jnp.where(keep, 0.5 * top * over, jnp.where(flag > 1.5, 0.5, 0.0))
        d_top = jnp.where(keep, every * over * over, 0.0)
        d_all = jnp.where(keep, -0.01 * top * over * over, 0.0)
        for i, row in ((0, alpha), (6, d_top), (8, d_all)):
            factors = jnp.where(sub16 == i + h, row, factors)
    msg[...] = factors

    def one(step):
        d = step // 2
        base = (step % 2) * 64

        def load(k):
            start = base + 8 * k
            return [lines[d, q, pl.ds(start, 8), :] for q in range(NQ)]

        gained = jnp.zeros((8, 128), F32)
        for k in range(7):
            a = load(k)
            for j in range(k + 1, 8):
                skew = float(SKEW[k, j])
                b = load(j)
                vn, v1, v2 = (a[i] + b[i] for i in range(3))
                delta = [a[8 + i] - b[8 + i] for i in range(5)]
                y = a[5] - b[5]
                mean = ((0.5 * skew) * (a[4] * b[4])) * horner(MEAN_R, y * y)
                yb = a[7] - b[7]
                quot = rcp(horner(MEAN_B, yb * yb))
                inv5 = (a[6] * b[6]) * quot
                dot = a[0] * b[0] + a[1] * b[1] + a[2] * b[2] + inv5
                phi = delta[0] + delta[1] * vn + delta[2] * v1 + delta[3] * v2 + delta[4] * dot
                for q, value in enumerate((mean, quot, inv5, dot, phi)):
                    mid[step, 5 * PAIR[k, j] + q] = value
                work = delta[1] * (a[3] + b[3]) + delta[4] * (a[3] * b[0] + b[3] * a[0])
                gained = gained + (mean * vn) * phi + skew * work
        low = None
        for k in range(8):
            a = load(k)
            node = Node(a[0:3], a[3], a[4], a[6], [0.5 * a[8]] + a[9:13])
            if k:
                for q, rate in enumerate(face_rate(low, node)):
                    mid[step, RATES + 5 * (k - 1) + q] = rate
                    gained = gained + rate * (node.cot[q] - low.cot[q])
            low = node
        gsum[step] = gained

    for step in range(6):
        one(step)

    half_lane = lax.broadcasted_iota(jnp.int32, (16, 128), 1) >> 6
    along = jnp.concatenate([gsum[4], gsum[5]], axis=0)
    factors = msg[...]
    for h in range(2):
        row = jnp.sum(gsum[h] + gsum[2 + h], axis=0, keepdims=True)
        both = jnp.where(half_lane == h, along, 0.0) + jnp.where(spread, row, 0.0)
        column = jnp.sum(both, axis=1, keepdims=True)
        gain = jnp.sum(jnp.where(spread, column, 0.0), axis=0, keepdims=True)
        factors = jnp.where(sub16 == 4 + h, gain, factors)
        factors = jnp.where(sub16 == 2 + h, gain * (1.0 - factors[h : h + 1]), factors)
    msg[...] = factors
    for target, row in ((to_partner, 160), (to_other, 160), (to_ahead, 80), (to_behind, 80)):
        target[pl.ds(row, 8), :] = factors[0:8]

    def two(step, carry):
        adjoint_step(lines, mid, out, step)
        return carry

    lax.fori_loop(0, steps_ahead(), two, 0)


def conserved_node(state, cot, direction):
    perm = PERMS[direction]
    density = state[0]
    inv = rcp(density)
    vel = [state[1 + i] * inv for i in perm]
    square = vel[0] * vel[0] + vel[1] * vel[1] + vel[2] * vel[2]
    pres = 0.4 * (state[4] - 0.5 * density * square)
    scaled = [cot[0]] + [cot[1 + i] for i in perm] + [cot[4]]
    return Node(vel, pres, jnp.sqrt(density), jnp.sqrt(5.0 * pres * inv), [c * (0.5 * INV_W[0]) for c in scaled])


def face_shares(low, up):
    rate = face_rate(low, up)
    weight, direct, dot = face_adjoint(low, up)
    return (
        [(-0.5 * INV_W[7]) * f for f in rate],
        low.pull(weight, direct, dot),
        [(0.5 * INV_W[0]) * f for f in rate],
        up.pull(weight, [-x for x in direct], dot),
    )


def steps_ahead():
    gx = lax.axis_index("gx")
    plane = 2 * lax.axis_index("gy") + gx // 32
    corner = jnp.where(plane < 4, 5 - plane, 0)
    return jnp.where(gx % 32 == 0, corner, jnp.where(plane < 2, 4 - plane, 0))


def adjoint_step(lines, mid, out, step):
    d = step // 2
    base = (step % 2) * 64

    def rows(k):
        return pl.ds(pl.multiple_of(base + 8 * k, 8), 8)

    for k in range(7):
        a = [lines[d, q, rows(k), :] for q in range(NQ)]
        acc = [None] * 13 if k == 0 else [out[d, q, rows(k), :] for q in range(13)]
        for j in range(k + 1, 8):
            skew = float(SKEW[k, j])
            b = [lines[d, q, rows(j), :] for q in range(NQ)]
            mean, quot, inv5, dot, phi = (mid[step, 5 * PAIR[k, j] + q] for q in range(5))
            vn, v1, v2, pres = (a[i] + b[i] for i in range(4))
            delta = [None] + [a[8 + i] - b[8 + i] for i in range(1, 5)]
            y = a[5] - b[5]
            slope = (((0.5 * skew) * (a[4] * b[4])) * y) * horner(SLOPE_R, y * y)
            yb = a[7] - b[7]
            tilt = yb * (horner(SLOPE_B, yb * yb) * quot)
            mass = mean * vn
            flux = [
                mass,
                mass * vn + skew * pres,
                mass * v1,
                mass * v2,
                mass * dot + skew * (a[3] * b[0] + b[3] * a[0]),
            ]
            t = skew * delta[4]
            w = mass * delta[4]
            pp = phi * mass
            qq = (phi * vn) * slope
            xx = w * inv5
            zz = xx * tilt
            shared = [
                phi * mean + mass * (delta[1] + delta[4] * vn) + t * pres,
                mass * (delta[2] + delta[4] * v1),
                mass * (delta[3] + delta[4] * v2),
                skew * (delta[1] + delta[4] * vn),
            ]
            ups = flux + [pp + qq] + shared + [xx + zz, w, t]
            downs = [None] * 5 + [pp - qq] + shared + [xx - zz, w, t]
            for q in range(13):
                acc[q] = ups[q] if acc[q] is None else acc[q] + ups[q]
                if q < 5:
                    value = -flux[q] if k == 0 else out[d, q, rows(j), :] - flux[q]
                else:
                    value = downs[q] if k == 0 else out[d, q, rows(j), :] + downs[q]
                out[d, q, rows(j), :] = value
        for q in range(13):
            out[d, q, rows(k), :] = acc[q]

    low = None
    zero = jnp.zeros((8, 128), F32)
    low_flux, low_weight, low_direct, low_dot = [zero] * 5, [zero] * 5, [zero] * 5, zero
    for k in range(9):
        if k < 8:
            a = [lines[d, q, rows(k), :] for q in range(NQ)]
            node = Node(a[0:3], a[3], a[4], a[6], [0.5 * a[8]] + a[9:13])
        if k == 0:
            low = node
            continue
        if k < 8:
            weight, direct, dot = face_adjoint(low, node)
            flux = [mid[step, RATES + 5 * (k - 1) + q] for q in range(5)]
        else:
            flux, weight, direct, dot = [zero] * 5, [zero] * 5, [zero] * 5, zero
        m = k - 1
        total = [out[d, q, rows(m), :] for q in range(13)]
        for i in range(3):
            total[6 + i] = total[6 + i] - total[11] * low.vel[i]
        total[6] = total[6] - total[12] * low.pres
        total[9] = total[9] - total[12] * low.vel[0]
        total[0] = 2.0 * total[0]
        for q in range(5):
            diff = total[q] - (flux[q] - low_flux[q])
            out[d, q, rows(m), :] = total[q] * (-0.5 * INV_W[m])
            out[d, 5 + q, rows(m), :] = diff * (0.5 * INV_W[m])
        fv = low.pull(
            [x + z for x, z in zip(low_weight, weight)],
            [x - z for x, z in zip(direct, low_direct)],
            low_dot + dot,
        )
        inv = rcp(low.state[0])
        beta = 0.5 * total[10]
        g_rho = (beta - 0.5 * total[5]) * inv
        g_e = -0.4 * (total[9] + beta * rcp(low.pres))
        g_m = [-(total[6 + i] * inv) - g_e * low.vel[i] for i in range(3)]
        inner = g_m[0] * low.vel[0] + g_m[1] * low.vel[1] + g_m[2] * low.vel[2]
        dg = [g_rho - inner - (0.5 * g_e) * low.square] + g_m + [g_e]
        for q in range(5):
            out[d, 10 + q, rows(m), :] = dg[q]
            out[d, 15 + q, rows(m), :] = fv[q] - dg[q]
        low, low_flux, low_weight, low_direct, low_dot = node, flux, weight, direct, dot


def place(d, q):
    return q if q in (0, 4) else 1 + PERMS[d][q - 1]


def own_node(flow, cot, direction, rows):
    return conserved_node(
        [flow[q, rows, :] for q in range(5)], [cot[q, rows, :] for q in range(5)], direction
    )


def near_node(first, other, choose, count, start, direction):
    def value(c):
        rows = pl.ds(c * count + start, 8)
        return jnp.where(choose, first[rows, :], other[rows, :])

    return conserved_node([value(q) for q in range(5)], [value(5 + q) for q in range(5)], direction)


def kernel_second(
    ids_hbm,
    flow,
    cot,
    lines,
    mid,
    modes,
    msg,
    tables,
    ahead_sums,
    base,
    extra,
    slope,
    zsum,
    out,
    zacc,
    zends,
    znext,
    zback,
    ids,
    sem,
):
    copy = pltpu.make_async_copy(ids_hbm, ids, sem)
    copy.start()

    def one(step, carry):
        adjoint_step(lines, mid, out, step)
        return carry

    lax.fori_loop(steps_ahead(), 6, one, 0)
    sub, lane, high = lane_tables()
    tiles = []
    for h in range(2):
        d_top = msg[pl.ds(6 + h, 1), :]
        d_all = msg[pl.ds(8 + h, 1), :]
        both = d_top + d_all
        mixed = jnp.where(high, both, d_all)
        for x in range(8):
            tiles.append(modes[pl.ds(h * 64 + 8 * x, 8), :] * (both if x >= 6 else mixed))
    weighed = jnp.concatenate(tiles, axis=0)
    weighed = jnp.dot(tables[2], weighed, precision=HIGHEST, preferred_element_type=F32)
    weighed = jnp.dot(weighed, tables[3], precision=HIGHEST, preferred_element_type=F32)
    for h in range(2):
        for x in range(8):
            rows = pl.ds(x * 16 + h * 8, 8)
            density = flow[0, rows, :]
            inv = rcp(density)
            vel = [flow[1 + i, rows, :] * inv for i in range(3)]
            square = vel[0] * vel[0] + vel[1] * vel[1] + vel[2] * vel[2]
            pres = 0.4 * (flow[4, rows, :] - 0.5 * density * square)
            value = weighed[h * 64 + 8 * x : h * 64 + 8 * x + 8]
            pull_e = 0.4 * (value * density)
            slope[0, rows, :] = value * pres + (0.5 * pull_e) * square
            for i in range(3):
                slope[1 + i, rows, :] = -(pull_e * vel[i])
            slope[4, rows, :] = pull_e

    back = [[place(d, q) for q in range(5)] for d in range(3)]
    def combine(group_at, target, offset):
        for q in range(5):
            first = group_at * 5
            qx = first + back[0].index(q)
            qy = first + back[1].index(q)
            qz = back[2].index(q)
            pieces = []
            for slot in range(16):
                h, s = slot // 8, slot % 8
                pieces.append(out[2, first + qz, pl.ds(h * 64 + s, 8, stride=8), :])
            if group_at in (0, 2):
                source = qz + (0 if group_at == 0 else 5)
                for slot in range(16):
                    upper = zacc[source, pl.ds(slot, 1), :]
                    lower = zacc[source, pl.ds(16 + slot, 1), :]
                    add = jnp.where(sub == 7, upper, jnp.where(sub == 0, lower, 0.0))
                    pieces[slot] = pieces[slot] + add
            whole = jnp.transpose(jnp.concatenate(pieces, axis=0))
            for h in range(2):
                for x in range(8):
                    value = (
                        out[0, qx, pl.ds(h * 64 + 8 * x, 8), :]
                        + out[1, qy, pl.ds(h * 64 + x, 8, stride=8), :]
                        + whole[h * 64 + 8 * x : h * 64 + 8 * x + 8]
                    )
                    target[offset + q, pl.ds(x * 16 + h * 8, 8), :] = value

    combine(1, extra, 0)
    combine(3, extra, 5)

    copy.wait()
    row = lax.broadcasted_iota(jnp.int32, (128, 128), 0)
    lanes = lax.broadcasted_iota(jnp.int32, (8, 128), 1)
    above = jnp.zeros((8, 128), jnp.int32)
    for k in range(16):
        above = jnp.where((lanes >> 3) == k, ids[k], above)
    above = above * 8 + (lanes & 7)
    above = jnp.concatenate([above] * 16, axis=0)
    up = jnp.where(above == row, 1.0, 0.0)
    own = msg[0:8, :]
    zsum[...] = jnp.dot(own, up, precision=HIGHEST, preferred_element_type=F32) + lax.dot_general(
        own, up, (((1,), (1,)), ((), ())), precision=HIGHEST, preferred_element_type=F32
    )

    for q in range(NQ):
        for end in range(2):
            for h in range(2):
                zends[q, pl.ds(end * 16 + h * 8, 8), :] = lines[2, q, pl.ds(h * 64 + 56 * end, 8), :]
    for k in range(16):
        znext[:, pl.ds(k, 1), :] = zends[:, pl.ds(ids[k], 1), :]
    for h in range(2):
        def side(ref, start):
            v = [ref[q, pl.ds(start + h * 8, 8), :] for q in range(NQ)]
            return Node(v[0:3], v[3], v[4], v[6], [0.5 * v[8]] + v[9:13])

        low_r, low_g, up_r, up_g = face_shares(side(zends, 16), side(znext, 0))
        for q in range(5):
            zacc[q, pl.ds(h * 8, 8), :] = low_r[q]
            zacc[5 + q, pl.ds(h * 8, 8), :] = low_g[q]
            zback[q, pl.ds(h * 8, 8), :] = up_r[q]
            zback[5 + q, pl.ds(h * 8, 8), :] = up_g[q]
    for k in range(16):
        zacc[:, pl.ds(16 + ids[k], 1), :] = zback[:, pl.ds(k, 1), :]

    combine(0, base, 0)
    combine(2, base, 5)

    rows = [pl.ds(7, 8, stride=16), pl.ds(8, 8, stride=16)]
    shares = face_shares(own_node(flow, cot, 1, rows[0]), own_node(flow, cot, 1, rows[1]))
    for side in range(2):
        for q in range(5):
            p = place(1, q)
            base[p, rows[side], :] += shares[2 * side][q]
            base[5 + p, rows[side], :] += shares[2 * side + 1][q]


def kernel_blend(
    msg,
    zsum,
    partner,
    other,
    ahead,
    behind,
    flow,
    cot,
    base,
    extra,
    slope,
    residual_hbm,
    grad_hbm,
    total,
    sems,
):
    even_x = lax.axis_index("gx") % 2 == 0
    even_y = lax.axis_index("gy") % 2 == 0
    sides = partner[160:168, :] + other[160:168, :]
    met, left = ahead[80:88, :], behind[80:88, :]
    above, below = jnp.where(even_y, met, left), jnp.where(even_y, left, met)
    for h in range(2):

        def beside_of(i):
            r = 2 * i + h
            low = below[2 * i + 1 : 2 * i + 2] if h == 0 else msg[2 * i : 2 * i + 1, :]
            high = msg[2 * i + 1 : 2 * i + 2, :] if h == 0 else above[2 * i : 2 * i + 1]
            return zsum[r : r + 1, :] + sides[r : r + 1] + low + high

        alpha = msg[h : h + 1, :]
        gain = msg[4 + h : 5 + h, :]
        around = beside_of(0)
        smooth = alpha + (1.0 - alpha) * around * (0.5 / 6.0)
        pull = gain * (1.0 - around * (0.5 / 6.0)) + beside_of(1) * (0.5 / 6.0)
        smooth = jnp.broadcast_to(smooth, (8, 128))
        pull = jnp.broadcast_to(pull, (8, 128))
        for x in range(8):
            rows = pl.ds(x * 16 + h * 8, 8)
            for q in range(5):
                total[q, rows, :] = base[q, rows, :] + smooth * extra[q, rows, :]
                total[5 + q, rows, :] = (
                    base[5 + q, rows, :] + smooth * extra[5 + q, rows, :] + pull * slope[q, rows, :]
                )

    def add(direction, rows, res, grad):
        for q in range(5):
            p = place(direction, q)
            total[p, rows, :] += res[q]
            total[5 + p, rows, :] += grad[q]

    here, top = pl.ds(0, 8, stride=16), pl.ds(15, 8, stride=16)
    shares = face_shares(near_node(behind, ahead, even_y, 8, 0, 1), own_node(flow, cot, 1, here))
    add(1, here, shares[2], shares[3])
    shares = face_shares(own_node(flow, cot, 1, top), near_node(ahead, behind, even_y, 8, 0, 1))
    add(1, top, shares[0], shares[1])

    def send(i, start, count):
        rows = pl.ds(start, count)
        return [
            pltpu.make_async_copy(
                total.at[pl.ds(0, 5), rows], residual_hbm.at[pl.ds(0, 5), rows], sems.at[2 * i]
            ),
            pltpu.make_async_copy(
                total.at[pl.ds(5, 5), rows], grad_hbm.at[pl.ds(0, 5), rows], sems.at[2 * i + 1]
            ),
        ]

    copies = send(0, 16, 96)
    for copy in copies:
        copy.start()
    for h in range(2):
        here, top = pl.ds(h * 8, 8), pl.ds(112 + h * 8, 8)
        shares = face_shares(
            near_node(other, partner, even_x, 16, h * 8, 0), own_node(flow, cot, 0, here)
        )
        add(0, here, shares[2], shares[3])
        shares = face_shares(
            own_node(flow, cot, 0, top), near_node(partner, other, even_x, 16, h * 8, 0)
        )
        add(0, top, shares[0], shares[1])
    last = send(1, 0, 16) + send(2, 112, 16)
    for copy in last:
        copy.start()
    for copy in copies + last:
        copy.wait()


def swapped(value, axis, first):
    count = lax.axis_size(axis)
    pairs = []
    for i in range(first, count + first, 2):
        a, b = i % count, (i + 1) % count
        pairs += [(a, b), (b, a)]
    return lax.ppermute(value, axis, pairs)


def shape(*dims):
    return jax.ShapeDtypeStruct(dims, F32)


def in_hbm(value):
    return pltpu.with_memory_space_constraint(value, pltpu.HBM)


def shards(flow_state, cotangent, clip_flags, successor_ids):
    flow = flow_state.reshape(5, ROWS, 128)
    cot = cotangent.reshape(5, ROWS, 128)
    vmem = pl.BlockSpec(memory_space=pltpu.VMEM)
    hbm = pl.BlockSpec(memory_space=pltpu.HBM)
    modal = np.asarray(TO_MODAL, np.float32)
    kxy = np.kron(np.eye(2), np.kron(modal, modal)).astype(np.float32)
    kz = np.kron(np.eye(16), modal).astype(np.float32)
    constants = np.stack([kxy, kz.T, kxy.T, kz])

    lines, mid, modes, msg, to_partner, to_other, to_ahead, to_behind, flow_v, cot_v, tables, sums = pl.pallas_call(
        kernel_first,
        out_shape=(
            shape(3, NQ, ROWS, 128),
            shape(6, RATES + 35, 8, 128),
            shape(ROWS, 128),
            shape(16, 128),
            shape(168, 128),
            shape(168, 128),
            shape(88, 128),
            shape(88, 128),
            shape(5, ROWS, 128),
            shape(5, ROWS, 128),
            shape(4, 128, 128),
            shape(3, 20, ROWS, 128),
        ),
        in_specs=[hbm] * 4,
        out_specs=[vmem] * 12,
        scratch_shapes=[
            pltpu.VMEM((NQ, ROWS, 128), F32),
            pltpu.VMEM((NQ, ROWS, 128), F32),
            pltpu.VMEM((ROWS, 128), F32),
            pltpu.VMEM((6, 8, 128), F32),
            pltpu.VMEM((2, 16), jnp.int32),
            pltpu.SemaphoreType.DMA((4,)),
        ],
        compiler_params=pltpu.CompilerParams(vmem_limit_bytes=16 * 1024 * 1024),
        name="first",
    )(in_hbm(flow), in_hbm(cot), in_hbm(clip_flags.reshape(2, 16)), in_hbm(jnp.asarray(constants)))

    ahead = swapped(to_ahead, "gy", 0)
    behind = swapped(to_behind, "gy", 1)
    other = swapped(to_other, "gx", 1)
    partner = swapped(to_partner, "gx", 0)

    base, extra, slope, zsum, _ = pl.pallas_call(
        kernel_second,
        out_shape=(shape(10, ROWS, 128), shape(10, ROWS, 128), shape(5, ROWS, 128), shape(8, 128), shape(3, 20, ROWS, 128)),
        in_specs=[hbm] + [vmem] * 8,
        out_specs=[vmem] * 5,
        input_output_aliases={8: 4},
        scratch_shapes=[
            pltpu.VMEM((10, 32, 128), F32),
            pltpu.VMEM((NQ, 32, 128), F32),
            pltpu.VMEM((NQ, 16, 128), F32),
            pltpu.VMEM((10, 16, 128), F32),
            pltpu.SMEM((16,), jnp.int32),
            pltpu.SemaphoreType.DMA(()),
        ],
        compiler_params=pltpu.CompilerParams(vmem_limit_bytes=16 * 1024 * 1024),
        name="second",
    )(in_hbm(successor_ids), flow_v, cot_v, lines, mid, modes, msg, tables, sums)

    residual, grad = pl.pallas_call(
        kernel_blend,
        out_shape=(shape(5, ROWS, 128), shape(5, ROWS, 128)),
        in_specs=[vmem] * 11,
        out_specs=[hbm] * 2,
        scratch_shapes=[pltpu.VMEM((10, ROWS, 128), F32), pltpu.SemaphoreType.DMA((6,))],
        compiler_params=pltpu.CompilerParams(vmem_limit_bytes=16 * 1024 * 1024),
        name="blend",
    )(msg, zsum, partner, other, ahead, behind, flow_v, cot_v, base, extra, slope)
    return residual.reshape(flow_state.shape), grad.reshape(flow_state.shape)


def solution(mesh):
    placed = P(None, "gx", "gy", None)
    return jax.shard_map(
        shards,
        mesh=mesh,
        in_specs=(placed, placed, P("gx", "gy", None), P()),
        out_specs=(placed, placed),
        check_vma=False,
    )
```

```python
import jax
import jax.numpy as jnp
import numpy as np
from jax import lax
from jax.experimental import pallas as pl
from jax.experimental.pallas import tpu as pltpu
from jax.sharding import PartitionSpec as P
from numpy.polynomial import chebyshev, polynomial

F32 = jnp.float32
HIGHEST = lax.Precision.HIGHEST
EPS = 1e-05
PERMS = ((0, 1, 2), (1, 0, 2), (2, 0, 1))
NQ = 13
ROWS = 128


def legendre_values(points, node_count):
    values_table = np.zeros((points.shape[0], node_count))
    values_table[:, 0] = 1.0
    values_table[:, 1] = points
    for degree_index in range(2, node_count):
        values_table[:, degree_index] = (
            (2 * degree_index - 1) * points * values_table[:, degree_index - 1]
            - (degree_index - 1) * values_table[:, degree_index - 2]
        ) / degree_index
    return values_table


def node_tables():
    degree = 7
    node_count = degree + 1
    points = -np.cos(np.pi * np.arange(node_count) / degree)
    for newton_step in range(60):
        legend = legendre_values(points, node_count)
        points = points - (points * legend[:, degree] - legend[:, degree - 1]) / (
            node_count * legend[:, degree]
        )
    legend = legendre_values(points, node_count)
    weights = 2.0 / (degree * node_count * legend[:, degree] * legend[:, degree])
    differ = np.zeros((node_count, node_count))
    for row_index in range(node_count):
        for col_index in range(node_count):
            if row_index != col_index:
                differ[row_index, col_index] = legend[row_index, degree] / (
                    legend[col_index, degree] * (points[row_index] - points[col_index])
                )
    norm_table = 2.0 / (2.0 * np.arange(node_count) + 1.0)
    norm_table[degree] = 2.0 / degree
    to_modal = legend.T * weights[None, :] / norm_table[:, None]
    return (weights, differ, to_modal)


WEIGHTS, DIFFER, TO_MODAL = node_tables()
INV_W = [float(1.0 / w) for w in WEIGHTS]
SKEW = 2.0 * DIFFER * WEIGHTS[:, None]


def fitted(function, top, degree):
    series = chebyshev.Chebyshev.interpolate(function, degree, domain=[0.0, top])
    return [float(np.float32(c)) for c in series.convert(kind=polynomial.Polynomial).coef]


def sinhc(square):
    root = np.sqrt(np.maximum(square, 1e-12))
    return np.sinh(root) / root


def sinhc_slope(square):
    root = np.sqrt(np.maximum(square, 1e-12))
    exact = (np.cosh(root) - np.sinh(root) / root) / (root * root)
    series = 1.0 / 3.0 + square / 30.0 + square**2 / 840.0 + square**3 / 45360.0
    return np.where(square < 1e-2, series, exact)


RATES = 5 * 28
PAIR = {pair: i for i, pair in enumerate((k, j) for k in range(7) for j in range(k + 1, 8))}

MEAN_R = fitted(sinhc, 3.0, 4)
SLOPE_R = fitted(sinhc_slope, 3.0, 3)
MEAN_B = fitted(sinhc, 12.0, 5)
SLOPE_B = fitted(sinhc_slope, 12.0, 5)


def horner(coeffs, value):
    total = coeffs[-1] * value + coeffs[-2]
    for c in coeffs[-3::-1]:
        total = total * value + c
    return total


def rcp(value):
    return 1.0 / value


def log_parts(density, pressure):
    inv = rcp(density)
    ratio = pressure * inv
    half_log = 0.5 * jnp.log(density)
    return (
        jnp.sqrt(density),
        half_log,
        jnp.sqrt(5.0 * ratio),
        half_log - 0.5 * jnp.log(pressure),
    )


class Node:
    def __init__(self, vel, pres, root, theta, cot):
        self.vel, self.pres, self.cot = vel, pres, cot
        density = root * root
        vn, v1, v2 = vel
        mom = [density * v for v in vel]
        self.square = vn * vn + v1 * v1 + v2 * v2
        energy = 2.5 * pres + (0.5 * density) * self.square
        self.state = [density] + mom + [energy]
        mn = mom[0]
        self.flux = [mn, mn * vn + pres, mn * v1, mn * v2, (energy + pres) * vn]
        self.sound = theta * float(np.sqrt(1.4 / 5.0))
        self.speed = jnp.abs(vn) + self.sound

    def pull(self, half, direct, speed_cot):
        density = self.state[0]
        vn, v1, v2 = self.vel
        grad = [direct[i] + half[i] * vn for i in range(5)]
        sign = jnp.where(vn >= 0.0, 1.0, -1.0)
        dvn = half[0] * self.state[0]
        for i in range(1, 5):
            dvn = dvn + half[i] * self.state[i]
        dvn = dvn + half[4] * self.pres + speed_cot * sign
        inv = rcp(density)
        part = (0.5 * speed_cot) * self.sound
        dpres = half[1] + half[4] * vn + part * rcp(self.pres)
        over = dvn * inv
        pull_e = 0.4 * dpres
        grad[0] = grad[0] - part * inv - over * vn + (0.5 * pull_e) * self.square
        grad[1] = grad[1] + over - pull_e * vn
        grad[2] = grad[2] - pull_e * v1
        grad[3] = grad[3] - pull_e * v2
        grad[4] = grad[4] + pull_e
        return grad


def face_adjoint(low, up):
    jump = [b - a for a, b in zip(low.state, up.state)]
    weight = [b - a for a, b in zip(low.cot, up.cot)]
    speed = 0.5 * (low.speed + up.speed)
    dot = weight[0] * jump[0]
    for i in range(1, 5):
        dot = dot + weight[i] * jump[i]
    return weight, [speed * w for w in weight], -0.5 * dot


def face_rate(low, up):
    speed = 0.5 * (low.speed + up.speed)
    return [
        a + b - speed * (y - x) for a, b, x, y in zip(low.flux, up.flux, low.state, up.state)
    ]


def lane_tables():
    sub = lax.broadcasted_iota(jnp.int32, (8, 128), 0)
    lane = lax.broadcasted_iota(jnp.int32, (8, 128), 1)
    return sub, lane, (sub >= 6) | ((lane & 7) >= 6)


def kernel_first(
    flow_hbm,
    cot_hbm,
    flags_hbm,
    tables_hbm,
    lines,
    mid,
    modes,
    msg,
    to_partner,
    to_other,
    to_ahead,
    to_behind,
    flow,
    cot,
    tables,
    out,
    nat,
    turned,
    prod,
    gsum,
    flags,
    sems,
):
    copies = [
        pltpu.make_async_copy(source, target, sems.at[i])
        for i, (source, target) in enumerate(
            (
                (flow_hbm, flow),
                (cot_hbm, cot),
                (tables_hbm.at[pl.ds(0, 2)], tables.at[pl.ds(0, 2)]),
                (flags_hbm, flags),
                (tables_hbm.at[pl.ds(2, 2)], tables.at[pl.ds(2, 2)]),
            )
        )
    ]
    for copy in copies:
        copy.start()
    even_x = lax.axis_index("gx") % 2 == 0
    even_y = lax.axis_index("gy") % 2 == 0
    for copy in copies[:4]:
        copy.wait()
    for c in range(10):
        source, q = (flow, c) if c < 5 else (cot, c - 5)
        top, low = source[q, pl.ds(112, 16), :], source[q, pl.ds(0, 16), :]
        to_partner[pl.ds(16 * c, 16), :] = jnp.where(even_x, top, low)
        to_other[pl.ds(16 * c, 16), :] = jnp.where(even_x, low, top)
        top, low = source[q, pl.ds(15, 8, stride=16), :], source[q, pl.ds(0, 8, stride=16), :]
        to_ahead[pl.ds(8 * c, 8), :] = jnp.where(even_y, top, low)
        to_behind[pl.ds(8 * c, 8), :] = jnp.where(even_y, low, top)

    for x in range(8):
        for h in range(2):
            src = pl.ds(x * 16 + h * 8, 8)
            dst = pl.ds(h * 64 + x * 8, 8)
            density = flow[0, src, :]
            inv = rcp(density)
            mom = [flow[1 + i, src, :] for i in range(3)]
            vel = [m * inv for m in mom]
            kinetic = mom[0] * vel[0] + mom[1] * vel[1] + mom[2] * vel[2]
            pres = 0.4 * (flow[4, src, :] - 0.5 * kinetic)
            prod[dst, :] = density * pres
            parts = vel + [pres] + list(log_parts(density, pres))
            for q in range(8):
                nat[q, dst, :] = parts[q]
            for q in range(5):
                value = cot[q, src, :]
                nat[8 + q, dst, :] = 2.0 * value if q == 0 else value
    for q in range(NQ):
        turned[q] = jnp.transpose(nat[q])
    for d in range(3):
        perm = PERMS[d]
        order = [perm[0], perm[1], perm[2], 3, 4, 5, 6, 7, 8] + [9 + i for i in perm] + [12]
        source = nat if d < 2 else turned
        for q in range(NQ):
            for h in range(2):
                for k in range(8):
                    rows = pl.ds(h * 64 + 8 * k, 8) if d == 0 else pl.ds(h * 64 + k, 8, stride=8)
                    value = source[order[q], rows, :]
                    lines[d, q, pl.ds(h * 64 + 8 * k, 8), :] = value * (0.5 * INV_W[k]) if q >= 8 else value

    sub, lane, high = lane_tables()
    coeffs = jnp.dot(tables[0], prod[...], precision=HIGHEST, preferred_element_type=F32)
    coeffs = jnp.dot(coeffs, tables[1], precision=HIGHEST, preferred_element_type=F32)
    modes[...] = coeffs
    squares = coeffs * coeffs
    group = jnp.where(
        lax.broadcasted_iota(jnp.int32, (128, 128), 0) >> 3
        == lax.broadcasted_iota(jnp.int32, (128, 128), 1) >> 3,
        1.0,
        0.0,
    )
    spread = (
        lax.broadcasted_iota(jnp.int32, (16, 128), 0)
        == lax.broadcasted_iota(jnp.int32, (16, 128), 1) >> 3
    )
    packed = jnp.zeros((8, 128), F32)
    for h in range(2):
        every = squares[h * 64 : h * 64 + 8]
        for x in range(1, 6):
            every = every + squares[h * 64 + 8 * x : h * 64 + 8 * x + 8]
        ends = squares[h * 64 + 48 : h * 64 + 56] + squares[h * 64 + 56 : h * 64 + 64]
        top = jnp.sum(jnp.where(high, every, 0.0) + ends, axis=0, keepdims=True)
        packed = jnp.where(sub == h, top, packed)
        packed = jnp.where(sub == 2 + h, jnp.sum(every + ends, axis=0, keepdims=True), packed)
    sums = jnp.dot(packed, group, precision=HIGHEST, preferred_element_type=F32)
    flag_rows = jnp.dot(
        flags[...].astype(F32),
        jnp.where(spread, 1.0, 0.0),
        precision=HIGHEST,
        preferred_element_type=F32,
    )
    sub16 = lax.broadcasted_iota(jnp.int32, (16, 128), 0)
    factors = jnp.zeros((16, 128), F32)
    for h in range(2):
        top = sums[h : h + 1] + EPS
        every = 0.01 * (sums[2 + h : 3 + h] + EPS)
        flag = flag_rows[h : h + 1]
        over = rcp(top + every)
        keep = flag < 0.5
        alpha = jnp.where(keep, 0.5 * top * over, jnp.where(flag > 1.5, 0.5, 0.0))
        d_top = jnp.where(keep, every * over * over, 0.0)
        d_all = jnp.where(keep, -0.01 * top * over * over, 0.0)
        for i, row in ((0, alpha), (6, d_top), (8, d_all)):
            factors = jnp.where(sub16 == i + h, row, factors)
    msg[...] = factors

    def one(step):
        d = step // 2
        base = (step % 2) * 64

        def load(k):
            start = base + 8 * k
            return [lines[d, q, pl.ds(start, 8), :] for q in range(NQ)]

        gained = jnp.zeros((8, 128), F32)
        for k in range(7):
            a = load(k)
            for j in range(k + 1, 8):
                skew = float(SKEW[k, j])
                b = load(j)
                vn, v1, v2 = (a[i] + b[i] for i in range(3))
                delta = [a[8 + i] - b[8 + i] for i in range(5)]
                y = a[5] - b[5]
                mean = ((0.5 * skew) * (a[4] * b[4])) * horner(MEAN_R, y * y)
                yb = a[7] - b[7]
                quot = rcp(horner(MEAN_B, yb * yb))
                inv5 = (a[6] * b[6]) * quot
                dot = a[0] * b[0] + a[1] * b[1] + a[2] * b[2] + inv5
                phi = delta[0] + delta[1] * vn + delta[2] * v1 + delta[3] * v2 + delta[4] * dot
                for q, value in enumerate((mean, quot, inv5, dot, phi)):
                    mid[step, 5 * PAIR[k, j] + q] = value
                work = delta[1] * (a[3] + b[3]) + delta[4] * (a[3] * b[0] + b[3] * a[0])
                gained = gained + (mean * vn) * phi + skew * work
        low = None
        for k in range(8):
            a = load(k)
            node = Node(a[0:3], a[3], a[4], a[6], [0.5 * a[8]] + a[9:13])
            if k:
                for q, rate in enumerate(face_rate(low, node)):
                    mid[step, RATES + 5 * (k - 1) + q] = rate
                    gained = gained + rate * (node.cot[q] - low.cot[q])
            low = node
        gsum[step] = gained

    for step in range(6):
        one(step)

    half_lane = lax.broadcasted_iota(jnp.int32, (16, 128), 1) >> 6
    along = jnp.concatenate([gsum[4], gsum[5]], axis=0)
    factors = msg[...]
    for h in range(2):
        row = jnp.sum(gsum[h] + gsum[2 + h], axis=0, keepdims=True)
        both = jnp.where(half_lane == h, along, 0.0) + jnp.where(spread, row, 0.0)
        column = jnp.sum(both, axis=1, keepdims=True)
        gain = jnp.sum(jnp.where(spread, column, 0.0), axis=0, keepdims=True)
        factors = jnp.where(sub16 == 4 + h, gain, factors)
        factors = jnp.where(sub16 == 2 + h, gain * (1.0 - factors[h : h + 1]), factors)
    msg[...] = factors
    for target, row in ((to_partner, 160), (to_other, 160), (to_ahead, 80), (to_behind, 80)):
        target[pl.ds(row, 8), :] = factors[0:8]

    def two(step, carry):
        adjoint_step(lines, mid, out, step)
        return carry

    lax.fori_loop(0, steps_ahead(), two, 0)
    copies[4].wait()


def conserved_node(state, cot, direction):
    perm = PERMS[direction]
    density = state[0]
    inv = rcp(density)
    vel = [state[1 + i] * inv for i in perm]
    square = vel[0] * vel[0] + vel[1] * vel[1] + vel[2] * vel[2]
    pres = 0.4 * (state[4] - 0.5 * density * square)
    scaled = [cot[0]] + [cot[1 + i] for i in perm] + [cot[4]]
    return Node(vel, pres, jnp.sqrt(density), jnp.sqrt(5.0 * pres * inv), [c * (0.5 * INV_W[0]) for c in scaled])


def face_shares(low, up):
    rate = face_rate(low, up)
    weight, direct, dot = face_adjoint(low, up)
    return (
        [(-0.5 * INV_W[7]) * f for f in rate],
        low.pull(weight, direct, dot),
        [(0.5 * INV_W[0]) * f for f in rate],
        up.pull(weight, [-x for x in direct], dot),
    )


def steps_ahead():
    gx = lax.axis_index("gx")
    plane = 2 * lax.axis_index("gy") + gx // 32
    corner = jnp.where(plane < 4, 5 - plane, 0)
    return jnp.where(gx % 32 == 0, corner, jnp.where(plane < 2, 4 - plane, 0))


def adjoint_step(lines, mid, out, step):
    d = step // 2
    base = (step % 2) * 64

    def rows(k):
        return pl.ds(pl.multiple_of(base + 8 * k, 8), 8)

    for k in range(7):
        a = [lines[d, q, rows(k), :] for q in range(NQ)]
        acc = [None] * 13 if k == 0 else [out[d, q, rows(k), :] for q in range(13)]
        for j in range(k + 1, 8):
            skew = float(SKEW[k, j])
            b = [lines[d, q, rows(j), :] for q in range(NQ)]
            mean, quot, inv5, dot, phi = (mid[step, 5 * PAIR[k, j] + q] for q in range(5))
            vn, v1, v2, pres = (a[i] + b[i] for i in range(4))
            delta = [None] + [a[8 + i] - b[8 + i] for i in range(1, 5)]
            y = a[5] - b[5]
            slope = (((0.5 * skew) * (a[4] * b[4])) * y) * horner(SLOPE_R, y * y)
            yb = a[7] - b[7]
            tilt = yb * (horner(SLOPE_B, yb * yb) * quot)
            mass = mean * vn
            flux = [
                mass,
                mass * vn + skew * pres,
                mass * v1,
                mass * v2,
                mass * dot + skew * (a[3] * b[0] + b[3] * a[0]),
            ]
            t = skew * delta[4]
            w = mass * delta[4]
            pp = phi * mass
            qq = (phi * vn) * slope
            xx = w * inv5
            zz = xx * tilt
            shared = [
                phi * mean + mass * (delta[1] + delta[4] * vn) + t * pres,
                mass * (delta[2] + delta[4] * v1),
                mass * (delta[3] + delta[4] * v2),
                skew * (delta[1] + delta[4] * vn),
            ]
            ups = flux + [pp + qq] + shared + [xx + zz, w, t]
            downs = [None] * 5 + [pp - qq] + shared + [xx - zz, w, t]
            for q in range(13):
                acc[q] = ups[q] if acc[q] is None else acc[q] + ups[q]
                if q < 5:
                    value = -flux[q] if k == 0 else out[d, q, rows(j), :] - flux[q]
                else:
                    value = downs[q] if k == 0 else out[d, q, rows(j), :] + downs[q]
                out[d, q, rows(j), :] = value
        for q in range(13):
            out[d, q, rows(k), :] = acc[q]

    low = None
    zero = jnp.zeros((8, 128), F32)
    low_flux, low_weight, low_direct, low_dot = [zero] * 5, [zero] * 5, [zero] * 5, zero
    for k in range(9):
        if k < 8:
            a = [lines[d, q, rows(k), :] for q in range(NQ)]
            node = Node(a[0:3], a[3], a[4], a[6], [0.5 * a[8]] + a[9:13])
        if k == 0:
            low = node
            continue
        if k < 8:
            weight, direct, dot = face_adjoint(low, node)
            flux = [mid[step, RATES + 5 * (k - 1) + q] for q in range(5)]
        else:
            flux, weight, direct, dot = [zero] * 5, [zero] * 5, [zero] * 5, zero
        m = k - 1
        total = [out[d, q, rows(m), :] for q in range(13)]
        for i in range(3):
            total[6 + i] = total[6 + i] - total[11] * low.vel[i]
        total[6] = total[6] - total[12] * low.pres
        total[9] = total[9] - total[12] * low.vel[0]
        total[0] = 2.0 * total[0]
        for q in range(5):
            diff = total[q] - (flux[q] - low_flux[q])
            out[d, q, rows(m), :] = total[q] * (-0.5 * INV_W[m])
            out[d, 5 + q, rows(m), :] = diff * (0.5 * INV_W[m])
        fv = low.pull(
            [x + z for x, z in zip(low_weight, weight)],
            [x - z for x, z in zip(direct, low_direct)],
            low_dot + dot,
        )
        inv = rcp(low.state[0])
        beta = 0.5 * total[10]
        g_rho = (beta - 0.5 * total[5]) * inv
        g_e = -0.4 * (total[9] + beta * rcp(low.pres))
        g_m = [-(total[6 + i] * inv) - g_e * low.vel[i] for i in range(3)]
        inner = g_m[0] * low.vel[0] + g_m[1] * low.vel[1] + g_m[2] * low.vel[2]
        dg = [g_rho - inner - (0.5 * g_e) * low.square] + g_m + [g_e]
        for q in range(5):
            out[d, 10 + q, rows(m), :] = dg[q]
            out[d, 15 + q, rows(m), :] = fv[q] - dg[q]
        low, low_flux, low_weight, low_direct, low_dot = node, flux, weight, direct, dot


def place(d, q):
    return q if q in (0, 4) else 1 + PERMS[d][q - 1]


def own_node(flow, cot, direction, rows):
    return conserved_node(
        [flow[q, rows, :] for q in range(5)], [cot[q, rows, :] for q in range(5)], direction
    )


def near_node(first, other, choose, count, start, direction):
    def value(c):
        rows = pl.ds(c * count + start, 8)
        return jnp.where(choose, first[rows, :], other[rows, :])

    return conserved_node([value(q) for q in range(5)], [value(5 + q) for q in range(5)], direction)


def kernel_second(
    ids_hbm,
    flow,
    cot,
    lines,
    mid,
    modes,
    msg,
    tables,
    ahead_sums,
    base,
    extra,
    slope,
    zsum,
    out,
    zacc,
    zends,
    znext,
    zback,
    ids,
    sem,
):
    copy = pltpu.make_async_copy(ids_hbm, ids, sem)
    copy.start()

    def one(step, carry):
        adjoint_step(lines, mid, out, step)
        return carry

    lax.fori_loop(steps_ahead(), 6, one, 0)
    sub, lane, high = lane_tables()
    tiles = []
    for h in range(2):
        d_top = msg[pl.ds(6 + h, 1), :]
        d_all = msg[pl.ds(8 + h, 1), :]
        both = d_top + d_all
        mixed = jnp.where(high, both, d_all)
        for x in range(8):
            tiles.append(modes[pl.ds(h * 64 + 8 * x, 8), :] * (both if x >= 6 else mixed))
    weighed = jnp.concatenate(tiles, axis=0)
    weighed = jnp.dot(tables[2], weighed, precision=HIGHEST, preferred_element_type=F32)
    weighed = jnp.dot(weighed, tables[3], precision=HIGHEST, preferred_element_type=F32)
    for h in range(2):
        for x in range(8):
            rows = pl.ds(x * 16 + h * 8, 8)
            density = flow[0, rows, :]
            inv = rcp(density)
            vel = [flow[1 + i, rows, :] * inv for i in range(3)]
            square = vel[0] * vel[0] + vel[1] * vel[1] + vel[2] * vel[2]
            pres = 0.4 * (flow[4, rows, :] - 0.5 * density * square)
            value = weighed[h * 64 + 8 * x : h * 64 + 8 * x + 8]
            pull_e = 0.4 * (value * density)
            slope[0, rows, :] = value * pres + (0.5 * pull_e) * square
            for i in range(3):
                slope[1 + i, rows, :] = -(pull_e * vel[i])
            slope[4, rows, :] = pull_e

    back = [[place(d, q) for q in range(5)] for d in range(3)]
    def combine(group_at, target, offset):
        for q in range(5):
            first = group_at * 5
            qx = first + back[0].index(q)
            qy = first + back[1].index(q)
            qz = back[2].index(q)
            pieces = []
            for slot in range(16):
                h, s = slot // 8, slot % 8
                pieces.append(out[2, first + qz, pl.ds(h * 64 + s, 8, stride=8), :])
            if group_at in (0, 2):
                source = qz + (0 if group_at == 0 else 5)
                for slot in range(16):
                    upper = zacc[source, pl.ds(slot, 1), :]
                    lower = zacc[source, pl.ds(16 + slot, 1), :]
                    add = jnp.where(sub == 7, upper, jnp.where(sub == 0, lower, 0.0))
                    pieces[slot] = pieces[slot] + add
            whole = jnp.transpose(jnp.concatenate(pieces, axis=0))
            for h in range(2):
                for x in range(8):
                    value = (
                        out[0, qx, pl.ds(h * 64 + 8 * x, 8), :]
                        + out[1, qy, pl.ds(h * 64 + x, 8, stride=8), :]
                        + whole[h * 64 + 8 * x : h * 64 + 8 * x + 8]
                    )
                    target[offset + q, pl.ds(x * 16 + h * 8, 8), :] = value

    combine(1, extra, 0)
    combine(3, extra, 5)

    copy.wait()
    row = lax.broadcasted_iota(jnp.int32, (128, 128), 0)
    lanes = lax.broadcasted_iota(jnp.int32, (8, 128), 1)
    above = jnp.zeros((8, 128), jnp.int32)
    for k in range(16):
        above = jnp.where((lanes >> 3) == k, ids[k], above)
    above = above * 8 + (lanes & 7)
    above = jnp.concatenate([above] * 16, axis=0)
    up = jnp.where(above == row, 1.0, 0.0)
    own = msg[0:8, :]
    zsum[...] = jnp.dot(own, up, precision=HIGHEST, preferred_element_type=F32) + lax.dot_general(
        own, up, (((1,), (1,)), ((), ())), precision=HIGHEST, preferred_element_type=F32
    )

    for q in range(NQ):
        for end in range(2):
            for h in range(2):
                zends[q, pl.ds(end * 16 + h * 8, 8), :] = lines[2, q, pl.ds(h * 64 + 56 * end, 8), :]
    for k in range(16):
        znext[:, pl.ds(k, 1), :] = zends[:, pl.ds(ids[k], 1), :]
    for h in range(2):
        def side(ref, start):
            v = [ref[q, pl.ds(start + h * 8, 8), :] for q in range(NQ)]
            return Node(v[0:3], v[3], v[4], v[6], [0.5 * v[8]] + v[9:13])

        low_r, low_g, up_r, up_g = face_shares(side(zends, 16), side(znext, 0))
        for q in range(5):
            zacc[q, pl.ds(h * 8, 8), :] = low_r[q]
            zacc[5 + q, pl.ds(h * 8, 8), :] = low_g[q]
            zback[q, pl.ds(h * 8, 8), :] = up_r[q]
            zback[5 + q, pl.ds(h * 8, 8), :] = up_g[q]
    for k in range(16):
        zacc[:, pl.ds(16 + ids[k], 1), :] = zback[:, pl.ds(k, 1), :]

    combine(0, base, 0)
    combine(2, base, 5)

    rows = [pl.ds(7, 8, stride=16), pl.ds(8, 8, stride=16)]
    shares = face_shares(own_node(flow, cot, 1, rows[0]), own_node(flow, cot, 1, rows[1]))
    for side in range(2):
        for q in range(5):
            p = place(1, q)
            base[p, rows[side], :] += shares[2 * side][q]
            base[5 + p, rows[side], :] += shares[2 * side + 1][q]


def kernel_blend(
    msg,
    zsum,
    partner,
    other,
    ahead,
    behind,
    flow,
    cot,
    base,
    extra,
    slope,
    residual_hbm,
    grad_hbm,
    total,
    sems,
):
    even_x = lax.axis_index("gx") % 2 == 0
    even_y = lax.axis_index("gy") % 2 == 0
    sides = partner[160:168, :] + other[160:168, :]
    met, left = ahead[80:88, :], behind[80:88, :]
    above, below = jnp.where(even_y, met, left), jnp.where(even_y, left, met)
    for h in range(2):

        def beside_of(i):
            r = 2 * i + h
            low = below[2 * i + 1 : 2 * i + 2] if h == 0 else msg[2 * i : 2 * i + 1, :]
            high = msg[2 * i + 1 : 2 * i + 2, :] if h == 0 else above[2 * i : 2 * i + 1]
            return zsum[r : r + 1, :] + sides[r : r + 1] + low + high

        alpha = msg[h : h + 1, :]
        gain = msg[4 + h : 5 + h, :]
        around = beside_of(0)
        smooth = alpha + (1.0 - alpha) * around * (0.5 / 6.0)
        pull = gain * (1.0 - around * (0.5 / 6.0)) + beside_of(1) * (0.5 / 6.0)
        smooth = jnp.broadcast_to(smooth, (8, 128))
        pull = jnp.broadcast_to(pull, (8, 128))
        for x in range(8):
            rows = pl.ds(x * 16 + h * 8, 8)
            for q in range(5):
                total[q, rows, :] = base[q, rows, :] + smooth * extra[q, rows, :]
                total[5 + q, rows, :] = (
                    base[5 + q, rows, :] + smooth * extra[5 + q, rows, :] + pull * slope[q, rows, :]
                )

    def add(direction, rows, res, grad):
        for q in range(5):
            p = place(direction, q)
            total[p, rows, :] += res[q]
            total[5 + p, rows, :] += grad[q]

    here, top = pl.ds(0, 8, stride=16), pl.ds(15, 8, stride=16)
    shares = face_shares(near_node(behind, ahead, even_y, 8, 0, 1), own_node(flow, cot, 1, here))
    add(1, here, shares[2], shares[3])
    shares = face_shares(own_node(flow, cot, 1, top), near_node(ahead, behind, even_y, 8, 0, 1))
    add(1, top, shares[0], shares[1])

    def send(i, start, count):
        rows = pl.ds(start, count)
        return [
            pltpu.make_async_copy(
                total.at[pl.ds(0, 5), rows], residual_hbm.at[pl.ds(0, 5), rows], sems.at[2 * i]
            ),
            pltpu.make_async_copy(
                total.at[pl.ds(5, 5), rows], grad_hbm.at[pl.ds(0, 5), rows], sems.at[2 * i + 1]
            ),
        ]

    copies = send(0, 16, 96)
    for copy in copies:
        copy.start()
    for h in range(2):
        here, top = pl.ds(h * 8, 8), pl.ds(112 + h * 8, 8)
        shares = face_shares(
            near_node(other, partner, even_x, 16, h * 8, 0), own_node(flow, cot, 0, here)
        )
        add(0, here, shares[2], shares[3])
        shares = face_shares(
            own_node(flow, cot, 0, top), near_node(partner, other, even_x, 16, h * 8, 0)
        )
        add(0, top, shares[0], shares[1])
    last = send(1, 0, 16) + send(2, 112, 16)
    for copy in last:
        copy.start()
    for copy in copies + last:
        copy.wait()


def swapped(value, axis, first):
    count = lax.axis_size(axis)
    pairs = []
    for i in range(first, count + first, 2):
        a, b = i % count, (i + 1) % count
        pairs += [(a, b), (b, a)]
    return lax.ppermute(value, axis, pairs)


def shape(*dims):
    return jax.ShapeDtypeStruct(dims, F32)


def in_hbm(value):
    return pltpu.with_memory_space_constraint(value, pltpu.HBM)


def shards(flow_state, cotangent, clip_flags, successor_ids):
    flow = flow_state.reshape(5, ROWS, 128)
    cot = cotangent.reshape(5, ROWS, 128)
    vmem = pl.BlockSpec(memory_space=pltpu.VMEM)
    hbm = pl.BlockSpec(memory_space=pltpu.HBM)
    modal = np.asarray(TO_MODAL, np.float32)
    kxy = np.kron(np.eye(2), np.kron(modal, modal)).astype(np.float32)
    kz = np.kron(np.eye(16), modal).astype(np.float32)
    constants = np.stack([kxy, kz.T, kxy.T, kz])

    lines, mid, modes, msg, to_partner, to_other, to_ahead, to_behind, flow_v, cot_v, tables, sums = pl.pallas_call(
        kernel_first,
        out_shape=(
            shape(3, NQ, ROWS, 128),
            shape(6, RATES + 35, 8, 128),
            shape(ROWS, 128),
            shape(16, 128),
            shape(168, 128),
            shape(168, 128),
            shape(88, 128),
            shape(88, 128),
            shape(5, ROWS, 128),
            shape(5, ROWS, 128),
            shape(4, 128, 128),
            shape(3, 20, ROWS, 128),
        ),
        in_specs=[hbm] * 4,
        out_specs=[vmem] * 12,
        scratch_shapes=[
            pltpu.VMEM((NQ, ROWS, 128), F32),
            pltpu.VMEM((NQ, ROWS, 128), F32),
            pltpu.VMEM((ROWS, 128), F32),
            pltpu.VMEM((6, 8, 128), F32),
            pltpu.VMEM((2, 16), jnp.int32),
            pltpu.SemaphoreType.DMA((5,)),
        ],
        compiler_params=pltpu.CompilerParams(vmem_limit_bytes=16 * 1024 * 1024),
        name="first",
    )(in_hbm(flow), in_hbm(cot), in_hbm(clip_flags.reshape(2, 16)), in_hbm(jnp.asarray(constants)))

    ahead = swapped(to_ahead, "gy", 0)
    behind = swapped(to_behind, "gy", 1)
    other = swapped(to_other, "gx", 1)
    partner = swapped(to_partner, "gx", 0)

    base, extra, slope, zsum, _ = pl.pallas_call(
        kernel_second,
        out_shape=(shape(10, ROWS, 128), shape(10, ROWS, 128), shape(5, ROWS, 128), shape(8, 128), shape(3, 20, ROWS, 128)),
        in_specs=[hbm] + [vmem] * 8,
        out_specs=[vmem] * 5,
        input_output_aliases={8: 4},
        scratch_shapes=[
            pltpu.VMEM((10, 32, 128), F32),
            pltpu.VMEM((NQ, 32, 128), F32),
            pltpu.VMEM((NQ, 16, 128), F32),
            pltpu.VMEM((10, 16, 128), F32),
            pltpu.SMEM((16,), jnp.int32),
            pltpu.SemaphoreType.DMA(()),
        ],
        compiler_params=pltpu.CompilerParams(vmem_limit_bytes=16 * 1024 * 1024),
        name="second",
    )(in_hbm(successor_ids), flow_v, cot_v, lines, mid, modes, msg, tables, sums)

    residual, grad = pl.pallas_call(
        kernel_blend,
        out_shape=(shape(5, ROWS, 128), shape(5, ROWS, 128)),
        in_specs=[vmem] * 11,
        out_specs=[hbm] * 2,
        scratch_shapes=[pltpu.VMEM((10, ROWS, 128), F32), pltpu.SemaphoreType.DMA((6,))],
        compiler_params=pltpu.CompilerParams(vmem_limit_bytes=16 * 1024 * 1024),
        name="blend",
    )(msg, zsum, partner, other, ahead, behind, flow_v, cot_v, base, extra, slope)
    return residual.reshape(flow_state.shape), grad.reshape(flow_state.shape)


def solution(mesh):
    placed = P(None, "gx", "gy", None)
    return jax.shard_map(
        shards,
        mesh=mesh,
        in_specs=(placed, placed, P("gx", "gy", None), P()),
        out_specs=(placed, placed),
        check_vma=False,
    )
```
